32 devices in a mesh: dp: 16 (over z, y, core), head: 2 (over x).
Axes of the slice: x: 2, y: 2, z: 4, core: 2. Of those that a mesh axis runs over, the one named last changes fastest.
Arguments:
- tokens: bfloat16 [32768, 768], P('dp'), may hold values from -6 to 6
- segments: int32 [64, 512], P('dp'), may hold values from 0 to 7, never falling along the last dimension, each value on 1 to 128 neighbouring positions
- qkv_weight: bfloat16 [2, 3, 192, 768], P(None, None, None, 'head'), may hold values from -0.4375 to 0.4375
- out_weight: bfloat16 [2, 768, 768], P(None, 'head'), may hold values from -0.625 to 0.625
- inner_weight: bfloat16 [2, 192, 3072], P(None, None, 'head'), may hold values from -0.4375 to 0.4375
- outer_weight: bfloat16 [2, 768, 768], P(None, None, 'head'), may hold values from -0.21875 to 0.21875
- norm_gains: float32 [2, 2, 768], replicated, may hold values from 0.5 to 1.5
- cotangent: bfloat16 [32768, 768], P('dp'), may hold values from -6 to 6
Outputs:
- activations: bfloat16 [32768, 768], P('dp')
- input_grad: bfloat16 [32768, 768], P('dp')
- qkv_grad: float32 [2, 3, 192, 768], P(None, None, None, 'head')
- out_grad: float32 [2, 768, 768], P(None, 'head')
- inner_grad: float32 [2, 192, 3072], P(None, None, 'head')
- outer_grad: float32 [2, 768, 768], P(None, None, 'head')
- gain_grad: float32 [2, 2, 768], replicated
The draws below stay inside these ranges and needn't reach their ends.
Inputs may be any that keep to these rules, and one draw needn't show every extreme that they name: `segments`: along each packed row the ids never fall; a document holds at most 128 positions and some document holds exactly that many.
All inputs are finite; a program needn't handle non-finite values.
Results may differ from the reference program's by a relative error of at most 0.035.
Values may be sent and summed in bfloat16 or wider, within the bound.
No kernel may reach another device: no remote copies, remote signals or barrier semaphores. Data moves between devices by JAX's collectives and lax.ppermute only.
A program may use at most 256 MiB of HBM per device.

```python
import math
import jax
import jax.numpy as jnp
import numpy as np
from jax import lax

D = 768
HEADS = 12
HEAD_DIM = 64
FF = 3072
GROUPS = 4
SEQ = 512
LAYERS = 2
ROWS = 64
TOKENS = 32768
N_HEAD = 2


def level_of(own_key, extent, split, least, high):
    factor_of = 1.0
    for position, shards_of in split:
        heights = jax.random.uniform(jax.random.fold_in(jax.random.fold_in(own_key, 6), position), (shards_of,), jnp.float32, least / len(split), high / len(split))
        factor_of = factor_of * jnp.repeat(jnp.exp(heights), extent[position] // shards_of).reshape((-1,) + (1,) * (len(extent) - 1 - position))
    return factor_of


def length_profile(number_of, total, limit, slope):
    weights = [(1 << 20) // math.isqrt(rank ** slope) + 1 for rank in range(2, number_of + 1)]
    spare, given = total - limit - (number_of - 1), [1] * (number_of - 1)
    while spare > 0:
        movable = [i for i in range(number_of - 1) if given[i] < limit]
        mass, left = sum([weights[i] for i in movable]), spare
        for i in movable:
            more = min(limit - given[i], max(1, left * weights[i] // mass), spare)
            given[i] = given[i] + more
            spare = spare - more
    return np.array([limit] + given)


def uneven(rng, amount, total, limit, skew):
    if amount == 2:
        one = jax.random.randint(rng, (), max(1, total - limit), min(limit, total - 1) + 1)
        return jnp.stack([one, total - one])
    tallies = jnp.asarray(length_profile(amount, total, limit, skew), jnp.int32)
    pairs = (amount - 1) // 2
    source_of, taker = tallies[1:1 + 2 * pairs:2], tallies[2:2 + 2 * pairs:2]
    room = jnp.minimum(source_of - 1, limit - taker)
    shifted = jax.random.randint(jax.random.fold_in(rng, 1), (pairs,), 0, 1 << 20) % (room + 1)
    tallies = tallies.at[1:1 + 2 * pairs:2].set(source_of - shifted).at[2:2 + 2 * pairs:2].set(taker + shifted)
    return tallies[jax.random.permutation(jax.random.fold_in(rng, 2), amount)]


def normal_values(rng, extent, width, most, cuts=(), held_as=jnp.bfloat16):
    values = width * jax.random.normal(rng, extent, jnp.float32)
    if cuts:
        values = values * level_of(rng, extent, cuts, -0.22, 0.18)
    return jnp.clip(values, -most, most).astype(held_as)


def setup_inputs(seed: int = 0) -> dict:
    seeds = jax.random.split(jax.random.key(seed), 9)
    tokens = normal_values(seeds[0], (TOKENS, D), 1.0, 6.0, ((0, 16),))
    segments = jax.vmap(lambda own: jnp.searchsorted(jnp.cumsum(uneven(own, 8, SEQ, SEQ // 4, 1)), jnp.arange(SEQ), side="right"))(jax.random.split(seeds[1], ROWS)).reshape((ROWS, SEQ)).astype(jnp.int32)
    qkv_weight = normal_values(seeds[2], (LAYERS, 3, D // GROUPS, D), (D // GROUPS) ** -0.5, 0.4375, ((3, 2),))
    out_weight = normal_values(seeds[3], (LAYERS, D, D), (D // 8) ** -0.5, 0.625, ((1, 2),))
    inner_weight = normal_values(seeds[4], (LAYERS, D // GROUPS, FF), (D // GROUPS) ** -0.5, 0.4375, ((2, 2),))
    outer_weight = normal_values(seeds[5], (LAYERS, FF // GROUPS, D), (FF // GROUPS) ** -0.5, 0.21875, ((2, 2),))
    norm_gains = jnp.clip(1.0 + 0.1 * jax.random.normal(seeds[6], (LAYERS, 2, D), jnp.float32), 0.5, 1.5)
    cotangent = normal_values(seeds[7], (TOKENS, D), 1.0, 6.0, ((0, 16),))
    return dict(tokens=tokens, segments=segments, qkv_weight=qkv_weight, out_weight=out_weight, inner_weight=inner_weight, outer_weight=outer_weight, norm_gains=norm_gains, cotangent=cotangent)


@jax.custom_vjp
def low(v):
    return lax.optimization_barrier(v.astype(jnp.bfloat16)).astype(jnp.float32)

@jax.custom_vjp
def low_back(v):
    return v

def low_keep(v):
    return (low(v), None)

def low_pass(kept, grad):
    return (grad,)

def back_keep(v):
    return (v, None)

def back_low(kept, grad):
    return (low(grad),)
low.defvjp(low_keep, low_pass)
low_back.defvjp(back_keep, back_low)
epsilon = 1e-12
masked_score = -1e+30
highest = lax.Precision.HIGHEST

def both_ways(values):
    return low(low_back(values))

def normalize(before, gains):
    average = lax.optimization_barrier(jnp.mean(before, axis=-1, keepdims=True))
    centered = before - average
    spread = lax.optimization_barrier(jnp.mean(centered * centered, axis=-1, keepdims=True))
    return centered * lax.rsqrt(spread + epsilon) * gains

def grouped(inputs, weight):
    in_width = weight.shape[0]
    groups = inputs.shape[1] // in_width
    in_parts = inputs.reshape(inputs.shape[0], groups, in_width)
    kernel = weight.reshape(in_width, groups, weight.shape[1] // groups)
    result = jnp.einsum('tgi,igo->tgo', in_parts, kernel, precision=highest)
    return result.reshape(inputs.shape[0], -1)

def attend_row(bundle):
    queries, key_rows, value_rows, segment_ids = bundle
    length = queries.shape[0]
    split_shape = (length, HEADS, HEAD_DIM)
    scores = jnp.einsum('qhe,khe->hqk', queries.reshape(split_shape), key_rows.reshape(split_shape), precision=highest) * HEAD_DIM ** (-0.5)
    scores = low_back(scores)
    same_doc = segment_ids[:, None] == segment_ids[None, :]
    scores = jnp.where(same_doc[None], scores, masked_score)
    maximum = lax.optimization_barrier(jnp.max(scores, axis=-1, keepdims=True))
    weights = jnp.exp(scores - maximum)
    probabilities = low(weights / lax.optimization_barrier(jnp.sum(weights, axis=-1, keepdims=True)))
    context = jnp.einsum('hqk,khe->qhe', probabilities, value_rows.reshape(split_shape), precision=highest)
    return context.reshape(length, -1)

def encoder_block(current, qkv_w, out_w, inner_w, outer_w, gains, segments):
    token_count = current.shape[0]
    low_state = low(current)
    kernel = qkv_w.reshape(3, qkv_w.shape[1], GROUPS, D // GROUPS)
    in_parts = low_state.reshape(token_count, GROUPS, D // GROUPS)
    qkv = jnp.einsum('tgi,sigo->stgo', in_parts, kernel, precision=highest).reshape(3, token_count, D)
    qkv = both_ways(qkv)
    stacked = qkv.reshape(3, token_count // SEQ, SEQ, D)
    context = lax.map(jax.checkpoint(attend_row), (stacked[0], stacked[1], stacked[2], segments))
    context = both_ways(context.reshape(token_count, D))
    pieces = context.reshape(token_count, N_HEAD, D // N_HEAD)
    partial_out = jnp.einsum('tjc,jcd->jtd', pieces, out_w.reshape(N_HEAD, D // N_HEAD, D), precision=highest)
    attention = low_back(lax.optimization_barrier(jnp.sum(low(partial_out), axis=0)))
    first = normalize(current + attention, gains[0])
    pre_act = low_back(grouped(low(first), inner_w))
    activated = both_ways(jax.nn.gelu(pre_act, approximate=False))
    branch = both_ways(grouped(activated, outer_w))
    return normalize(first + branch, gains[1])

def reference(tokens, segments, qkv_weight, out_weight, inner_weight, outer_weight, norm_gains, cotangent):

    def forward(current, qkv_w, out_w, inner_w, outer_w, gains):
        for layer_index in range(LAYERS):
            current = encoder_block(current, qkv_w[layer_index], out_w[layer_index], inner_w[layer_index], outer_w[layer_index], gains[layer_index], segments)
        return current
    result, backward = jax.vjp(forward, tokens.astype(jnp.float32), qkv_weight.astype(jnp.float32), out_weight.astype(jnp.float32), inner_weight.astype(jnp.float32), outer_weight.astype(jnp.float32), norm_gains.astype(jnp.float32))
    grads = backward(cotangent.astype(jnp.float32))
    return (result.astype(jnp.bfloat16), grads[0].astype(jnp.bfloat16), grads[1], grads[2], grads[3], grads[4], grads[5])
```

```python
import functools
import jax
import jax.numpy as jnp
from jax import lax
from jax.experimental import pallas as pl
from jax.experimental.pallas import tpu as pltpu
from jax.sharding import PartitionSpec as P

HEAD_DIM = 64
QUERY_TILE = 256
REACH = 128

epsilon = 1e-12
masked_score = -1e30
f32 = jnp.float32
bf16 = jnp.bfloat16

NN = (((1,), (0,)), ((), ()))
NT = (((1,), (1,)), ((), ()))
TN = (((0,), (0,)), ((), ()))


def mm(left, right, dims):
    return lax.dot_general(left, right, dims, preferred_element_type=f32)


def key_start(tile, seq_len):
    return min(max(tile * QUERY_TILE - REACH, 0), seq_len - QUERY_TILE - REACH)


def live_keys(tile, piece, seq_len):
    window = QUERY_TILE + REACH
    first_query = tile * QUERY_TILE + piece * REACH
    start = key_start(tile, seq_len)
    low = max(first_query - REACH - start, 0)
    high = min(first_query + 2 * REACH - start, window)
    return low, high


def block_diagonal(parts):
    rows = []
    for index, part in enumerate(parts):
        empty = jnp.zeros_like(part)
        rows.append(
            jnp.concatenate([part if at == index else empty for at in range(len(parts))], axis=1)
        )
    return jnp.concatenate(rows, axis=0)


def fill_rows(middle, low, high, total):
    pieces = []
    if low > 0:
        pieces.append(jnp.zeros((low, middle.shape[1]), middle.dtype))
    pieces.append(middle)
    if high < total:
        pieces.append(jnp.zeros((total - high, middle.shape[1]), middle.dtype))
    return jnp.concatenate(pieces, axis=0) if len(pieces) > 1 else middle


def attend_kernel(
    place, x_ref, w_ref, segq_ref, segk_ref, xt_ref, qt_ref, kt_ref, v_ref, p_ref, ct_ref
):
    seq_len, channels = x_ref.shape
    width = w_ref.shape[1]
    window = QUERY_TILE + REACH
    heads = width // HEAD_DIM
    tiles = seq_len // QUERY_TILE
    x = x_ref[...]
    xt = x.T
    xt_ref[0] = xt
    segq = segq_ref[0]
    segk = segk_ref[0]
    masks = {}
    for tile in range(tiles):
        start = key_start(tile, seq_len)
        for piece in range(QUERY_TILE // REACH):
            low, high = live_keys(tile, piece, seq_len)
            at = tile * QUERY_TILE + piece * REACH
            same = segk[start + low : start + high] == segq[:, at : at + REACH]
            masks[tile, piece] = jnp.where(same, 0.0, masked_score)
    for group in range(channels // width):
        span = slice(group * width, (group + 1) * width)
        xg = x[:, span]
        xtg = xt[span]
        wq, wk, wv = (w_ref[s][:, span] for s in range(3))
        qt = mm(wq, xtg, TN).astype(bf16) * jnp.asarray(HEAD_DIM**-0.5, bf16)
        kt = mm(wk, xtg, TN).astype(bf16)
        vt = mm(wv, xtg, TN).astype(bf16)
        keys = mm(xg, wk, NN).astype(bf16)
        values = mm(xg, wv, NN).astype(bf16)
        qt_ref[0, span] = qt
        kt_ref[0, span] = kt * jnp.asarray(HEAD_DIM**-0.5, bf16)
        v_ref[0, group] = values
        for tile in range(tiles):
            start = key_start(tile, seq_len)
            asked = slice(tile * QUERY_TILE, (tile + 1) * QUERY_TILE)
            spread = block_diagonal(
                [qt[i * HEAD_DIM : (i + 1) * HEAD_DIM, asked] for i in range(heads)]
            )
            scores = mm(keys[start : start + window], spread, NN)
            for i in range(heads):
                probs = []
                for piece in range(QUERY_TILE // REACH):
                    low, high = live_keys(tile, piece, seq_len)
                    at = i * QUERY_TILE + piece * REACH
                    s = scores[low:high, at : at + REACH] + masks[tile, piece]
                    top = jnp.max(s, axis=0, keepdims=True)
                    e = jnp.exp(s - top)
                    total = jnp.sum(e, axis=0, keepdims=True)
                    p = (e * (1.0 / total)).astype(bf16)
                    probs.append(fill_rows(p, low, high, window))
                probs = jnp.concatenate(probs, axis=1)
                p_ref[0, group, tile, :, i * QUERY_TILE : (i + 1) * QUERY_TILE] = probs
                context = mm(
                    vt[i * HEAD_DIM : (i + 1) * HEAD_DIM, start : start + window], probs, NN
                )
                at = group * width + i * HEAD_DIM
                ct_ref[0, at : at + HEAD_DIM, asked] = context.astype(bf16)


def attend_back_kernel(
    last,
    place,
    dc_ref,
    ct_ref,
    p_ref,
    qt_ref,
    kt_ref,
    v_ref,
    xt_ref,
    w_ref,
    dz_ref,
    dx_ref,
    grad_ref,
    ds_ref,
):
    channels, seq_len = xt_ref.shape[1:]
    width = w_ref.shape[1]
    window = QUERY_TILE + REACH
    heads = width // HEAD_DIM
    tiles = seq_len // QUERY_TILE
    step = pl.program_id(0)
    grads = [[], [], []]
    d_inputs = []
    for group in range(channels // width):
        span = slice(group * width, (group + 1) * width)
        dq_tiles = []
        dk_tiles = []
        dv_tiles = []
        for tile in range(tiles):
            start = key_start(tile, seq_len)
            asked = slice(tile * QUERY_TILE, (tile + 1) * QUERY_TILE)
            d_context = dc_ref[0, span, asked]
            context = ct_ref[0, span, asked]
            both = d_context.astype(f32) * context.astype(f32)
            spread_dc = block_diagonal(
                [d_context[i * HEAD_DIM : (i + 1) * HEAD_DIM] for i in range(heads)]
            )
            qt = qt_ref[0, span, asked]
            spread_q = block_diagonal(
                [qt[i * HEAD_DIM : (i + 1) * HEAD_DIM] for i in range(heads)]
            )
            d_probs = mm(v_ref[0, group, start : start + window], spread_dc, NN)
            dq_heads = []
            for i in range(heads):
                shared = jnp.sum(both[i * HEAD_DIM : (i + 1) * HEAD_DIM], axis=0, keepdims=True)
                for piece in range(QUERY_TILE // REACH):
                    low, high = live_keys(tile, piece, seq_len)
                    at = i * QUERY_TILE + piece * REACH
                    p = p_ref[0, group, tile, low:high, at : at + REACH].astype(f32)
                    dp = d_probs[low:high, at : at + REACH]
                    ds = (p * (dp - shared[:, piece * REACH : (piece + 1) * REACH])).astype(bf16)
                    ds_ref[:, at : at + REACH] = fill_rows(ds, low, high, window)
                rows = slice(group * width + i * HEAD_DIM, group * width + (i + 1) * HEAD_DIM)
                dq_heads.append(
                    mm(
                        kt_ref[0, rows, start : start + window],
                        ds_ref[:, i * QUERY_TILE : (i + 1) * QUERY_TILE],
                        NN,
                    )
                )
            dq_tiles.append(jnp.concatenate(dq_heads, axis=0))
            dk_tiles.append(mm(ds_ref[...], spread_q, NT))
            dv_tiles.append(mm(p_ref[0, group, tile], spread_dc, NT))
        dq = jnp.concatenate(dq_tiles, axis=1).astype(bf16)
        dk = join_windows(dk_tiles, seq_len).astype(bf16)
        dv = join_windows(dv_tiles, seq_len).astype(bf16)
        xtg = xt_ref[0, span]
        grads[0].append(mm(xtg, dq, NT))
        grads[1].append(mm(xtg, dk, NN))
        grads[2].append(mm(xtg, dv, NN))
        wq, wk, wv = (w_ref[s][:, span] for s in range(3))
        d_inputs.append(
            dz_ref[0, 0, span] + mm(wq, dq, NN) + mm(wk, dk, NT) + mm(wv, dv, NT)
        )
    joined = [jnp.concatenate(parts, axis=1) for parts in grads]

    @pl.when(step == 0)
    def _():
        for s in range(3):
            grad_ref[s] = joined[s]

    @pl.when(step > 0)
    def _():
        for s in range(3):
            grad_ref[s] += joined[s]

    d_input = jnp.concatenate(d_inputs, axis=0)
    if last:
        dx_ref[...] = d_input.astype(bf16).T
    else:
        dx_ref[0] = d_input


def join_windows(pieces, seq_len):
    window = QUERY_TILE + REACH
    rows = []
    for at in range(0, seq_len, REACH):
        held = []
        for tile, piece in enumerate(pieces):
            start = key_start(tile, seq_len)
            if start <= at < start + window:
                held.append(piece[at - start : at - start + REACH])
        rows.append(functools.reduce(jnp.add, held))
    return jnp.concatenate(rows, axis=0)


def feature_mean(values):
    return jnp.sum(values, axis=0, keepdims=True) * (1.0 / values.shape[0])


def normalize(before):
    centered = before - feature_mean(before)
    inverse = lax.rsqrt(feature_mean(centered * centered) + epsilon)
    return centered * inverse, inverse


def normalize_back(gradient, gains, normal, inverse):
    scaled = gradient * gains
    return inverse * (scaled - feature_mean(scaled) - normal * feature_mean(scaled * normal))


def ffn_kernel(first_layer, place, *refs):
    if first_layer:
        xt0, xt1, *refs = refs
    else:
        x_ref, *refs = refs
    (ct0, ct1, ow0, ow1, iw0, iw1, uw0, uw1, gains, *refs) = refs
    (n1_ref, r1_ref, act_ref, slope_ref, n2_ref, r2_ref, tok_ref, *refs) = refs
    if first_layer:
        next_ref, *refs = refs
    z_scr, fb_scr = refs
    half, seq_len = z_scr.shape[1:]
    wide = 2 * half
    width = iw0.shape[0]
    own = place[0]
    sides = (own, 1 - own)
    attention = mm(ow0[...], ct0[0], TN) + mm(ow1[...], ct1[0], TN)
    z_scr[...] = attention.reshape(2, half, seq_len)
    if first_layer:
        z_scr[sides[0]] += xt0[0].astype(f32)
        z_scr[sides[1]] += xt1[0].astype(f32)
        before = z_scr[...].reshape(wide, seq_len)
    else:
        before = (z_scr[...] + x_ref[0]).reshape(wide, seq_len)
    normal, inverse = normalize(before)
    first = normal * gains[0]
    n1_ref[0] = normal.reshape(2, half, seq_len)
    r1_ref[0] = inverse
    z_scr[...] = first.reshape(2, half, seq_len)
    fb_scr[...] = first.astype(bf16).reshape(2, half, seq_len)
    for j, (iw, uw) in enumerate(((iw0, uw0), (iw1, uw1))):
        hidden = iw.shape[1] // (half // width)
        for group in range(half // width):
            span = slice(group * width, (group + 1) * width)
            pre = mm(iw[:, group * hidden : (group + 1) * hidden], fb_scr[sides[j], span], TN)
            below = 0.5 + 0.5 * lax.erf(pre * 0.7071067811865476)
            act = (pre * below).astype(bf16)
            slope = below + pre * (jnp.exp(-0.5 * pre * pre) * 0.3989422804014327)
            act_ref[0, j, group] = act
            slope_ref[0, j, group] = slope.astype(bf16)
            z_scr[sides[j], span] += mm(uw[:, span], act, TN)
    normal, inverse = normalize(z_scr[...].reshape(wide, seq_len))
    n2_ref[0] = normal.reshape(2, half, seq_len)
    r2_ref[0] = inverse
    output = normal * gains[1]
    if first_layer:
        next_ref[0] = output.reshape(2, half, seq_len)
    tok_ref[...] = output.astype(bf16).T


def ffn_back_kernel(last_layer, place, *refs):
    if last_layer:
        cot_ref, *refs = refs
    else:
        g0, g1, *refs = refs
    (n2_ref, r2_ref, act_ref, slope_ref, n1_ref, r1_ref, ct0, ct1, *refs) = refs
    (ow0, ow1, iw0, iw1, uw0, uw1, gains, *refs) = refs
    (dz1_ref, dc0, dc1, outer_ref, inner_ref, out_ref, gain_ref, d_scr, b_scr, f_scr) = refs
    half, seq_len = d_scr.shape[1:]
    wide = 2 * half
    width = iw0.shape[0]
    own = place[0]
    sides = (own, 1 - own)
    step = pl.program_id(0)

    @pl.when(step == 0)
    def _():
        outer_ref[...] = jnp.zeros_like(outer_ref)
        inner_ref[...] = jnp.zeros_like(inner_ref)
        out_ref[...] = jnp.zeros_like(out_ref)
        gain_ref[...] = jnp.zeros_like(gain_ref)

    if last_layer:
        g = cot_ref[...].T.astype(f32)
    else:
        d_scr[sides[0]] = g0[0]
        d_scr[sides[1]] = g1[0]
        g = d_scr[...].reshape(wide, seq_len)
    normal = n2_ref[0].reshape(wide, seq_len)
    gain_ref[1] += jnp.sum(g * normal, axis=1, keepdims=True)
    d_second = normalize_back(g, gains[1], normal, r2_ref[0])
    d_scr[...] = d_second.reshape(2, half, seq_len)
    b_scr[...] = d_second.astype(bf16).reshape(2, half, seq_len)
    normal = n1_ref[0].reshape(wide, seq_len)
    f_scr[...] = (normal * gains[0]).astype(bf16).reshape(2, half, seq_len)
    for j, (iw, uw) in enumerate(((iw0, uw0), (iw1, uw1))):
        hidden = iw.shape[1] // (half // width)
        outers = []
        for group in range(half // width):
            span = slice(group * width, (group + 1) * width)
            units = slice(group * hidden, (group + 1) * hidden)
            d_branch = b_scr[sides[j], span]
            first = f_scr[sides[j], span]
            outers.append(mm(act_ref[0, j, group], d_branch, NT))
            d_act = mm(uw[:, span], d_branch, NN)
            d_pre = (d_act * slope_ref[0, j, group].astype(f32)).astype(bf16)
            inner_ref[j, :, units] += mm(first, d_pre, NT)
            d_scr[sides[j], span] += mm(iw[:, units], d_pre, NN)
        outer_ref[j] += jnp.concatenate(outers, axis=1)
    d_first = d_scr[...].reshape(wide, seq_len)
    gain_ref[0] += jnp.sum(d_first * normal, axis=1, keepdims=True)
    d_before = normalize_back(d_first, gains[0], normal, r1_ref[0])
    dz1_ref[0] = d_before.reshape(2, half, seq_len)
    d_attention = d_before.astype(bf16)
    for j, (ow, ct, dc) in enumerate(((ow0, ct0, dc0), (ow1, ct1, dc1))):
        out_ref[j] += mm(ct[0], d_attention, NT)
        dc[0] = mm(ow[...], d_attention, NN).astype(bf16)


def whole(shape):
    return pl.BlockSpec(shape, lambda r, place: (0,) * len(shape))


def per_row(shape):
    rest = (0,) * (len(shape) - 1)
    return pl.BlockSpec((1,) + tuple(shape[1:]), lambda r, place: (r,) + rest)


def struct(shape, dtype):
    return jax.ShapeDtypeStruct(shape, dtype)


def call(kernel, rows, place, operands, in_specs, outs, out_specs, scratch, name):
    return pl.pallas_call(
        kernel,
        out_shape=outs,
        grid_spec=pltpu.PrefetchScalarGridSpec(
            num_scalar_prefetch=1,
            grid=(rows,),
            in_specs=in_specs,
            out_specs=out_specs,
            scratch_shapes=scratch,
        ),
        compiler_params=pltpu.CompilerParams(vmem_limit_bytes=60 * 2**20),
        name=name,
    )(place, *operands)


def attend(x_tok, w, segq, segk, place, rows):
    seq_len = segq.shape[-1]
    channels = w.shape[-1]
    width = w.shape[1]
    heads = width // HEAD_DIM
    groups = channels // width
    tiles = seq_len // QUERY_TILE
    window = QUERY_TILE + REACH
    outs = [
        struct((rows, channels, seq_len), bf16),
        struct((rows, channels, seq_len), bf16),
        struct((rows, channels, seq_len), bf16),
        struct((rows, groups, seq_len, width), bf16),
        struct((rows, groups, tiles, window, heads * QUERY_TILE), bf16),
        struct((rows, channels, seq_len), bf16),
    ]
    return call(
        attend_kernel,
        rows,
        place,
        (x_tok, w, segq, segk),
        [
            pl.BlockSpec((seq_len, channels), lambda r, place: (place[0] + r, place[1])),
            whole(w.shape),
            pl.BlockSpec((1, 1, seq_len), lambda r, place: (place[2] + r, 0, 0)),
            pl.BlockSpec((1, seq_len, 1), lambda r, place: (place[2] + r, 0, 0)),
        ],
        outs,
        [per_row(o.shape) for o in outs],
        [],
        "attend",
    )


def attend_back(d_context, saved, w, d_before, place, rows, last):
    xt, qt, kt, values, probs, ct = saved
    channels, seq_len = xt.shape[1:]
    window = QUERY_TILE + REACH
    heads = w.shape[1] // HEAD_DIM
    if last:
        dx = struct((rows * seq_len, channels), bf16)
        dx_spec = pl.BlockSpec((seq_len, channels), lambda r, place: (r, 0))
    else:
        dx = struct((rows, channels, seq_len), f32)
        dx_spec = per_row(dx.shape)
    operands = (d_context, ct, probs, qt, kt, values, xt)
    return call(
        functools.partial(attend_back_kernel, last),
        rows,
        place,
        operands + (w, d_before),
        [per_row(o.shape) for o in operands]
        + [
            whole(w.shape),
            pl.BlockSpec((1, 1, channels, seq_len), lambda r, place: (r, place[1], 0, 0)),
        ],
        [dx, struct(w.shape, f32)],
        [dx_spec, whole(w.shape)],
        [pltpu.VMEM((window, heads * QUERY_TILE), bf16)],
        "attend_back",
    )


def ffn(x_parts, contexts, weights, gains, place, rows, first_layer):
    half, seq_len = contexts[0].shape[1:]
    hidden = weights[2].shape[1] * 2 // (2 * (half // weights[2].shape[0]))
    groups = half // weights[2].shape[0]
    stream = (rows, 2, half, seq_len)
    acts = (rows, 2, groups, hidden, seq_len)
    outs = [
        struct(stream, f32),
        struct((rows, 1, seq_len), f32),
        struct(acts, bf16),
        struct(acts, bf16),
        struct(stream, f32),
        struct((rows, 1, seq_len), f32),
        struct((rows * seq_len, 2 * half), bf16),
    ]
    out_specs = [per_row(o.shape) for o in outs]
    out_specs[-1] = pl.BlockSpec((seq_len, 2 * half), lambda r, place: (r, 0))
    if first_layer:
        outs.append(struct(stream, f32))
        out_specs.append(per_row(stream))
    return call(
        functools.partial(ffn_kernel, first_layer),
        rows,
        place,
        tuple(x_parts) + tuple(contexts) + tuple(weights) + (gains,),
        [per_row(o.shape) for o in x_parts]
        + [per_row(o.shape) for o in contexts]
        + [whole(o.shape) for o in weights]
        + [whole(gains.shape)],
        outs,
        out_specs,
        [pltpu.VMEM((2, half, seq_len), f32), pltpu.VMEM((2, half, seq_len), bf16)],
        "ffn",
    )


def ffn_back(g_parts, saved, contexts, weights, gains, place, rows, last_layer):
    half, seq_len = contexts[0].shape[1:]
    if last_layer:
        g_specs = [pl.BlockSpec((seq_len, 2 * half), lambda r, place: (place[1] + r, 0))]
    else:
        g_specs = [per_row(o.shape) for o in g_parts]
    stream = (rows, 2, half, seq_len)
    ow, iw, uw = weights[0], weights[2], weights[4]
    grad_shapes = [(2,) + uw.shape, (2,) + iw.shape, (2,) + ow.shape, gains.shape]
    outs = [
        struct(stream, f32),
        struct(contexts[0].shape, bf16),
        struct(contexts[0].shape, bf16),
    ]
    out_specs = [per_row(o.shape) for o in outs] + [whole(s) for s in grad_shapes]
    outs += [struct(s, f32) for s in grad_shapes]
    operands = tuple(saved) + tuple(contexts)
    return call(
        functools.partial(ffn_back_kernel, last_layer),
        rows,
        place,
        tuple(g_parts) + operands + tuple(weights) + (gains,),
        g_specs
        + [per_row(o.shape) for o in operands]
        + [whole(o.shape) for o in weights]
        + [whole(gains.shape)],
        outs,
        out_specs,
        [
            pltpu.VMEM((2, half, seq_len), f32),
            pltpu.VMEM((2, half, seq_len), bf16),
            pltpu.VMEM((2, half, seq_len), bf16),
        ],
        "ffn_back",
    )


def swap(values):
    return lax.ppermute(values, "head", [(0, 1), (1, 0)])


def shards(
    tokens, segments, qkv_weight, out_weight, inner_weight, outer_weight, norm_gains, cotangent
):
    head_place = lax.axis_index("head").astype(jnp.int32)
    layers = qkv_weight.shape[0]
    row_total, seq_len = segments.shape
    rows = row_total // 2
    offset = head_place * rows
    segq = segments.reshape(row_total, 1, seq_len)
    segk = segments.reshape(row_total, seq_len, 1)
    gains = norm_gains[..., None]
    zero = jnp.zeros((), jnp.int32)
    far_qkv = [swap(qkv_weight[i]) for i in range(layers)]
    far_rest = [
        [swap(w[i]) for w in (out_weight, inner_weight, outer_weight)] for i in range(layers)
    ]
    ffn_weights = []
    for i in range(layers):
        both = []
        for near, far in zip((out_weight, inner_weight, outer_weight), far_rest[i]):
            both += [near[i], far]
        ffn_weights.append(both)
    sides = (head_place, 1 - head_place)
    x_tok = tokens
    x_stream = None
    saved_attend = []
    saved_ffn = []
    contexts = []
    for i in range(layers):
        held = []
        for j, w in enumerate((qkv_weight[i], far_qkv[i])):
            place = jnp.stack([offset if i == 0 else zero, sides[j], offset])
            held.append(attend(x_tok, w, segq, segk, place, rows))
        saved_attend.append(held)
        contexts.append([h[5] for h in held])
        first_layer = i == 0
        x_parts = [h[0] for h in held] if first_layer else [x_stream]
        place = jnp.stack([head_place, offset])
        results = ffn(x_parts, contexts[i], ffn_weights[i], gains[i], place, rows, i < layers - 1)
        n1, r1, act, slope, n2, r2, x_tok = results[:7]
        if i < layers - 1:
            x_stream = results[7]
        saved_ffn.append((n2, r2, act, slope, n1, r1))
    far_tok = swap(x_tok)
    activations = in_order(x_tok, far_tok, head_place)
    g_parts = [cotangent]
    grads = [None] * layers
    for i in reversed(range(layers)):
        place = jnp.stack([head_place, offset])
        d_before, dc0, dc1, outer, inner, out, gain = ffn_back(
            g_parts, saved_ffn[i], contexts[i], ffn_weights[i], gains[i], place, rows, i == layers - 1
        )
        g_parts = []
        qkv = []
        for j, (w, dc) in enumerate(((qkv_weight[i], dc0), (far_qkv[i], dc1))):
            place = jnp.stack([zero, sides[j], zero])
            dx, grad = attend_back(dc, saved_attend[i][j], w, d_before, place, rows, i == 0)
            g_parts.append(dx)
            qkv.append(grad)
        grads[i] = (qkv, out, inner, outer, gain[..., 0])
    mine = jnp.where(head_place == 0, jnp.concatenate(g_parts, 1), jnp.concatenate(g_parts[::-1], 1))
    input_grad = in_order(mine, swap(mine), head_place)
    totals = []
    for at in range(4):
        near = jnp.stack([g[at][0] for g in grads])
        far = jnp.stack([g[at][1] for g in grads])
        totals.append(near + swap(far.astype(bf16)).astype(f32))
    totals = lax.psum(tuple(totals), "dp")
    gain_total = lax.psum(jnp.stack([g[4] for g in grads]), ("dp", "head"))
    return (activations, input_grad, *totals, gain_total)


def in_order(near, far, head_place):
    return jnp.where(
        head_place == 0, jnp.concatenate([near, far]), jnp.concatenate([far, near])
    )


def solution(mesh):
    return jax.shard_map(
        shards,
        mesh=mesh,
        in_specs=(
            P("dp", None),
            P("dp", None),
            P(None, None, None, "head"),
            P(None, "head", None),
            P(None, None, "head"),
            P(None, None, "head"),
            P(),
            P("dp", None),
        ),
        out_specs=(
            P("dp", None),
            P("dp", None),
            P(None, None, None, "head"),
            P(None, "head", None),
            P(None, None, "head"),
            P(None, None, "head"),
            P(),
        ),
        check_vma=False,
    )
```

```python
import functools
import jax
import jax.numpy as jnp
from jax import lax
from jax.experimental import pallas as pl
from jax.experimental.pallas import tpu as pltpu
from jax.sharding import PartitionSpec as P

HEAD_DIM = 64
QUERY_TILE = 256
REACH = 128

SELF, OTHER, OFFSET, CORE, ROW = range(5)

epsilon = 1e-12
masked_score = -1e30
f32 = jnp.float32
bf16 = jnp.bfloat16

NN = (((1,), (0,)), ((), ()))
NT = (((1,), (1,)), ((), ()))
TN = (((0,), (0,)), ((), ()))


def mm(left, right, dims):
    return lax.dot_general(left, right, dims, preferred_element_type=f32)


def key_start(tile, seq_len):
    return min(max(tile * QUERY_TILE - REACH, 0), seq_len - QUERY_TILE - REACH)


def live_keys(tile, piece, seq_len):
    window = QUERY_TILE + REACH
    first_query = tile * QUERY_TILE + piece * REACH
    start = key_start(tile, seq_len)
    low = max(first_query - REACH - start, 0)
    high = min(first_query + 2 * REACH - start, window)
    return low, high


def block_diagonal(parts):
    rows = []
    for index, part in enumerate(parts):
        empty = jnp.zeros_like(part)
        rows.append(
            jnp.concatenate([part if at == index else empty for at in range(len(parts))], axis=1)
        )
    return jnp.concatenate(rows, axis=0)


def fill_rows(middle, low, high, total):
    pieces = []
    if low > 0:
        pieces.append(jnp.zeros((low, middle.shape[1]), middle.dtype))
    pieces.append(middle)
    if high < total:
        pieces.append(jnp.zeros((total - high, middle.shape[1]), middle.dtype))
    return jnp.concatenate(pieces, axis=0) if len(pieces) > 1 else middle


def across(row):
    return jnp.broadcast_to(row, (128, row.shape[1])).T


def attend_kernel(place, x_ref, w_ref, seg_ref, xt_ref, qt_ref, kt_ref, v_ref, p_ref, ct_ref):
    seq_len, channels = x_ref.shape
    width = w_ref.shape[1]
    window = QUERY_TILE + REACH
    heads = width // HEAD_DIM
    tiles = seq_len // QUERY_TILE
    x = x_ref[...]
    xt = x.T
    xt_ref[0] = xt
    segq = seg_ref[pl.ds(place[OFFSET] + pl.program_id(0), 1), :].astype(f32)
    segk = across(segq)
    masks = {}
    for tile in range(tiles):
        start = key_start(tile, seq_len)
        for piece in range(QUERY_TILE // REACH):
            low, high = live_keys(tile, piece, seq_len)
            at = tile * QUERY_TILE + piece * REACH
            same = segk[start + low : start + high] == segq[:, at : at + REACH]
            masks[tile, piece] = jnp.where(same, 0.0, masked_score)
    for group in range(channels // width):
        span = slice(group * width, (group + 1) * width)
        xg = x[:, span]
        xtg = xt[span]
        wq, wk, wv = (w_ref[s][:, span] for s in range(3))
        qt = mm(wq, xtg, TN).astype(bf16) * jnp.asarray(HEAD_DIM**-0.5, bf16)
        kt = mm(wk, xtg, TN).astype(bf16)
        vt = mm(wv, xtg, TN).astype(bf16)
        keys = mm(xg, wk, NN).astype(bf16)
        values = mm(xg, wv, NN).astype(bf16)
        qt_ref[0, span] = qt
        kt_ref[0, span] = kt * jnp.asarray(HEAD_DIM**-0.5, bf16)
        v_ref[0, group] = values
        for tile in range(tiles):
            start = key_start(tile, seq_len)
            asked = slice(tile * QUERY_TILE, (tile + 1) * QUERY_TILE)
            spread = block_diagonal(
                [qt[i * HEAD_DIM : (i + 1) * HEAD_DIM, asked] for i in range(heads)]
            )
            scores = mm(keys[start : start + window], spread, NN)
            for i in range(heads):
                probs = []
                for piece in range(QUERY_TILE // REACH):
                    low, high = live_keys(tile, piece, seq_len)
                    at = i * QUERY_TILE + piece * REACH
                    s = scores[low:high, at : at + REACH] + masks[tile, piece]
                    top = jnp.max(s, axis=0, keepdims=True)
                    e = jnp.exp(s - top)
                    total = jnp.sum(e, axis=0, keepdims=True)
                    p = (e * (1.0 / total)).astype(bf16)
                    probs.append(fill_rows(p, low, high, window))
                probs = jnp.concatenate(probs, axis=1)
                p_ref[0, group, tile, :, i * QUERY_TILE : (i + 1) * QUERY_TILE] = probs
                context = mm(
                    vt[i * HEAD_DIM : (i + 1) * HEAD_DIM, start : start + window], probs, NN
                )
                at = group * width + i * HEAD_DIM
                ct_ref[0, at : at + HEAD_DIM, asked] = context.astype(bf16)


def attend_back_kernel(
    last,
    aliased,
    place,
    dc_ref,
    ct_ref,
    p_ref,
    qt_ref,
    kt_ref,
    v_ref,
    xt_ref,
    w_ref,
    dz_ref,
    *refs,
):
    if last:
        later_ref, gain0_ref, gain1_ref, *refs = refs
        if aliased:
            _, *refs = refs
        dx_ref, full_ref, keep_ref, send_ref, grad_ref, ds_ref = refs
    else:
        dx_ref, grad_ref, ds_ref = refs
    channels, seq_len = xt_ref.shape[1:]
    width = w_ref.shape[1]
    window = QUERY_TILE + REACH
    heads = width // HEAD_DIM
    tiles = seq_len // QUERY_TILE
    step = pl.program_id(0)
    grads = [[], [], []]
    d_inputs = []
    for group in range(channels // width):
        span = slice(group * width, (group + 1) * width)
        dq_tiles = []
        dk_tiles = []
        dv_tiles = []
        for tile in range(tiles):
            start = key_start(tile, seq_len)
            asked = slice(tile * QUERY_TILE, (tile + 1) * QUERY_TILE)
            d_context = dc_ref[0, span, asked]
            context = ct_ref[0, span, asked]
            both = d_context.astype(f32) * context.astype(f32)
            spread_dc = block_diagonal(
                [d_context[i * HEAD_DIM : (i + 1) * HEAD_DIM] for i in range(heads)]
            )
            qt = qt_ref[0, span, asked]
            spread_q = block_diagonal(
                [qt[i * HEAD_DIM : (i + 1) * HEAD_DIM] for i in range(heads)]
            )
            d_probs = mm(v_ref[0, group, start : start + window], spread_dc, NN)
            dq_heads = []
            for i in range(heads):
                shared = jnp.sum(both[i * HEAD_DIM : (i + 1) * HEAD_DIM], axis=0, keepdims=True)
                for piece in range(QUERY_TILE // REACH):
                    low, high = live_keys(tile, piece, seq_len)
                    at = i * QUERY_TILE + piece * REACH
                    p = p_ref[0, group, tile, low:high, at : at + REACH].astype(f32)
                    dp = d_probs[low:high, at : at + REACH]
                    ds = (p * (dp - shared[:, piece * REACH : (piece + 1) * REACH])).astype(bf16)
                    ds_ref[:, at : at + REACH] = fill_rows(ds, low, high, window)
                rows = slice(group * width + i * HEAD_DIM, group * width + (i + 1) * HEAD_DIM)
                dq_heads.append(
                    mm(
                        kt_ref[0, rows, start : start + window],
                        ds_ref[:, i * QUERY_TILE : (i + 1) * QUERY_TILE],
                        NN,
                    )
                )
            dq_tiles.append(jnp.concatenate(dq_heads, axis=0))
            dk_tiles.append(mm(ds_ref[...], spread_q, NT))
            dv_tiles.append(mm(p_ref[0, group, tile], spread_dc, NT))
        dq = jnp.concatenate(dq_tiles, axis=1).astype(bf16)
        dk = join_windows(dk_tiles, seq_len).astype(bf16)
        dv = join_windows(dv_tiles, seq_len).astype(bf16)
        xtg = xt_ref[0, span]
        grads[0].append(mm(xtg, dq, NT))
        grads[1].append(mm(xtg, dk, NN))
        grads[2].append(mm(xtg, dv, NN))
        wq, wk, wv = (w_ref[s][:, span] for s in range(3))
        d_inputs.append(
            dz_ref[0, 0, span] + mm(wq, dq, NN) + mm(wk, dk, NT) + mm(wv, dv, NT)
        )
    joined = [jnp.concatenate(parts, axis=1) for parts in grads]

    @pl.when(step == 0)
    def _():
        for s in range(3):
            grad_ref[s] = joined[s]

    @pl.when(step > 0)
    def _():
        for s in range(3):
            grad_ref[s] += joined[s]

    d_input = jnp.concatenate(d_inputs, axis=0)
    if not last:
        dx_ref[0] = d_input
        return
    tok = d_input.astype(bf16).T
    dx_ref[...] = tok
    full_ref[...] = tok

    @pl.when(step == pl.num_programs(0) - 1)
    def _():
        piece = width // 4
        gain_rows = jnp.concatenate([gain0_ref[...], gain1_ref[...]], axis=0).astype(bf16)
        gain_rows = jnp.concatenate([gain_rows[:, :channels], gain_rows[:, channels:]], axis=0)
        for c, out_ref in enumerate((keep_ref, send_ref)):
            for y in range(2):
                at = ((place[CORE] ^ c) * 2 + (place[ROW] ^ y)) * piece
                rows = pl.ds(pl.multiple_of(at, piece), piece)
                for layer, source in enumerate((grad_ref, later_ref)):
                    for s in range(3):
                        out_ref[y, pl.ds((layer * 3 + s) * piece, piece)] = source[
                            s, rows
                        ].astype(bf16)
                out_ref[y, pl.ds(6 * piece, 16)] = gain_rows


def join_windows(pieces, seq_len):
    window = QUERY_TILE + REACH
    rows = []
    for at in range(0, seq_len, REACH):
        held = []
        for tile, piece in enumerate(pieces):
            start = key_start(tile, seq_len)
            if start <= at < start + window:
                held.append(piece[at - start : at - start + REACH])
        rows.append(functools.reduce(jnp.add, held))
    return jnp.concatenate(rows, axis=0)


def feature_mean(values):
    return jnp.sum(values, axis=0, keepdims=True) * (1.0 / values.shape[0])


def normalize(before):
    centered = before - feature_mean(before)
    inverse = lax.rsqrt(feature_mean(centered * centered) + epsilon)
    return centered * inverse, inverse


def normalize_back(gradient, gains, normal, inverse):
    scaled = gradient * gains
    return inverse * (scaled - feature_mean(scaled) - normal * feature_mean(scaled * normal))


def gather_far(place, x_ref, c_ref, scr):
    scr[place[CORE]] = x_ref[...]
    scr[1 - place[CORE]] = c_ref[...]


def out_rows(pack):
    rows = pack[:, 0]
    return rows.reshape(2 * rows.shape[1], rows.shape[2])


def inner_rows(pack, group):
    return pack[group, 1]


def outer_rows(pack, group, width):
    rows = pack[:, 2]
    rows = rows.reshape(2 * rows.shape[1], rows.shape[2])
    half = rows.shape[1] // 2
    at = group * width
    return jnp.concatenate([rows[:, at : at + width], rows[:, half + at : half + at + width]], axis=0)


def spread_gains(gains_ref, layer, g_scr):
    for i in range(2):
        g_scr[i] = across(gains_ref[layer, i : i + 1, :])


def wide_gain(g_scr, i, seq_len):
    return jnp.concatenate([g_scr[i]] * (seq_len // 128), axis=1)


def ffn_kernel(layer, more, place, *refs):
    if layer == 0:
        xt0, xt1, *refs = refs
    else:
        x_ref, *refs = refs
    (ct0, ct1, near_ref, farx_ref, farc_ref, gains_ref, *refs) = refs
    (n1_ref, r1_ref, act_ref, slope_ref, n2_ref, r2_ref, tok_ref, next_ref, *refs) = refs
    z_scr, fb_scr, far_scr, g_scr = refs
    half, seq_len = z_scr.shape[1:]
    wide = 2 * half
    width = half // 2
    sides = (place[SELF], place[OTHER])

    @pl.when(pl.program_id(0) == 0)
    def _():
        gather_far(place, farx_ref, farc_ref, far_scr)
        spread_gains(gains_ref, layer, g_scr)

    packs = (near_ref, far_scr)
    attention = mm(out_rows(packs[0]), ct0[0], TN) + mm(out_rows(packs[1]), ct1[0], TN)
    z_scr[...] = attention.reshape(2, half, seq_len)
    if layer == 0:
        z_scr[sides[0]] += xt0[0].astype(f32)
        z_scr[sides[1]] += xt1[0].astype(f32)
        before = z_scr[...].reshape(wide, seq_len)
    else:
        before = (z_scr[...] + x_ref[0]).reshape(wide, seq_len)
    normal, inverse = normalize(before)
    first = normal * wide_gain(g_scr, 0, seq_len)
    n1_ref[0] = normal.reshape(2, half, seq_len)
    r1_ref[0] = inverse
    z_scr[...] = first.reshape(2, half, seq_len)
    fb_scr[...] = first.astype(bf16).reshape(2, half, seq_len)
    for j, pack in enumerate(packs):
        for group in range(half // width):
            span = slice(group * width, (group + 1) * width)
            pre = mm(inner_rows(pack, group), fb_scr[sides[j], span], TN)
            below = 0.5 + 0.5 * lax.erf(pre * 0.7071067811865476)
            act = (pre * below).astype(bf16)
            slope = below + pre * (jnp.exp(-0.5 * pre * pre) * 0.3989422804014327)
            act_ref[0, j, group] = act
            slope_ref[0, j, group] = slope.astype(bf16)
            z_scr[sides[j], span] += mm(outer_rows(pack, group, width), act, TN)
    normal, inverse = normalize(z_scr[...].reshape(wide, seq_len))
    n2_ref[0] = normal.reshape(2, half, seq_len)
    r2_ref[0] = inverse
    output = normal * wide_gain(g_scr, 1, seq_len)
    tok = output.astype(bf16).T
    tok_ref[...] = tok
    if more:
        next_ref[0] = output.reshape(2, half, seq_len)
    else:
        next_ref[...] = tok


def ffn_back_kernel(layer, more, place, *refs):
    if more:
        g0, g1, *refs = refs
    else:
        cot_ref, *refs = refs
    (n2_ref, r2_ref, act_ref, slope_ref, n1_ref, r1_ref, ct0, ct1, *refs) = refs
    (near_ref, farx_ref, farc_ref, gains_ref, *refs) = refs
    (dz1_ref, dc0, dc1, keep_ref, send_ref, gain_ref, *refs) = refs
    d_scr, b_scr, f_scr, far_scr, g_scr, acc, gain_acc = refs
    half, seq_len = d_scr.shape[1:]
    wide = 2 * half
    width = half // 2
    sides = (place[SELF], place[OTHER])
    step = pl.program_id(0)

    @pl.when(step == 0)
    def _():
        gather_far(place, farx_ref, farc_ref, far_scr)
        spread_gains(gains_ref, layer, g_scr)
        acc[...] = jnp.zeros_like(acc)
        gain_acc[...] = jnp.zeros_like(gain_acc)

    packs = (near_ref, far_scr)
    if more:
        d_scr[sides[0]] = g0[0]
        d_scr[sides[1]] = g1[0]
        g = d_scr[...].reshape(wide, seq_len)
    else:
        g = cot_ref[...].T.astype(f32)
    normal = n2_ref[0].reshape(wide, seq_len)
    gain_acc[1] += lane_sum(g * normal)
    d_second = normalize_back(g, wide_gain(g_scr, 1, seq_len), normal, r2_ref[0])
    d_scr[...] = d_second.reshape(2, half, seq_len)
    b_scr[...] = d_second.astype(bf16).reshape(2, half, seq_len)
    normal = n1_ref[0].reshape(wide, seq_len)
    gain1 = wide_gain(g_scr, 0, seq_len)
    f_scr[...] = (normal * gain1).astype(bf16).reshape(2, half, seq_len)
    for j, pack in enumerate(packs):
        outers = []
        for group in range(half // width):
            span = slice(group * width, (group + 1) * width)
            d_branch = b_scr[sides[j], span]
            first = f_scr[sides[j], span]
            outers.append(mm(act_ref[0, j, group], d_branch, NT))
            d_act = mm(outer_rows(pack, group, width), d_branch, NN)
            d_pre = (d_act * slope_ref[0, j, group].astype(f32)).astype(bf16)
            acc[j, 1, span] += mm(first, d_pre, NT)
            d_scr[sides[j], span] += mm(inner_rows(pack, group), d_pre, NN)
        acc[j, 2] += jnp.concatenate(
            [o[:half] for o in outers] + [o[half:] for o in outers], axis=1
        )
    d_first = d_scr[...].reshape(wide, seq_len)
    gain_acc[0] += lane_sum(d_first * normal)
    d_before = normalize_back(d_first, gain1, normal, r1_ref[0])
    dz1_ref[0] = d_before.reshape(2, half, seq_len)
    d_attention = d_before.astype(bf16)
    for j, (pack, ct, dc) in enumerate(zip(packs, (ct0, ct1), (dc0, dc1))):
        acc[j, 0] += mm(ct[0], d_attention, NT)
        dc[0] = mm(out_rows(pack), d_attention, NN).astype(bf16)

    @pl.when(step == pl.num_programs(0) - 1)
    def _():
        piece = half // 8
        for c, out_ref in enumerate((keep_ref, send_ref)):
            for s in range(2):
                for j in range(2):
                    for y in range(2):
                        at = ((s * 2 + (place[CORE] ^ c)) * 2 + (place[ROW] ^ y)) * piece
                        rows = pl.ds(pl.multiple_of(at, piece), piece)
                        first, second = (j, y) if s == 0 else (y, j)
                        for k in range(3):
                            out_ref[s, first, second, k] = acc[j, k, rows].astype(bf16)
        sums = [jnp.sum(gain_acc[i], axis=1, keepdims=True) for i in range(2)]
        lane = lax.broadcasted_iota(jnp.int32, (wide, 128), 1)
        gain_ref[...] = jnp.where(lane == 0, sums[0], sums[1]).T[:4]


def lane_sum(values):
    chunks = [values[:, at : at + 128] for at in range(0, values.shape[1], 128)]
    return functools.reduce(jnp.add, chunks)


def finish_kernel(place, *refs):
    ffn_parts = [[refs[(layer * 2 + s) * 3 : (layer * 2 + s) * 3 + 3] for s in range(2)] for layer in range(2)]
    qkv_parts = refs[12:15]
    qkv_ref, out_ref, inner_ref, outer_ref, gain_ref = refs[15:]

    def pieces(parts):
        mine, row, core = parts
        yield 0, 0, mine[...]
        yield 0, 1, row[...]
        yield 1, 0, core[0]
        yield 1, 1, core[1]

    half = out_ref.shape[1]
    wide = out_ref.shape[2]
    piece = half // 8
    for layer in range(2):
        for s in range(2):
            for c, y, value in pieces(ffn_parts[layer][s]):
                value = value.astype(f32)
                at = ((place[CORE] ^ c) * 2 + (place[ROW] ^ y)) * piece
                rows = pl.ds(pl.multiple_of(at, piece), piece)
                low = pl.ds(pl.multiple_of(s * half // 2 + at, piece), piece)
                high = pl.ds(pl.multiple_of(half + s * half // 2 + at, piece), piece)
                out_ref[layer, low, :] = value[0]
                inner_ref[layer, rows, s * wide : (s + 1) * wide] = value[1]
                outer_ref[layer, low, :] = value[2][:, :half]
                outer_ref[layer, high, :] = value[2][:, half:]
    piece = qkv_ref.shape[2] // 4
    for c, y, value in pieces(qkv_parts):
        at = ((place[CORE] ^ c) * 2 + (place[ROW] ^ y)) * piece
        rows = pl.ds(pl.multiple_of(at, piece), piece)
        for layer in range(2):
            for s in range(3):
                index = (layer * 3 + s) * piece
                qkv_ref[layer, s, rows, :] = value[index : index + piece].astype(f32)
        if c == 0 and y == 0:
            gains = value[6 * piece : 6 * piece + 16].astype(f32)
            for layer in range(2):
                for i in range(2):
                    at = layer * 4 + i
                    gain_ref[layer, i : i + 1, :half] = gains[at : at + 1]
                    gain_ref[layer, i : i + 1, half:] = gains[8 + at : 9 + at]


def whole(shape):
    return pl.BlockSpec(shape, lambda r, place: (0,) * len(shape))


def per_row(shape):
    rest = (0,) * (len(shape) - 1)
    return pl.BlockSpec((1,) + tuple(shape[1:]), lambda r, place: (r,) + rest)


def struct(shape, dtype):
    return jax.ShapeDtypeStruct(shape, dtype)


def call(kernel, rows, place, operands, in_specs, outs, out_specs, scratch, name, us, aliases=None):
    return pl.pallas_call(
        kernel,
        out_shape=outs,
        grid_spec=pltpu.PrefetchScalarGridSpec(
            num_scalar_prefetch=1,
            grid=(rows,),
            in_specs=in_specs,
            out_specs=out_specs,
            scratch_shapes=scratch,
        ),
        compiler_params=pltpu.CompilerParams(vmem_limit_bytes=60 * 2**20),
        cost_estimate=pl.CostEstimate(
            flops=int(us * 1.1e9), bytes_accessed=int(us * 1e6), transcendentals=0
        ),
        input_output_aliases=aliases or {},
        name=name,
    )(place, *operands)


def attend(x_tok, w, w_layer, segments, place, rows, j, from_input):
    row_total, seq_len = segments.shape
    width, channels = w.shape[-2:]
    heads = width // HEAD_DIM
    groups = channels // width
    tiles = seq_len // QUERY_TILE
    window = QUERY_TILE + REACH
    outs = [
        struct((rows, channels, seq_len), bf16),
        struct((rows, channels, seq_len), bf16),
        struct((rows, channels, seq_len), bf16),
        struct((rows, groups, seq_len, width), bf16),
        struct((rows, groups, tiles, window, heads * QUERY_TILE), bf16),
        struct((rows, channels, seq_len), bf16),
    ]
    if from_input:
        x_spec = pl.BlockSpec((seq_len, channels), lambda r, place: (place[OFFSET] + r, place[j]))
    else:
        x_spec = pl.BlockSpec((seq_len, channels), lambda r, place: (r, place[j]))
    return call(
        attend_kernel,
        rows,
        place,
        (x_tok, w, segments),
        [x_spec, layer_block(w.shape, w_layer), whole(segments.shape)],
        outs,
        [per_row(o.shape) for o in outs],
        [],
        "attend",
        4.7 * rows,
    )


def layer_block(shape, layer):
    rest = (0,) * (len(shape) - 1)
    return pl.BlockSpec((None,) + tuple(shape[1:]), lambda r, place: (layer,) + rest)


def attend_back(d_context, saved, w, w_layer, d_before, place, rows, j, extra):
    xt, qt, kt, values, probs, ct = saved
    channels, seq_len = xt.shape[1:]
    window = QUERY_TILE + REACH
    width = w.shape[-2]
    heads = width // HEAD_DIM
    operands = (d_context, ct, probs, qt, kt, values, xt)
    in_specs = [per_row(o.shape) for o in operands] + [
        layer_block(w.shape, w_layer),
        pl.BlockSpec((1, 1, channels, seq_len), lambda r, place: (r, place[j], 0, 0)),
    ]
    operands += (w, d_before)
    scratch = [pltpu.VMEM((window, heads * QUERY_TILE), bf16)]
    aliases = {}
    if extra is None:
        dx = struct((rows, channels, seq_len), f32)
        outs = [dx, struct(w.shape[1:], f32)]
        out_specs = [per_row(dx.shape), whole(w.shape[1:])]
    else:
        later, gain0, gain1, full = extra
        operands += (later, gain0, gain1)
        in_specs += [whole(o.shape) for o in (later, gain0, gain1)]
        if full is not None:
            aliases = {len(operands) + 1: 1}
            operands += (full,)
            in_specs.append(pl.BlockSpec(memory_space=pl.ANY))
        piece = struct((2, 6 * (width // 4) + 16, channels), bf16)
        outs = [
            struct((rows * seq_len, channels), bf16),
            struct((2 * rows * seq_len, 2 * channels), bf16),
            piece,
            piece,
        ]
        out_specs = [
            pl.BlockSpec((seq_len, channels), lambda r, place: (r, 0)),
            pl.BlockSpec((seq_len, channels), lambda r, place: (place[OFFSET] + r, place[j])),
            whole(piece.shape),
            whole(piece.shape),
        ]
        scratch = [pltpu.VMEM(w.shape[1:], f32)] + scratch
    return call(
        functools.partial(attend_back_kernel, extra is not None, bool(aliases)),
        rows,
        place,
        operands,
        in_specs,
        outs,
        out_specs,
        scratch,
        "attend_back",
        6.5 * rows,
        aliases,
    )


def ffn(x_parts, contexts, weights, gains, place, rows, layer, more):
    half, seq_len = contexts[0].shape[1:]
    stream = (rows, 2, half, seq_len)
    acts = (rows, 2, 2, 2 * half, seq_len)
    tok = (rows * seq_len, 2 * half)
    outs = [
        struct(stream, f32),
        struct((rows, 1, seq_len), f32),
        struct(acts, bf16),
        struct(acts, bf16),
        struct(stream, f32),
        struct((rows, 1, seq_len), f32),
        struct(tok, bf16),
    ]
    out_specs = [per_row(o.shape) for o in outs]
    out_specs[-1] = pl.BlockSpec((seq_len, 2 * half), lambda r, place: (r, 0))
    if more:
        outs.append(struct(stream, f32))
        out_specs.append(per_row(stream))
    else:
        outs.append(struct((2 * rows * seq_len, 2 * half), bf16))
        out_specs.append(
            pl.BlockSpec((seq_len, 2 * half), lambda r, place: (place[OFFSET] + r, 0))
        )
    return call(
        functools.partial(ffn_kernel, layer, more),
        rows,
        place,
        tuple(x_parts) + tuple(contexts) + tuple(weights) + (gains,),
        [per_row(o.shape) for o in x_parts]
        + [per_row(o.shape) for o in contexts]
        + [whole(o.shape) for o in weights]
        + [whole(gains.shape)],
        outs,
        out_specs,
        [
            pltpu.VMEM((2, half, seq_len), f32),
            pltpu.VMEM((2, half, seq_len), bf16),
            pltpu.VMEM(weights[0].shape, bf16),
            pltpu.VMEM((2, 2 * half, 128), f32),
        ],
        "ffn",
        10 * rows,
    )


def ffn_back(g_parts, saved, contexts, weights, gains, place, rows, layer, more):
    half, seq_len = contexts[0].shape[1:]
    if more:
        g_specs = [per_row(o.shape) for o in g_parts]
    else:
        g_specs = [pl.BlockSpec((seq_len, 2 * half), lambda r, place: (place[OFFSET] + r, 0))]
    piece = struct((2, 2, 2, 3, half // 8, 2 * half), bf16)
    outs = [
        struct((rows, 2, half, seq_len), f32),
        struct(contexts[0].shape, bf16),
        struct(contexts[0].shape, bf16),
        piece,
        piece,
        struct((4, 2 * half), f32),
    ]
    out_specs = [per_row(o.shape) for o in outs[:3]] + [whole(o.shape) for o in outs[3:]]
    operands = tuple(saved) + tuple(contexts)
    return call(
        functools.partial(ffn_back_kernel, layer, more),
        rows,
        place,
        tuple(g_parts) + operands + tuple(weights) + (gains,),
        g_specs
        + [per_row(o.shape) for o in operands]
        + [whole(o.shape) for o in weights]
        + [whole(gains.shape)],
        outs,
        out_specs,
        [
            pltpu.VMEM((2, half, seq_len), f32),
            pltpu.VMEM((2, half, seq_len), bf16),
            pltpu.VMEM((2, half, seq_len), bf16),
            pltpu.VMEM(weights[0].shape, bf16),
            pltpu.VMEM((2, 2 * half, 128), f32),
            pltpu.VMEM((2, 3, half, 2 * half), f32),
            pltpu.VMEM((2, 2 * half, 128), f32),
        ],
        "ffn_back",
        11.5 * rows,
    )


def finish(ffn_parts, qkv_parts, place, width):
    operands = []
    for layer in ffn_parts:
        for parts in layer:
            operands += parts
    operands += qkv_parts
    half = qkv_parts[0].shape[-1]
    layers = len(ffn_parts)
    outs = [
        struct((layers, 3, width, half), f32),
        struct((layers, half, 2 * half), f32),
        struct((layers, width, 4 * half), f32),
        struct((layers, 2 * half, half), f32),
        struct((layers, 2, 2 * half), f32),
    ]
    return call(
        finish_kernel,
        1,
        place,
        operands,
        [whole(o.shape) for o in operands],
        outs,
        [whole(o.shape) for o in outs],
        [],
        "finish",
        6,
    )


def swap(values):
    return lax.ppermute(values, "head", [(0, 1), (1, 0)])


def trade(values, stride):
    count = lax.axis_size("dp")
    return lax.ppermute(values, "dp", [(a, a ^ stride) for a in range(count)])


def add(left, right):
    return (left.astype(f32) + right.astype(f32)).astype(bf16)


def far_strides():
    count = lax.axis_size("dp")
    strides = []
    stride = 4
    while stride < count:
        strides.append(stride)
        stride *= 2
    return strides


def pack_weights(out_w, inner_w, outer_w):
    half = out_w.shape[0]
    wide = out_w.shape[1]
    inner = jnp.stack([inner_w[:, :wide], inner_w[:, wide:]])
    out = out_w.reshape(2, half // 2, wide)
    outer = jnp.concatenate([outer_w[:half], outer_w[half:]], axis=1).reshape(2, half // 2, wide)
    return jnp.stack([out, inner, outer], axis=1)


def spread_out(total):
    row = trade(total, 2)
    return [total, row, trade(jnp.stack([total, row]), 1)]


def shards(
    tokens, segments, qkv_weight, out_weight, inner_weight, outer_weight, norm_gains, cotangent
):
    side = lax.axis_index("head").astype(jnp.int32)
    spot = lax.axis_index("dp").astype(jnp.int32)
    layers = qkv_weight.shape[0]
    row_total, seq_len = segments.shape
    rows = row_total // 2
    width = qkv_weight.shape[2]
    place = jnp.stack([side, 1 - side, side * rows, spot & 1, (spot >> 1) & 1])
    core = place[CORE]

    far_qkv = [swap(qkv_weight[i]) for i in range(layers)]
    ffn_weights = []
    for i in range(layers):
        near = pack_weights(out_weight[i], inner_weight[i], outer_weight[i])
        crossed = swap(lax.dynamic_index_in_dim(near, core, 0, False))
        ffn_weights.append((near, crossed, trade(crossed, 1)))
    x_tok = tokens
    x_stream = None
    saved_attend = []
    saved_ffn = []
    contexts = []
    for i in range(layers):
        held = [
            attend(x_tok, qkv_weight, i, segments, place, rows, 0, i == 0),
            attend(x_tok, far_qkv[i][None], 0, segments, place, rows, 1, i == 0),
        ]
        saved_attend.append(held)
        contexts.append([h[5] for h in held])
        x_parts = [h[0] for h in held] if i == 0 else [x_stream]
        results = ffn(
            x_parts, contexts[i], ffn_weights[i], norm_gains, place, rows, i, i < layers - 1
        )
        n1, r1, act, slope, n2, r2, x_tok, x_stream = results
        saved_ffn.append((n2, r2, act, slope, n1, r1))
    other_rows = (1 - side) * rows * seq_len
    activations = lax.dynamic_update_slice(x_stream, swap(x_tok), (other_rows, jnp.int32(0)))

    d_before, dc0, dc1, keep, send, gain1 = ffn_back(
        [cotangent], saved_ffn[1], contexts[1], ffn_weights[1], norm_gains, place, rows, 1, False
    )
    late = reduce_parts(keep, send)
    dx1, later1 = attend_back(
        dc1, saved_attend[1][1], far_qkv[1][None], 0, d_before, place, rows, 1, None
    )
    dx0, later0 = attend_back(
        dc0, saved_attend[1][0], qkv_weight, 1, d_before, place, rows, 0, None
    )
    d_before, dc0, dc1, keep, send, gain0 = ffn_back(
        [dx0, dx1], saved_ffn[0], contexts[0], ffn_weights[0], norm_gains, place, rows, 0, True
    )
    early = reduce_parts(keep, send)
    dx1, full, keep1, send1 = attend_back(
        dc1,
        saved_attend[0][1],
        far_qkv[0][None],
        0,
        d_before,
        place,
        rows,
        1,
        (later1, gain0, gain1, None),
    )
    crossed = swap(add(keep1, trade(send1, 1)))
    far_dx1 = swap(dx1)
    dx0, full, keep0, send0 = attend_back(
        dc0, saved_attend[0][0], qkv_weight, 0, d_before, place, rows, 0, (later0, gain0, gain1, full)
    )
    core_part = trade(send0, 1)
    far_dx0 = swap(dx0)
    total = add3(keep0[0], core_part[0], crossed[0])
    total = add(total, trade(add3(keep0[1], core_part[1], crossed[1]), 2))
    for stride in far_strides():
        total = add(total, trade(total, stride))
    qkv_parts = spread_out(total)
    half = qkv_weight.shape[-1]
    input_grad = lax.dynamic_update_slice(full, far_dx1, (other_rows, side * half))
    input_grad = lax.dynamic_update_slice(input_grad, far_dx0, (other_rows, (1 - side) * half))
    totals = finish([early, late], qkv_parts, place, width)
    return (activations, input_grad, *totals)


def add3(a, b, c):
    return (a.astype(f32) + b.astype(f32) + c.astype(f32)).astype(bf16)


def reduce_parts(keep, send):
    received = trade(send, 1)
    results = []
    for s in range(2):
        steps = [swap, lambda v: trade(v, 2)]
        strides = far_strides()
        if s == 1:
            steps = steps[::-1]
            strides = strides[::-1]
        mine, got = keep[s], received[s]
        crossed = steps[0](add(mine[1], got[1]))
        low = add3(mine[0, 0], got[0, 0], crossed[0])
        high = add3(mine[0, 1], got[0, 1], crossed[1])
        total = add(low, steps[1](high))
        for stride in strides:
            total = add(total, trade(total, stride))
        results.append(total)
    both = jnp.stack(results)
    row = trade(both, 2)
    core = trade(jnp.stack([both, row]), 1)
    return [[both[s], row[s], core[:, s]] for s in range(2)]


def solution(mesh):
    return jax.shard_map(
        shards,
        mesh=mesh,
        in_specs=(
            P("dp", None),
            P("dp", None),
            P(None, None, None, "head"),
            P(None, "head", None),
            P(None, None, "head"),
            P(None, None, "head"),
            P(),
            P("dp", None),
        ),
        out_specs=(
            P("dp", None),
            P("dp", None),
            P(None, None, None, "head"),
            P(None, "head", None),
            P(None, None, "head"),
            P(None, None, "head"),
            P(),
        ),
        check_vma=False,
    )
```

```python
import functools
import jax
import jax.numpy as jnp
from jax import lax
from jax.experimental import pallas as pl
from jax.experimental.pallas import tpu as pltpu
from jax.sharding import PartitionSpec as P

HEAD_DIM = 64
QUERY_TILE = 256
REACH = 128

SELF, OTHER, OFFSET, CORE, ROW = range(5)

epsilon = 1e-12
masked_score = -1e30
f32 = jnp.float32
bf16 = jnp.bfloat16

NN = (((1,), (0,)), ((), ()))
NT = (((1,), (1,)), ((), ()))
TN = (((0,), (0,)), ((), ()))


def mm(left, right, dims):
    return lax.dot_general(left, right, dims, preferred_element_type=f32)


def key_start(tile, seq_len):
    return min(max(tile * QUERY_TILE - REACH, 0), seq_len - QUERY_TILE - REACH)


def live_keys(tile, piece, seq_len):
    window = QUERY_TILE + REACH
    first_query = tile * QUERY_TILE + piece * REACH
    start = key_start(tile, seq_len)
    low = max(first_query - REACH - start, 0)
    high = min(first_query + 2 * REACH - start, window)
    return low, high


def block_diagonal(parts):
    rows = []
    for index, part in enumerate(parts):
        empty = jnp.zeros_like(part)
        rows.append(
            jnp.concatenate([part if at == index else empty for at in range(len(parts))], axis=1)
        )
    return jnp.concatenate(rows, axis=0)


def fill_rows(middle, low, high, total):
    pieces = []
    if low > 0:
        pieces.append(jnp.zeros((low, middle.shape[1]), middle.dtype))
    pieces.append(middle)
    if high < total:
        pieces.append(jnp.zeros((total - high, middle.shape[1]), middle.dtype))
    return jnp.concatenate(pieces, axis=0) if len(pieces) > 1 else middle


def across(row):
    return jnp.broadcast_to(row, (128, row.shape[1])).T


def take_weights(place, far, refs):
    if not far:
        return (lambda s: refs[0][s]), refs[1:]
    crossed, traded, *refs = refs
    scr = refs.pop()

    @pl.when(pl.program_id(0) == 0)
    def _():
        scr[:, place[CORE]] = crossed[...]
        scr[:, 1 - place[CORE]] = traded[...]

    return (lambda s: scr[s].reshape(2 * scr.shape[2], scr.shape[3])), refs


def attend_kernel(far, place, x_ref, *refs):
    weight, refs = take_weights(place, far, refs)
    seg_ref, xt_ref, qt_ref, kt_ref, v_ref, p_ref, ct_ref = refs
    seq_len, channels = x_ref.shape
    width = v_ref.shape[-1]
    window = QUERY_TILE + REACH
    heads = width // HEAD_DIM
    tiles = seq_len // QUERY_TILE
    x = x_ref[...]
    xt = x.T
    xt_ref[0] = xt
    segq = seg_ref[pl.ds(place[OFFSET] + pl.program_id(0), 1), :].astype(f32)
    segk = across(segq)
    masks = {}
    for tile in range(tiles):
        start = key_start(tile, seq_len)
        for piece in range(QUERY_TILE // REACH):
            low, high = live_keys(tile, piece, seq_len)
            at = tile * QUERY_TILE + piece * REACH
            same = segk[start + low : start + high] == segq[:, at : at + REACH]
            masks[tile, piece] = jnp.where(same, 0.0, masked_score)
    for group in range(channels // width):
        span = slice(group * width, (group + 1) * width)
        xg = x[:, span]
        xtg = xt[span]
        wq, wk, wv = (weight(s)[:, span] for s in range(3))
        qt = mm(wq, xtg, TN).astype(bf16) * jnp.asarray(HEAD_DIM**-0.5, bf16)
        kt = mm(wk, xtg, TN).astype(bf16)
        vt = mm(wv, xtg, TN).astype(bf16)
        keys = mm(xg, wk, NN).astype(bf16)
        values = mm(xg, wv, NN).astype(bf16)
        qt_ref[0, span] = qt
        kt_ref[0, span] = kt * jnp.asarray(HEAD_DIM**-0.5, bf16)
        v_ref[0, group] = values
        for tile in range(tiles):
            start = key_start(tile, seq_len)
            asked = slice(tile * QUERY_TILE, (tile + 1) * QUERY_TILE)
            spread = block_diagonal(
                [qt[i * HEAD_DIM : (i + 1) * HEAD_DIM, asked] for i in range(heads)]
            )
            scores = mm(keys[start : start + window], spread, NN)
            for i in range(heads):
                probs = []
                for piece in range(QUERY_TILE // REACH):
                    low, high = live_keys(tile, piece, seq_len)
                    at = i * QUERY_TILE + piece * REACH
                    s = scores[low:high, at : at + REACH] + masks[tile, piece]
                    top = jnp.max(s, axis=0, keepdims=True)
                    e = jnp.exp(s - top)
                    total = jnp.sum(e, axis=0, keepdims=True)
                    p = (e * (1.0 / total)).astype(bf16)
                    probs.append(fill_rows(p, low, high, window))
                probs = jnp.concatenate(probs, axis=1)
                p_ref[0, group, tile, :, i * QUERY_TILE : (i + 1) * QUERY_TILE] = probs
                context = mm(
                    vt[i * HEAD_DIM : (i + 1) * HEAD_DIM, start : start + window], probs, NN
                )
                at = group * width + i * HEAD_DIM
                ct_ref[0, at : at + HEAD_DIM, asked] = context.astype(bf16)


def attend_back_kernel(
    last,
    aliased,
    far,
    place,
    dc_ref,
    ct_ref,
    p_ref,
    qt_ref,
    kt_ref,
    v_ref,
    xt_ref,
    dz_ref,
    *refs,
):
    weight, refs = take_weights(place, far, refs)
    if last:
        later_ref, gain0_ref, gain1_ref, *refs = refs
        if aliased:
            _, *refs = refs
        dx_ref, full_ref, keep_ref, send_ref, grad_ref, ds_ref = refs
    else:
        dx_ref, grad_ref, ds_ref = refs
    channels, seq_len = xt_ref.shape[1:]
    width = v_ref.shape[-1]
    window = QUERY_TILE + REACH
    heads = width // HEAD_DIM
    tiles = seq_len // QUERY_TILE
    step = pl.program_id(0)
    grads = [[], [], []]
    d_inputs = []
    for group in range(channels // width):
        span = slice(group * width, (group + 1) * width)
        dq_tiles = []
        dk_tiles = []
        dv_tiles = []
        for tile in range(tiles):
            start = key_start(tile, seq_len)
            asked = slice(tile * QUERY_TILE, (tile + 1) * QUERY_TILE)
            d_context = dc_ref[0, span, asked]
            context = ct_ref[0, span, asked]
            both = d_context.astype(f32) * context.astype(f32)
            spread_dc = block_diagonal(
                [d_context[i * HEAD_DIM : (i + 1) * HEAD_DIM] for i in range(heads)]
            )
            qt = qt_ref[0, span, asked]
            spread_q = block_diagonal(
                [qt[i * HEAD_DIM : (i + 1) * HEAD_DIM] for i in range(heads)]
            )
            d_probs = mm(v_ref[0, group, start : start + window], spread_dc, NN)
            dq_heads = []
            for i in range(heads):
                shared = jnp.sum(both[i * HEAD_DIM : (i + 1) * HEAD_DIM], axis=0, keepdims=True)
                for piece in range(QUERY_TILE // REACH):
                    low, high = live_keys(tile, piece, seq_len)
                    at = i * QUERY_TILE + piece * REACH
                    p = p_ref[0, group, tile, low:high, at : at + REACH].astype(f32)
                    dp = d_probs[low:high, at : at + REACH]
                    ds = (p * (dp - shared[:, piece * REACH : (piece + 1) * REACH])).astype(bf16)
                    ds_ref[:, at : at + REACH] = fill_rows(ds, low, high, window)
                rows = slice(group * width + i * HEAD_DIM, group * width + (i + 1) * HEAD_DIM)
                dq_heads.append(
                    mm(
                        kt_ref[0, rows, start : start + window],
                        ds_ref[:, i * QUERY_TILE : (i + 1) * QUERY_TILE],
                        NN,
                    )
                )
            dq_tiles.append(jnp.concatenate(dq_heads, axis=0))
            dk_tiles.append(mm(ds_ref[...], spread_q, NT))
            dv_tiles.append(mm(p_ref[0, group, tile], spread_dc, NT))
        dq = jnp.concatenate(dq_tiles, axis=1).astype(bf16)
        dk = join_windows(dk_tiles, seq_len).astype(bf16)
        dv = join_windows(dv_tiles, seq_len).astype(bf16)
        xtg = xt_ref[0, span]
        grads[0].append(mm(xtg, dq, NT))
        grads[1].append(mm(xtg, dk, NN))
        grads[2].append(mm(xtg, dv, NN))
        wq, wk, wv = (weight(s)[:, span] for s in range(3))
        d_inputs.append(
            dz_ref[0, 0, span] + mm(wq, dq, NN) + mm(wk, dk, NT) + mm(wv, dv, NT)
        )
    joined = [jnp.concatenate(parts, axis=1) for parts in grads]

    @pl.when(step == 0)
    def _():
        for s in range(3):
            grad_ref[s] = joined[s]

    @pl.when(step > 0)
    def _():
        for s in range(3):
            grad_ref[s] += joined[s]

    d_input = jnp.concatenate(d_inputs, axis=0)
    if not last:
        dx_ref[0] = d_input
        return
    tok = d_input.astype(bf16).T
    dx_ref[...] = tok
    full_ref[...] = tok

    @pl.when(step == pl.num_programs(0) - 1)
    def _():
        piece = width // 4
        gain_rows = jnp.concatenate([gain0_ref[...], gain1_ref[...]], axis=0).astype(bf16)
        gain_rows = jnp.concatenate([gain_rows[:, :channels], gain_rows[:, channels:]], axis=0)
        for c, out_ref in enumerate((keep_ref, send_ref)):
            for y in range(2):
                at = ((place[CORE] ^ c) * 2 + (place[ROW] ^ y)) * piece
                rows = pl.ds(pl.multiple_of(at, piece), piece)
                for layer, source in enumerate((grad_ref, later_ref)):
                    for s in range(3):
                        out_ref[y, pl.ds((layer * 3 + s) * piece, piece)] = source[
                            s, rows
                        ].astype(bf16)
                out_ref[y, pl.ds(6 * piece, 16)] = gain_rows


def join_windows(pieces, seq_len):
    window = QUERY_TILE + REACH
    rows = []
    for at in range(0, seq_len, REACH):
        held = []
        for tile, piece in enumerate(pieces):
            start = key_start(tile, seq_len)
            if start <= at < start + window:
                held.append(piece[at - start : at - start + REACH])
        rows.append(functools.reduce(jnp.add, held))
    return jnp.concatenate(rows, axis=0)


def feature_mean(values):
    return jnp.sum(values, axis=0, keepdims=True) * (1.0 / values.shape[0])


def normalize(before):
    centered = before - feature_mean(before)
    inverse = lax.rsqrt(feature_mean(centered * centered) + epsilon)
    return centered * inverse, inverse


def normalize_back(gradient, gains, normal, inverse):
    scaled = gradient * gains
    return inverse * (scaled - feature_mean(scaled) - normal * feature_mean(scaled * normal))


def gather_far(place, x_ref, c_ref, scr):
    scr[place[CORE]] = x_ref[...]
    scr[1 - place[CORE]] = c_ref[...]


def out_rows(pack):
    rows = pack[:, 0]
    return rows.reshape(2 * rows.shape[1], rows.shape[2])


def inner_rows(pack, group):
    return pack[group, 1]


def outer_rows(pack, group, width):
    rows = pack[:, 2]
    rows = rows.reshape(2 * rows.shape[1], rows.shape[2])
    half = rows.shape[1] // 2
    at = group * width
    return jnp.concatenate([rows[:, at : at + width], rows[:, half + at : half + at + width]], axis=0)


def spread_gains(gains_ref, layer, g_scr):
    for i in range(2):
        g_scr[i] = across(gains_ref[layer, i : i + 1, :])


def wide_gain(g_scr, i, seq_len):
    return jnp.concatenate([g_scr[i]] * (seq_len // 128), axis=1)


def ffn_kernel(layer, more, place, *refs):
    if layer == 0:
        xt0, xt1, *refs = refs
    else:
        x_ref, *refs = refs
    (ct0, ct1, near_ref, farx_ref, farc_ref, gains_ref, *refs) = refs
    (n1_ref, r1_ref, act_ref, slope_ref, n2_ref, r2_ref, tok_ref, next_ref, *refs) = refs
    z_scr, fb_scr, far_scr, g_scr = refs
    half, seq_len = z_scr.shape[1:]
    wide = 2 * half
    width = half // 2
    sides = (place[SELF], place[OTHER])

    @pl.when(pl.program_id(0) == 0)
    def _():
        gather_far(place, farx_ref, farc_ref, far_scr)
        spread_gains(gains_ref, layer, g_scr)

    packs = (near_ref, far_scr)
    attention = mm(out_rows(packs[0]), ct0[0], TN) + mm(out_rows(packs[1]), ct1[0], TN)
    z_scr[...] = attention.reshape(2, half, seq_len)
    if layer == 0:
        z_scr[sides[0]] += xt0[0].astype(f32)
        z_scr[sides[1]] += xt1[0].astype(f32)
        before = z_scr[...].reshape(wide, seq_len)
    else:
        before = (z_scr[...] + x_ref[0]).reshape(wide, seq_len)
    normal, inverse = normalize(before)
    first = normal * wide_gain(g_scr, 0, seq_len)
    n1_ref[0] = normal.reshape(2, half, seq_len)
    r1_ref[0] = inverse
    z_scr[...] = first.reshape(2, half, seq_len)
    fb_scr[...] = first.astype(bf16).reshape(2, half, seq_len)
    for j, pack in enumerate(packs):
        for group in range(half // width):
            span = slice(group * width, (group + 1) * width)
            pre = mm(inner_rows(pack, group), fb_scr[sides[j], span], TN)
            below = 0.5 + 0.5 * lax.erf(pre * 0.7071067811865476)
            act = (pre * below).astype(bf16)
            slope = below + pre * (jnp.exp(-0.5 * pre * pre) * 0.3989422804014327)
            act_ref[0, j, group] = act
            slope_ref[0, j, group] = slope.astype(bf16)
            z_scr[sides[j], span] += mm(outer_rows(pack, group, width), act, TN)
    normal, inverse = normalize(z_scr[...].reshape(wide, seq_len))
    n2_ref[0] = normal.reshape(2, half, seq_len)
    r2_ref[0] = inverse
    output = normal * wide_gain(g_scr, 1, seq_len)
    tok = output.astype(bf16).T
    tok_ref[...] = tok
    if more:
        next_ref[0] = output.reshape(2, half, seq_len)
    else:
        next_ref[...] = tok


def ffn_back_kernel(layer, more, place, *refs):
    if more:
        g0, g1, *refs = refs
    else:
        cot_ref, *refs = refs
    (n2_ref, r2_ref, act_ref, slope_ref, n1_ref, r1_ref, ct0, ct1, *refs) = refs
    (near_ref, farx_ref, farc_ref, gains_ref, *refs) = refs
    (dz1_ref, dc0, dc1, keep_ref, send_ref, gain_ref, *refs) = refs
    d_scr, b_scr, f_scr, far_scr, g_scr, acc, gain_acc = refs
    half, seq_len = d_scr.shape[1:]
    wide = 2 * half
    width = half // 2
    sides = (place[SELF], place[OTHER])
    step = pl.program_id(0)

    @pl.when(step == 0)
    def _():
        gather_far(place, farx_ref, farc_ref, far_scr)
        spread_gains(gains_ref, layer, g_scr)
        acc[...] = jnp.zeros_like(acc)
        gain_acc[...] = jnp.zeros_like(gain_acc)

    packs = (near_ref, far_scr)
    if more:
        d_scr[sides[0]] = g0[0]
        d_scr[sides[1]] = g1[0]
        g = d_scr[...].reshape(wide, seq_len)
    else:
        g = cot_ref[...].T.astype(f32)
    normal = n2_ref[0].reshape(wide, seq_len)
    gain_acc[1] += lane_sum(g * normal)
    d_second = normalize_back(g, wide_gain(g_scr, 1, seq_len), normal, r2_ref[0])
    d_scr[...] = d_second.reshape(2, half, seq_len)
    b_scr[...] = d_second.astype(bf16).reshape(2, half, seq_len)
    normal = n1_ref[0].reshape(wide, seq_len)
    gain1 = wide_gain(g_scr, 0, seq_len)
    f_scr[...] = (normal * gain1).astype(bf16).reshape(2, half, seq_len)
    for j, pack in enumerate(packs):
        outers = []
        for group in range(half // width):
            span = slice(group * width, (group + 1) * width)
            d_branch = b_scr[sides[j], span]
            first = f_scr[sides[j], span]
            outers.append(mm(act_ref[0, j, group], d_branch, NT))
            d_act = mm(outer_rows(pack, group, width), d_branch, NN)
            d_pre = (d_act * slope_ref[0, j, group].astype(f32)).astype(bf16)
            acc[j, 1, span] += mm(first, d_pre, NT)
            d_scr[sides[j], span] += mm(inner_rows(pack, group), d_pre, NN)
        acc[j, 2] += jnp.concatenate(
            [o[:half] for o in outers] + [o[half:] for o in outers], axis=1
        )
    d_first = d_scr[...].reshape(wide, seq_len)
    gain_acc[0] += lane_sum(d_first * normal)
    d_before = normalize_back(d_first, gain1, normal, r1_ref[0])
    dz1_ref[0] = d_before.reshape(2, half, seq_len)
    d_attention = d_before.astype(bf16)
    for j, (pack, ct, dc) in enumerate(zip(packs, (ct0, ct1), (dc0, dc1))):
        acc[j, 0] += mm(ct[0], d_attention, NT)
        dc[0] = mm(out_rows(pack), d_attention, NN).astype(bf16)

    @pl.when(step == pl.num_programs(0) - 1)
    def _():
        piece = half // 8
        for c, out_ref in enumerate((keep_ref, send_ref)):
            for s in range(2):
                for j in range(2):
                    for y in range(2):
                        at = ((s * 2 + (place[CORE] ^ c)) * 2 + (place[ROW] ^ y)) * piece
                        rows = pl.ds(pl.multiple_of(at, piece), piece)
                        first, second = (j, y) if s == 0 else (y, j)
                        for k in range(3):
                            out_ref[s, first, second, k] = acc[j, k, rows].astype(bf16)
        sums = [jnp.sum(gain_acc[i], axis=1, keepdims=True) for i in range(2)]
        lane = lax.broadcasted_iota(jnp.int32, (wide, 128), 1)
        gain_ref[...] = jnp.where(lane == 0, sums[0], sums[1]).T[:4]


def lane_sum(values):
    chunks = [values[:, at : at + 128] for at in range(0, values.shape[1], 128)]
    return functools.reduce(jnp.add, chunks)


def placed_pieces(place, parts, size):
    mine, row, core = parts
    for c, y, value in ((0, 0, mine[...]), (0, 1, row[...]), (1, 0, core[0]), (1, 1, core[1])):
        yield ((place[CORE] ^ c) * 2 + (place[ROW] ^ y)) * size, value


def rows_at(at, size):
    return pl.ds(pl.multiple_of(at, size), size)


def finish_ffn_kernel(place, *refs):
    out_ref, inner_ref, outer_ref = refs[-3:]
    half, wide = out_ref.shape[1:]
    size = half // 8
    for s in range(2):
        for at, value in placed_pieces(place, refs[3 * s : 3 * s + 3], size):
            value = value.astype(f32)
            low = s * (half // 2) + at
            out_ref[0, rows_at(low, size), :] = value[0]
            inner_ref[0, rows_at(at, size), s * wide : (s + 1) * wide] = value[1]
            outer_ref[0, rows_at(low, size), :] = value[2][:, :half]
            outer_ref[0, rows_at(half + low, size), :] = value[2][:, half:]


def finish_qkv_kernel(place, mine, row, core, qkv_ref, gain_ref):
    half = qkv_ref.shape[3]
    size = qkv_ref.shape[2] // 4
    for at, value in placed_pieces(place, (mine, row, core), size):
        for layer in range(2):
            for s in range(3):
                index = (layer * 3 + s) * size
                qkv_ref[layer, s, rows_at(at, size), :] = value[index : index + size].astype(f32)
    gains = mine[6 * size : 6 * size + 16].astype(f32)
    for layer in range(2):
        for i in range(2):
            at = layer * 4 + i
            gain_ref[layer, i : i + 1, :half] = gains[at : at + 1]
            gain_ref[layer, i : i + 1, half:] = gains[8 + at : 9 + at]


def pack_kernel(place, out_ref, inner_ref, outer_ref, qkv_ref, near_ref, piece_ref, part_ref):
    half, wide = out_ref.shape[1:]
    depth = half // 2
    for i in range(2):
        rows = slice(i * depth, (i + 1) * depth)
        near_ref[i, 0] = out_ref[0, rows]
        near_ref[i, 1] = inner_ref[0, :, i * wide : (i + 1) * wide]
        near_ref[i, 2, :, :half] = outer_ref[0, rows]
        near_ref[i, 2, :, half:] = outer_ref[0, half + i * depth : half + (i + 1) * depth]
    piece_ref[...] = near_ref[place[CORE]]
    size = qkv_ref.shape[2] // 2
    for s in range(3):
        part_ref[s] = qkv_ref[0, s, rows_at(place[CORE] * size, size), :]


def whole(shape):
    return pl.BlockSpec(shape, lambda r, place: (0,) * len(shape))


def per_row(shape):
    rest = (0,) * (len(shape) - 1)
    return pl.BlockSpec((1,) + tuple(shape[1:]), lambda r, place: (r,) + rest)


def struct(shape, dtype):
    return jax.ShapeDtypeStruct(shape, dtype)


def call(
    kernel, rows, place, operands, in_specs, outs, out_specs, scratch, name, us, aliases=None, after=()
):
    count = len(operands)
    in_specs = list(in_specs) + [pl.BlockSpec(memory_space=pl.ANY)] * len(after)
    operands = tuple(operands) + tuple(after)

    def body(place, *refs):
        kernel(place, *refs[:count], *refs[count + len(after) :])

    results = pl.pallas_call(
        body,
        out_shape=outs,
        grid_spec=pltpu.PrefetchScalarGridSpec(
            num_scalar_prefetch=1,
            grid=(rows,),
            in_specs=in_specs,
            out_specs=out_specs,
            scratch_shapes=scratch,
        ),
        compiler_params=pltpu.CompilerParams(vmem_limit_bytes=60 * 2**20),
        cost_estimate=pl.CostEstimate(
            flops=int(us * 5e9), bytes_accessed=int(us * 1e7), transcendentals=0
        ),
        input_output_aliases=aliases or {},
        name=name,
    )(place, *operands)
    return list(results)


def attend(x_tok, w, segments, place, rows, j, layer, after=()):
    row_total, seq_len = segments.shape
    far = j == 1
    channels = w[0].shape[-1]
    width = channels // 2
    heads = width // HEAD_DIM
    groups = channels // width
    tiles = seq_len // QUERY_TILE
    window = QUERY_TILE + REACH
    outs = [
        struct((rows, channels, seq_len), bf16),
        struct((rows, channels, seq_len), bf16),
        struct((rows, channels, seq_len), bf16),
        struct((rows, groups, seq_len, width), bf16),
        struct((rows, groups, tiles, window, heads * QUERY_TILE), bf16),
        struct((rows, channels, seq_len), bf16),
    ]
    if layer == 0:
        x_spec = pl.BlockSpec((seq_len, channels), lambda r, place: (place[OFFSET] + r, place[j]))
    else:
        x_spec = pl.BlockSpec((seq_len, channels), lambda r, place: (r, place[j]))
    return call(
        functools.partial(attend_kernel, far),
        rows,
        place,
        (x_tok, *w, segments),
        [x_spec, *weight_blocks(w, far, layer), whole(segments.shape)],
        outs,
        [per_row(o.shape) for o in outs],
        weight_scratch(w, far),
        "attend",
        0.2 if far and layer == 0 else 4.7 * rows,
        after=after,
    )


def weight_blocks(w, far, layer):
    return [whole(o.shape) for o in w] if far else [layer_block(w[0].shape, layer)]


def weight_scratch(w, far):
    if not far:
        return []
    three, depth, channels = w[0].shape
    return [pltpu.VMEM((three, 2, depth, channels), bf16)]


def layer_block(shape, layer):
    rest = (0,) * (len(shape) - 1)
    return pl.BlockSpec((None,) + tuple(shape[1:]), lambda r, place: (layer,) + rest)


def attend_back(d_context, saved, w, d_before, place, rows, j, layer, extra, after=()):
    xt, qt, kt, values, probs, ct = saved
    channels, seq_len = xt.shape[1:]
    window = QUERY_TILE + REACH
    width = values.shape[-1]
    far = j == 1
    heads = width // HEAD_DIM
    operands = (d_context, ct, probs, qt, kt, values, xt)
    in_specs = [per_row(o.shape) for o in operands] + [
        pl.BlockSpec((1, 1, channels, seq_len), lambda r, place: (r, place[j], 0, 0)),
        *weight_blocks(w, far, layer),
    ]
    operands += (d_before, *w)
    scratch = [pltpu.VMEM((window, heads * QUERY_TILE), bf16)] + weight_scratch(w, far)
    grad = (3, width, channels)
    aliases = {}
    if extra is None:
        dx = struct((rows, channels, seq_len), f32)
        outs = [dx, struct(grad, f32)]
        out_specs = [per_row(dx.shape), whole(grad)]
    else:
        later, gain0, gain1, full = extra
        operands += (later, gain0, gain1)
        in_specs += [whole(o.shape) for o in (later, gain0, gain1)]
        if full is not None:
            aliases = {len(operands) + 1: 1}
            operands += (full,)
            in_specs.append(pl.BlockSpec(memory_space=pl.ANY))
        piece = struct((2, 6 * (width // 4) + 16, channels), bf16)
        outs = [
            struct((rows * seq_len, channels), bf16),
            struct((2 * rows * seq_len, 2 * channels), bf16),
            piece,
            piece,
        ]
        out_specs = [
            pl.BlockSpec((seq_len, channels), lambda r, place: (r, 0)),
            pl.BlockSpec((seq_len, channels), lambda r, place: (place[OFFSET] + r, place[j])),
            whole(piece.shape),
            whole(piece.shape),
        ]
        scratch = [pltpu.VMEM(grad, f32)] + scratch
    return call(
        functools.partial(attend_back_kernel, extra is not None, bool(aliases), far),
        rows,
        place,
        operands,
        in_specs,
        outs,
        out_specs,
        scratch,
        "attend_back",
        6.5 * rows,
        aliases,
        after,
    )


def ffn(x_parts, contexts, weights, gains, place, rows, layer, more, after=()):
    half, seq_len = contexts[0].shape[1:]
    stream = (rows, 2, half, seq_len)
    acts = (rows, 2, 2, 2 * half, seq_len)
    tok = (rows * seq_len, 2 * half)
    outs = [
        struct(stream, f32),
        struct((rows, 1, seq_len), f32),
        struct(acts, bf16),
        struct(acts, bf16),
        struct(stream, f32),
        struct((rows, 1, seq_len), f32),
        struct(tok, bf16),
    ]
    out_specs = [per_row(o.shape) for o in outs]
    out_specs[-1] = pl.BlockSpec((seq_len, 2 * half), lambda r, place: (r, 0))
    if more:
        outs.append(struct(stream, f32))
        out_specs.append(per_row(stream))
    else:
        outs.append(struct((2 * rows * seq_len, 2 * half), bf16))
        out_specs.append(
            pl.BlockSpec((seq_len, 2 * half), lambda r, place: (place[OFFSET] + r, 0))
        )
    return call(
        functools.partial(ffn_kernel, layer, more),
        rows,
        place,
        tuple(x_parts) + tuple(contexts) + tuple(weights) + (gains,),
        [per_row(o.shape) for o in x_parts]
        + [per_row(o.shape) for o in contexts]
        + [whole(o.shape) for o in weights]
        + [whole(gains.shape)],
        outs,
        out_specs,
        [
            pltpu.VMEM((2, half, seq_len), f32),
            pltpu.VMEM((2, half, seq_len), bf16),
            pltpu.VMEM(weights[0].shape, bf16),
            pltpu.VMEM((2, 2 * half, 128), f32),
        ],
        "ffn",
        10 * rows,
        after=after,
    )


def ffn_back(g_parts, saved, contexts, weights, gains, place, rows, layer, more, after=()):
    half, seq_len = contexts[0].shape[1:]
    if more:
        g_specs = [per_row(o.shape) for o in g_parts]
    else:
        g_specs = [pl.BlockSpec((seq_len, 2 * half), lambda r, place: (place[OFFSET] + r, 0))]
    piece = struct((2, 2, 2, 3, half // 8, 2 * half), bf16)
    outs = [
        struct((rows, 2, half, seq_len), f32),
        struct(contexts[0].shape, bf16),
        struct(contexts[0].shape, bf16),
        piece,
        piece,
        struct((4, 2 * half), f32),
    ]
    out_specs = [per_row(o.shape) for o in outs[:3]] + [whole(o.shape) for o in outs[3:]]
    operands = tuple(saved) + tuple(contexts)
    return call(
        functools.partial(ffn_back_kernel, layer, more),
        rows,
        place,
        tuple(g_parts) + operands + tuple(weights) + (gains,),
        g_specs
        + [per_row(o.shape) for o in operands]
        + [whole(o.shape) for o in weights]
        + [whole(gains.shape)],
        outs,
        out_specs,
        [
            pltpu.VMEM((2, half, seq_len), f32),
            pltpu.VMEM((2, half, seq_len), bf16),
            pltpu.VMEM((2, half, seq_len), bf16),
            pltpu.VMEM(weights[0].shape, bf16),
            pltpu.VMEM((2, 2 * half, 128), f32),
            pltpu.VMEM((2, 3, half, 2 * half), f32),
            pltpu.VMEM((2, 2 * half, 128), f32),
        ],
        "ffn_back",
        11.5 * rows,
        after=after,
    )


def one_layer(shape, layer):
    rest = (0,) * (len(shape) - 1)
    return pl.BlockSpec((1,) + tuple(shape[1:]), lambda r, place: (layer,) + rest)


def finish_ffn(parts, place, layer, layers, held=()):
    operands = [p for part in parts for p in part]
    half = operands[0].shape[-1] // 2
    outs = [
        struct((layers, half, 2 * half), f32),
        struct((layers, half // 2, 4 * half), f32),
        struct((layers, 2 * half, half), f32),
    ]
    return call(
        finish_ffn_kernel,
        1,
        place,
        operands + list(held),
        [whole(o.shape) for o in operands] + [pl.BlockSpec(memory_space=pl.ANY)] * len(held),
        outs,
        [one_layer(o.shape, layer) for o in outs],
        [],
        "finish_ffn",
        3,
        {7 + i: i for i in range(len(held))},
    )


def finish_qkv(parts, place, layers, width):
    half = parts[0].shape[-1]
    outs = [struct((layers, 3, width, half), f32), struct((layers, 2, 2 * half), f32)]
    return call(
        finish_qkv_kernel,
        1,
        place,
        parts,
        [whole(o.shape) for o in parts],
        outs,
        [whole(o.shape) for o in outs],
        [],
        "finish_qkv",
        3,
    )


def pack(weights, place, layer, after=()):
    out_w, inner_w, outer_w, qkv_w = weights
    half, wide = out_w.shape[1:]
    three, depth, channels = qkv_w.shape[1:]
    outs = [
        struct((2, 3, half // 2, wide), bf16),
        struct((3, half // 2, wide), bf16),
        struct((three, depth // 2, channels), bf16),
    ]
    return call(
        pack_kernel,
        1,
        place,
        weights,
        [one_layer(o.shape, layer) for o in weights],
        outs,
        [whole(o.shape) for o in outs],
        [],
        "pack",
        3,
        after=after,
    )


def hold(values, place, after):
    anywhere = pl.BlockSpec(memory_space=pl.ANY)
    return call(
        lambda place, *refs: None,
        1,
        place,
        values,
        [anywhere] * len(values),
        [struct(v.shape, v.dtype) for v in values],
        [anywhere] * len(values),
        [],
        "hold",
        1,
        {i + 1: i for i in range(len(values))},
        after,
    )


def fill_input_kernel(place, full_ref, own_ref, far_ref, out_ref):
    column = pl.program_id(1)

    @pl.when(column == 0)
    def _():
        out_ref[...] = own_ref[...]

    @pl.when(column == 1)
    def _():
        out_ref[...] = far_ref[...]


def fill_input(full, from_own, from_far, place, rows, seq_len):
    half = from_own.shape[1]
    block = pl.BlockSpec((seq_len, half), lambda r, j, place: (r, 0))
    return pl.pallas_call(
        fill_input_kernel,
        out_shape=struct(full.shape, full.dtype),
        grid_spec=pltpu.PrefetchScalarGridSpec(
            num_scalar_prefetch=1,
            grid=(rows, 2),
            in_specs=[pl.BlockSpec(memory_space=pl.ANY), block, block],
            out_specs=pl.BlockSpec(
                (seq_len, half),
                lambda r, j, place: (rows - place[OFFSET] + r, (1 - place[SELF]) ^ j),
            ),
        ),
        input_output_aliases={1: 0},
        name="fill_input",
    )(place, full, from_own, from_far)


def swap(values):
    return lax.ppermute(values, "head", [(0, 1), (1, 0)])


def trade(values, stride):
    count = lax.axis_size("dp")
    return lax.ppermute(values, "dp", [(a, a ^ stride) for a in range(count)])


def far_strides():
    count = lax.axis_size("dp")
    strides = []
    stride = 4
    while stride < count:
        strides.append(stride)
        stride *= 2
    return strides


def sums(groups, place, after=(), casts=None):
    operands = []
    plan = []
    for group in groups:
        terms = []
        for term in group:
            value, *index = term if isinstance(term, tuple) else (term,)
            terms.append((len(operands), tuple(index)))
            operands.append(value)
        plan.append(terms)
    outs = [
        struct(operands[terms[0][0]].shape[len(terms[0][1]) :], operands[terms[0][0]].dtype)
        for terms in plan
    ]

    def kernel(place, *refs):
        for terms, out in zip(plan, refs[len(operands) :]):
            out[...] = functools.reduce(
                jnp.add, [refs[at][...].astype(f32) for at, _ in terms]
            ).astype(out.dtype)

    def spec(value, index):
        shape = value.shape[len(index) :]
        return pl.BlockSpec(
            (None,) * len(index) + tuple(shape),
            lambda r, place: tuple(index) + (0,) * len(shape),
        )

    return call(
        kernel,
        1,
        place,
        operands,
        [spec(operands[at], index) for terms in plan for at, index in terms],
        outs,
        [whole(o.shape) for o in outs],
        [],
        "sums",
        2,
        after=after,
    )


def first_sums(keep, got):
    return [[(keep, s, 1), (got, s, 1)] for s in range(2)]


def second_sums(keep, got, crossed):
    return [
        [(keep, s, 0, second), (got, s, 0, second), (crossed[s], second)]
        for second in (1, 0)
        for s in range(2)
    ]


def shards(
    tokens, segments, qkv_weight, out_weight, inner_weight, outer_weight, norm_gains, cotangent
):
    side = lax.axis_index("head").astype(jnp.int32)
    spot = lax.axis_index("dp").astype(jnp.int32)
    layers = qkv_weight.shape[0]
    row_total, seq_len = segments.shape
    rows = row_total // 2
    width = qkv_weight.shape[2]
    place = jnp.stack([side, 1 - side, side * rows, spot & 1, (spot >> 1) & 1])
    far_qkv = [None, None]
    ffn_weights = [None, None]

    def fetch(i, after=()):
        weights = (out_weight, inner_weight, outer_weight, qkv_weight)
        near, piece, part = pack(weights, place, i, after)
        return near, swap(part), swap(piece)

    packed, part, piece = fetch(0)
    near = attend(tokens, (qkv_weight,), segments, place, rows, 0, 0)
    (part,) = hold([part], place, [near[5]])
    far_qkv[0] = (part, trade(part, 1))
    ffn_weights[0] = (packed, piece, trade(piece, 1))
    far = attend(tokens, far_qkv[0], segments, place, rows, 1, 0, [near[5]])
    held = [near, far]
    packed, part, piece = fetch(1, [far[5], ffn_weights[0][1]])
    ffn_weights[1] = (packed, piece, trade(piece, 1))
    saved_attend = [held]
    contexts = [[h[5] for h in held]]
    n1, r1, act, slope, n2, r2, x_tok, x_stream = ffn(
        [h[0] for h in held], contexts[0], ffn_weights[0], norm_gains, place, rows, 0, True
    )
    (part,) = hold([part], place, [x_tok])
    far_qkv[1] = (part, trade(part, 1))
    saved_ffn = [(n2, r2, act, slope, n1, r1)]
    held = [
        attend(x_tok, (qkv_weight,), segments, place, rows, 0, 1),
        attend(x_tok, far_qkv[1], segments, place, rows, 1, 1),
    ]
    saved_attend.append(held)
    contexts.append([h[5] for h in held])
    n1, r1, act, slope, n2, r2, x_tok, x_full = ffn(
        [x_stream], contexts[1], ffn_weights[1], norm_gains, place, rows, 1, False
    )
    saved_ffn.append((n2, r2, act, slope, n1, r1))
    part = x_tok.shape[0] // 2
    far_tok = [swap(x_tok[:part])]
    d_before, dc0, dc1, keep, send, gain1 = ffn_back(
        [cotangent], saved_ffn[1], contexts[1], ffn_weights[1], norm_gains, place, rows, 1, False
    )

    strides = far_strides()
    orders = (strides, strides[::-1])
    got = trade(send, 1)
    dx1, later1 = attend_back(
        dc1, saved_attend[1][1], far_qkv[1], d_before, place, rows, 1, 1, None, [far_tok[0]]
    )
    late = sums(first_sums(keep, got), place, [dx1])
    crossed = [swap(late[0]), trade(late[1], 2)]
    dx0, later0 = attend_back(
        dc0, saved_attend[1][0], (qkv_weight,), d_before, place, rows, 0, 1, None, late
    )
    late = sums(second_sums(keep, got, crossed), place, [dx0])
    crossed = [trade(late[0], 2), swap(late[1])]
    far_tok.append(swap(x_tok[part:]))
    d_before, dc0, dc1, keep, send, gain0 = ffn_back(
        [dx0, dx1],
        saved_ffn[0],
        contexts[0],
        ffn_weights[0],
        norm_gains,
        place,
        rows,
        0,
        True,
        late,
    )
    late = sums([[late[2 + s], crossed[s]] for s in range(2)], place, [d_before])
    crossed = [trade(late[s], orders[s][0]) for s in range(2)]
    got = trade(send, 1)
    dx1, full, keep1, send1 = attend_back(
        dc1,
        saved_attend[0][1],
        far_qkv[0],
        d_before,
        place,
        rows,
        1,
        0,
        (later1, gain0, gain1, None),
        late + [far_tok[1]],
    )
    far_dx1 = swap(dx1)
    early = sums(
        first_sums(keep, got) + [[late[s], crossed[s]] for s in range(2)], place, [dx1]
    )
    early, late = early[:2], early[2:]
    crossed = [swap(early[0]), trade(early[1], 2)]
    received = [trade(late[s], orders[s][1]) for s in range(2)]
    far_part = sums([[keep1, trade(send1, 1)]], place, early)
    far_part = swap(far_part[0])
    dx0, full, keep0, send0 = attend_back(
        dc0,
        saved_attend[0][0],
        (qkv_weight,),
        d_before,
        place,
        rows,
        0,
        0,
        (later0, gain0, gain1, full),
        early,
    )
    core_part = trade(send0, 1)
    far_dx0 = swap(dx0)
    results = sums(
        second_sums(keep, got, crossed) + [[late[s], received[s]] for s in range(2)],
        place,
        [dx0],
    )
    early, late = results[:4], results[4:]
    for at in range(2, len(strides)):
        late = sums([[late[s], trade(late[s], orders[s][at])] for s in range(2)], place)
    crossed = [trade(early[0], 2), swap(early[1])]
    late_row = [trade(v, 2) for v in late]
    total = sums(
        [[(keep0, y), (core_part, y), (far_part, y)] for y in (1, 0)], place, early[:1]
    )
    row = trade(total[0], 2)
    early = sums([[early[2 + s], crossed[s]] for s in range(2)], place, [total[0]])
    late_core = [trade(jnp.stack([a, b]), 1) for a, b in zip(late, late_row)]
    total = sums([[total[1], row]], place, early)
    for at in range(len(strides)):
        crossed = [trade(early[s], orders[s][at]) for s in range(2)]
        row = trade(total[0], strides[at])
        early = sums([[early[s], crossed[s]] for s in range(2)], place, total)
        total = sums([[total[0], row]], place, early)
    early_row = [trade(v, 2) for v in early]
    row = trade(total[0], 2)
    grads = finish_ffn(
        [[late[s], late_row[s], late_core[s]] for s in range(2)], place, 1, layers
    )
    early_core = [trade(jnp.stack([a, b]), 1) for a, b in zip(early, early_row)]
    core_part = trade(jnp.stack([total[0], row]), 1)
    input_grad = fill_input(full, far_dx0, far_dx1, place, rows, seq_len)
    other_rows = (1 - side) * rows * seq_len
    activations = x_full
    for at in range(2):
        activations = lax.dynamic_update_slice(
            activations, far_tok[at], (other_rows + at * part, jnp.int32(0))
        )
    qkv_grad, gain_grad = finish_qkv([total[0], row, core_part], place, layers, width)
    out_grad, inner_grad, outer_grad = finish_ffn(
        [[early[s], early_row[s], early_core[s]] for s in range(2)], place, 0, layers, grads
    )
    return (activations, input_grad, qkv_grad, out_grad, inner_grad, outer_grad, gain_grad)


def solution(mesh):
    return jax.shard_map(
        shards,
        mesh=mesh,
        in_specs=(
            P("dp", None),
            P("dp", None),
            P(None, None, None, "head"),
            P(None, "head", None),
            P(None, None, "head"),
            P(None, None, "head"),
            P(),
            P("dp", None),
        ),
        out_specs=(
            P("dp", None),
            P("dp", None),
            P(None, None, None, "head"),
            P(None, "head", None),
            P(None, None, "head"),
            P(None, None, "head"),
            P(),
        ),
        check_vma=False,
    )
```

```python
import functools
import jax
import jax.numpy as jnp
from jax import lax
from jax.experimental import pallas as pl
from jax.experimental.pallas import tpu as pltpu
from jax.sharding import PartitionSpec as P

HEAD_DIM = 64
QUERY_TILE = 256
REACH = 128

SELF, OTHER, OFFSET, CORE, ROW = range(5)

epsilon = 1e-12
masked_score = -1e30
f32 = jnp.float32
bf16 = jnp.bfloat16

NN = (((1,), (0,)), ((), ()))
NT = (((1,), (1,)), ((), ()))
TN = (((0,), (0,)), ((), ()))


def mm(left, right, dims):
    return lax.dot_general(left, right, dims, preferred_element_type=f32)


def key_start(tile, seq_len):
    return min(max(tile * QUERY_TILE - REACH, 0), seq_len - QUERY_TILE - REACH)


def live_keys(tile, piece, seq_len):
    window = QUERY_TILE + REACH
    first_query = tile * QUERY_TILE + piece * REACH
    start = key_start(tile, seq_len)
    low = max(first_query - REACH - start, 0)
    high = min(first_query + 2 * REACH - start, window)
    return low, high


def block_diagonal(parts):
    rows = []
    for index, part in enumerate(parts):
        empty = jnp.zeros_like(part)
        rows.append(
            jnp.concatenate([part if at == index else empty for at in range(len(parts))], axis=1)
        )
    return jnp.concatenate(rows, axis=0)


def fill_rows(middle, low, high, total):
    pieces = []
    if low > 0:
        pieces.append(jnp.zeros((low, middle.shape[1]), middle.dtype))
    pieces.append(middle)
    if high < total:
        pieces.append(jnp.zeros((total - high, middle.shape[1]), middle.dtype))
    return jnp.concatenate(pieces, axis=0) if len(pieces) > 1 else middle


def across(row):
    return jnp.broadcast_to(row, (128, row.shape[1])).T


def take_weights(place, far, refs):
    if not far:
        return (lambda s: refs[0][s]), refs[1:]
    crossed, traded, *refs = refs
    scr = refs.pop()

    @pl.when(pl.program_id(0) == 0)
    def _():
        scr[:, place[CORE]] = crossed[...]
        scr[:, 1 - place[CORE]] = traded[...]

    return (lambda s: scr[s].reshape(2 * scr.shape[2], scr.shape[3])), refs


def attend_kernel(far, place, x_ref, *refs):
    weight, refs = take_weights(place, far, refs)
    seg_ref, *refs = refs
    xt_ref, qt_ref, kt_ref, v_ref, p_ref, ct_ref = refs[-6:]
    seq_len, channels = x_ref.shape
    width = v_ref.shape[-1]
    window = QUERY_TILE + REACH
    heads = width // HEAD_DIM
    tiles = seq_len // QUERY_TILE
    x = x_ref[...]
    xt = x.T
    xt_ref[0, 0] = xt
    segq = seg_ref[pl.ds(place[OFFSET] + pl.program_id(0), 1), :].astype(f32)
    segk = across(segq)
    masks = {}
    for tile in range(tiles):
        start = key_start(tile, seq_len)
        for piece in range(QUERY_TILE // REACH):
            low, high = live_keys(tile, piece, seq_len)
            at = tile * QUERY_TILE + piece * REACH
            same = segk[start + low : start + high] == segq[:, at : at + REACH]
            masks[tile, piece] = jnp.where(same, 0.0, masked_score)
    for group in range(channels // width):
        span = slice(group * width, (group + 1) * width)
        xg = x[:, span]
        xtg = xt[span]
        wq, wk, wv = (weight(s)[:, span] for s in range(3))
        qt = mm(wq, xtg, TN).astype(bf16) * jnp.asarray(HEAD_DIM**-0.5, bf16)
        kt = mm(wk, xtg, TN).astype(bf16)
        vt = mm(wv, xtg, TN).astype(bf16)
        keys = mm(xg, wk, NN).astype(bf16)
        values = mm(xg, wv, NN).astype(bf16)
        qt_ref[0, 0, span] = qt
        kt_ref[0, 0, span] = kt * jnp.asarray(HEAD_DIM**-0.5, bf16)
        v_ref[0, 0, group] = values
        for tile in range(tiles):
            start = key_start(tile, seq_len)
            asked = slice(tile * QUERY_TILE, (tile + 1) * QUERY_TILE)
            spread = block_diagonal(
                [qt[i * HEAD_DIM : (i + 1) * HEAD_DIM, asked] for i in range(heads)]
            )
            scores = mm(keys[start : start + window], spread, NN)
            for i in range(heads):
                probs = []
                for piece in range(QUERY_TILE // REACH):
                    low, high = live_keys(tile, piece, seq_len)
                    at = i * QUERY_TILE + piece * REACH
                    s = scores[low:high, at : at + REACH] + masks[tile, piece]
                    top = jnp.max(s, axis=0, keepdims=True)
                    e = jnp.exp(s - top)
                    total = jnp.sum(e, axis=0, keepdims=True)
                    p = (e * (1.0 / total)).astype(bf16)
                    probs.append(fill_rows(p, low, high, window))
                probs = jnp.concatenate(probs, axis=1)
                p_ref[0, 0, group, tile, :, i * QUERY_TILE : (i + 1) * QUERY_TILE] = probs
                context = mm(
                    vt[i * HEAD_DIM : (i + 1) * HEAD_DIM, start : start + window], probs, NN
                )
                at = group * width + i * HEAD_DIM
                ct_ref[0, 0, at : at + HEAD_DIM, asked] = context.astype(bf16)


def attend_back_kernel(
    last,
    aliased,
    sides,
    rows,
    place,
    dc_ref,
    ct_ref,
    p_ref,
    qt_ref,
    kt_ref,
    v_ref,
    xt_ref,
    dz_ref,
    *refs,
):
    step = pl.program_id(0)
    row = step % rows
    if len(sides) == 2:
        near_ref, crossed, traded, *refs = refs
        scr = refs.pop()

        @pl.when(step == 0)
        def _():
            scr[0] = near_ref[0].reshape(scr.shape[1:])
            scr[1, :, place[CORE]] = crossed[...]
            scr[1, :, 1 - place[CORE]] = traded[...]

        def weight(s):
            rows_of = scr[step // rows, s]
            return rows_of.reshape(2 * rows_of.shape[1], rows_of.shape[2])

    else:
        weight, refs = take_weights(place, sides[0] == 1, refs)
    if last:
        later_ref, gain0_ref, gain1_ref, *refs = refs
        if aliased:
            _, *refs = refs
        dx_ref, full_ref, keep_ref, send_ref, grad_ref, ds_ref = refs
    else:
        dx_ref, grad_ref, ds_ref = refs
        grad_ref = grad_ref.at[0]
    channels, seq_len = xt_ref.shape[2:]
    width = v_ref.shape[-1]
    window = QUERY_TILE + REACH
    heads = width // HEAD_DIM
    tiles = seq_len // QUERY_TILE
    grads = [[], [], []]
    d_inputs = []
    for group in range(channels // width):
        span = slice(group * width, (group + 1) * width)
        dq_tiles = []
        dk_tiles = []
        dv_tiles = []
        for tile in range(tiles):
            start = key_start(tile, seq_len)
            asked = slice(tile * QUERY_TILE, (tile + 1) * QUERY_TILE)
            d_context = dc_ref[0, 0, span, asked]
            context = ct_ref[0, 0, span, asked]
            both = d_context.astype(f32) * context.astype(f32)
            spread_dc = block_diagonal(
                [d_context[i * HEAD_DIM : (i + 1) * HEAD_DIM] for i in range(heads)]
            )
            qt = qt_ref[0, 0, span, asked]
            spread_q = block_diagonal(
                [qt[i * HEAD_DIM : (i + 1) * HEAD_DIM] for i in range(heads)]
            )
            d_probs = mm(v_ref[0, 0, group, start : start + window], spread_dc, NN)
            dq_heads = []
            for i in range(heads):
                shared = jnp.sum(both[i * HEAD_DIM : (i + 1) * HEAD_DIM], axis=0, keepdims=True)
                for piece in range(QUERY_TILE // REACH):
                    low, high = live_keys(tile, piece, seq_len)
                    at = i * QUERY_TILE + piece * REACH
                    p = p_ref[0, 0, group, tile, low:high, at : at + REACH].astype(f32)
                    dp = d_probs[low:high, at : at + REACH]
                    ds = (p * (dp - shared[:, piece * REACH : (piece + 1) * REACH])).astype(bf16)
                    ds_ref[:, at : at + REACH] = fill_rows(ds, low, high, window)
                of_head = slice(group * width + i * HEAD_DIM, group * width + (i + 1) * HEAD_DIM)
                dq_heads.append(
                    mm(
                        kt_ref[0, 0, of_head, start : start + window],
                        ds_ref[:, i * QUERY_TILE : (i + 1) * QUERY_TILE],
                        NN,
                    )
                )
            dq_tiles.append(jnp.concatenate(dq_heads, axis=0))
            dk_tiles.append(mm(ds_ref[...], spread_q, NT))
            dv_tiles.append(mm(p_ref[0, 0, group, tile], spread_dc, NT))
        dq = jnp.concatenate(dq_tiles, axis=1).astype(bf16)
        dk = join_windows(dk_tiles, seq_len).astype(bf16)
        dv = join_windows(dv_tiles, seq_len).astype(bf16)
        xtg = xt_ref[0, 0, span]
        grads[0].append(mm(xtg, dq, NT))
        grads[1].append(mm(xtg, dk, NN))
        grads[2].append(mm(xtg, dv, NN))
        wq, wk, wv = (weight(s)[:, span] for s in range(3))
        d_inputs.append(
            dz_ref[0, 0, span] + mm(wq, dq, NN) + mm(wk, dk, NT) + mm(wv, dv, NT)
        )
    joined = [jnp.concatenate(parts, axis=1) for parts in grads]

    @pl.when(row == 0)
    def _():
        for s in range(3):
            grad_ref[s] = joined[s]

    @pl.when(row > 0)
    def _():
        for s in range(3):
            grad_ref[s] += joined[s]

    d_input = jnp.concatenate(d_inputs, axis=0)
    if not last:
        dx_ref[0, 0] = d_input
        return
    tok = d_input.astype(bf16).T
    dx_ref[...] = tok
    full_ref[...] = tok

    @pl.when(step == pl.num_programs(0) - 1)
    def _():
        piece = width // 4
        gain_rows = jnp.concatenate([gain0_ref[...], gain1_ref[...]], axis=0).astype(bf16)
        gain_rows = jnp.concatenate([gain_rows[:, :channels], gain_rows[:, channels:]], axis=0)
        for c, out_ref in enumerate((keep_ref, send_ref)):
            for y in range(2):
                at = ((place[CORE] ^ c) * 2 + (place[ROW] ^ y)) * piece
                at_rows = pl.ds(pl.multiple_of(at, piece), piece)
                for layer, source in enumerate((grad_ref, later_ref.at[0])):
                    for s in range(3):
                        out_ref[y, pl.ds((layer * 3 + s) * piece, piece)] = source[
                            s, at_rows
                        ].astype(bf16)
                out_ref[y, pl.ds(6 * piece, 16)] = gain_rows


def join_windows(pieces, seq_len):
    window = QUERY_TILE + REACH
    rows = []
    for at in range(0, seq_len, REACH):
        held = []
        for tile, piece in enumerate(pieces):
            start = key_start(tile, seq_len)
            if start <= at < start + window:
                held.append(piece[at - start : at - start + REACH])
        rows.append(functools.reduce(jnp.add, held))
    return jnp.concatenate(rows, axis=0)


def feature_mean(values):
    return jnp.sum(values, axis=0, keepdims=True) * (1.0 / values.shape[0])


def normalize(before):
    centered = before - feature_mean(before)
    inverse = lax.rsqrt(feature_mean(centered * centered) + epsilon)
    return centered * inverse, inverse


def normalize_back(gradient, gains, normal, inverse):
    scaled = gradient * gains
    return inverse * (scaled - feature_mean(scaled) - normal * feature_mean(scaled * normal))


def gather_far(place, x_ref, c_ref, scr):
    scr[place[CORE]] = x_ref[...]
    scr[1 - place[CORE]] = c_ref[...]


class Near:
    def __init__(self, out_ref, inner_ref, outer_ref):
        self.refs = out_ref, inner_ref, outer_ref

    def out(self):
        return self.refs[0][0]

    def inner(self, group):
        hidden = self.refs[1].shape[2] // 2
        return self.refs[1][0, :, group * hidden : (group + 1) * hidden]

    def outer(self, group):
        width = self.refs[2].shape[2] // 2
        return self.refs[2][0, :, group * width : (group + 1) * width]


class Far:
    def __init__(self, pack):
        self.pack = pack

    def rows(self, k):
        rows = self.pack[:, k]
        return rows.reshape(2 * rows.shape[1], rows.shape[2])

    def out(self):
        return self.rows(0)

    def inner(self, group):
        return self.pack[group, 1]

    def outer(self, group):
        rows = self.rows(2)
        half = rows.shape[1] // 2
        width = half // 2
        at = group * width
        return jnp.concatenate(
            [rows[:, at : at + width], rows[:, half + at : half + at + width]], axis=0
        )


def spread_gains(gains_ref, layer, g_scr):
    for i in range(2):
        g_scr[i] = across(gains_ref[layer, i : i + 1, :])


def wide_gain(g_scr, i, seq_len):
    return jnp.concatenate([g_scr[i]] * (seq_len // 128), axis=1)


def split(values):
    return values.reshape(2, values.shape[0] // 2, values.shape[1])


def join(values):
    return values.reshape(2 * values.shape[1], values.shape[2])


def up(first, weights, group):
    pre = mm(weights.inner(group), first, TN)
    below = 0.5 + 0.5 * lax.erf(pre * 0.7071067811865476)
    slope = below + pre * (jnp.exp(-0.5 * pre * pre) * 0.3989422804014327)
    return (pre * below).astype(bf16), slope.astype(bf16)


def ffn_kernel(layer, place, *refs):
    (xt_ref, ct_ref, out_ref, inner_ref, outer_ref, farx_ref, farc_ref, gains_ref, *refs) = refs
    (n1_ref, r1_ref, act_ref, slope_ref, n2_ref, r2_ref, tok_ref, next_ref, *refs) = refs
    z_scr, fb_scr, far_scr, g_scr = refs
    half, tokens = z_scr.shape[1:]
    width = half // 2
    sides = (place[SELF], place[OTHER])

    @pl.when(pl.program_id(0) == 0)
    def _():
        gather_far(place, farx_ref, farc_ref, far_scr)
        spread_gains(gains_ref, layer, g_scr)

    weights = (Near(out_ref, inner_ref, outer_ref), Far(far_scr))
    z_scr[...] = split(sum(mm(weights[j].out(), ct_ref[j, 0], TN) for j in range(2)))
    for j in range(2):
        z_scr[sides[j]] += xt_ref[j, 0].astype(f32)
    normal, inverse = normalize(join(z_scr[...]))
    n1_ref[0] = split(normal.astype(bf16))
    r1_ref[0] = inverse
    first = normal * wide_gain(g_scr, 0, tokens)
    z_scr[...] = split(first)
    fb_scr[...] = split(first.astype(bf16))
    for j in range(2):
        for group in range(2):
            span = slice(group * width, (group + 1) * width)
            act, slope = up(fb_scr[sides[j], span], weights[j], group)
            act_ref[0, j, group] = act
            slope_ref[0, j, group] = slope
            z_scr[sides[j], span] += mm(weights[j].outer(group), act, TN)
    normal, inverse = normalize(join(z_scr[...]))
    n2_ref[0] = split(normal.astype(bf16))
    r2_ref[0] = inverse
    output = normal * wide_gain(g_scr, 1, tokens)
    tok_ref[...] = output.astype(bf16).T
    next_ref[0] = split(output)


def down(place, weights, acc, d_scr, b_scr, f_scr, act_of, slope_of):
    half = d_scr.shape[1]
    width = half // 2
    sides = (place[SELF], place[OTHER])
    for j in range(2):
        outers = []
        for group in range(2):
            span = slice(group * width, (group + 1) * width)
            d_branch = b_scr[sides[j], span]
            outers.append(mm(act_of(j, group), d_branch, NT))
            d_act = mm(weights[j].outer(group), d_branch, NN)
            d_pre = (d_act * slope_of(j, group).astype(f32)).astype(bf16)
            acc[j, 1, span] += mm(f_scr[sides[j], span], d_pre, NT)
            d_scr[sides[j], span] += mm(weights[j].inner(group), d_pre, NN)
        acc[j, 2] += jnp.concatenate(
            [o[:half] for o in outers] + [o[half:] for o in outers], axis=1
        )


def into_attention(d_before, weights, acc, ct_ref, dc_ref):
    d_attention = d_before.astype(bf16)
    for j in range(2):
        acc[j, 0] += mm(ct_ref[j, 0], d_attention, NT)
        dc_ref[j, 0] = mm(weights[j].out(), d_attention, NN).astype(bf16)


def hand_out(place, acc, keep_ref, send_ref):
    piece = acc.shape[2] // 8
    for c, out_ref in enumerate((keep_ref, send_ref)):
        for s in range(2):
            for j in range(2):
                for y in range(2):
                    at = ((s * 2 + (place[CORE] ^ c)) * 2 + (place[ROW] ^ y)) * piece
                    rows = pl.ds(pl.multiple_of(at, piece), piece)
                    spot = j, y, s
                    for k in range(3):
                        out_ref[(*spot, k)] = acc[j, k, rows].astype(bf16)


def hand_out_gains(gain_acc, gain_ref):
    sums = [jnp.sum(gain_acc[i], axis=1, keepdims=True) for i in range(2)]
    lane = lax.broadcasted_iota(jnp.int32, gain_acc.shape[1:], 1)
    gain_ref[...] = jnp.where(lane == 0, sums[0], sums[1]).T[:4]


def ffn_last_kernel(layer, place, *refs):
    (x_ref, ct_ref, cot_ref, out_ref, inner_ref, outer_ref, *refs) = refs
    (farx_ref, farc_ref, gains_ref, tok_ref, full_ref, *refs) = refs
    (dz1_ref, dc_ref, keep_ref, send_ref, gain_ref, *refs) = refs
    (z_scr, fb_scr, b_scr, n_scr, act_scr, slope_scr, far_scr, g_scr, acc, gain_acc) = refs
    half, tokens = z_scr.shape[1:]
    width = half // 2
    sides = (place[SELF], place[OTHER])
    step = pl.program_id(0)

    @pl.when(step == 0)
    def _():
        gather_far(place, farx_ref, farc_ref, far_scr)
        spread_gains(gains_ref, layer, g_scr)
        acc[...] = jnp.zeros_like(acc)
        gain_acc[...] = jnp.zeros_like(gain_acc)

    weights = (Near(out_ref, inner_ref, outer_ref), Far(far_scr))
    attention = sum(mm(weights[j].out(), ct_ref[j, 0], TN) for j in range(2))
    normal, inverse1 = normalize(attention + join(x_ref[0]))
    n_scr[...] = normal
    first = normal * wide_gain(g_scr, 0, tokens)
    z_scr[...] = split(first)
    fb_scr[...] = split(first.astype(bf16))
    for j in range(2):
        for group in range(2):
            span = slice(group * width, (group + 1) * width)
            act, slope = up(fb_scr[sides[j], span], weights[j], group)
            act_scr[j, group] = act
            slope_scr[j, group] = slope
            z_scr[sides[j], span] += mm(weights[j].outer(group), act, TN)
    normal, inverse = normalize(join(z_scr[...]))
    gain = wide_gain(g_scr, 1, tokens)
    tok = (normal * gain).astype(bf16).T
    tok_ref[...] = tok
    full_ref[...] = tok

    g = cot_ref[...].T.astype(f32)
    gain_acc[1] += lane_sum(g * normal)
    d_second = normalize_back(g, gain, normal, inverse)
    z_scr[...] = split(d_second)
    b_scr[...] = split(d_second.astype(bf16))
    down(
        place,
        weights,
        acc,
        z_scr,
        b_scr,
        fb_scr,
        lambda j, group: act_scr[j, group],
        lambda j, group: slope_scr[j, group],
    )
    d_first = join(z_scr[...])
    normal = n_scr[...]
    gain_acc[0] += lane_sum(d_first * normal)
    d_before = normalize_back(d_first, wide_gain(g_scr, 0, tokens), normal, inverse1)
    dz1_ref[0] = split(d_before)
    into_attention(d_before, weights, acc, ct_ref, dc_ref)

    @pl.when(step == pl.num_programs(0) - 1)
    def _():
        hand_out(place, acc, keep_ref, send_ref)
        hand_out_gains(gain_acc, gain_ref)


def ffn_back_kernel(layer, place, *refs):
    (g_ref, n2_ref, r2_ref, act_ref, slope_ref, n1_ref, r1_ref, ct_ref, *refs) = refs
    (out_ref, inner_ref, outer_ref, farx_ref, farc_ref, gains_ref, *refs) = refs
    (dz1_ref, dc_ref, keep_ref, send_ref, gain_ref, *refs) = refs
    d_scr, b_scr, f_scr, far_scr, g_scr, acc, gain_acc = refs
    tokens = d_scr.shape[2]
    sides = (place[SELF], place[OTHER])
    step = pl.program_id(0)

    @pl.when(step == 0)
    def _():
        gather_far(place, farx_ref, farc_ref, far_scr)
        spread_gains(gains_ref, layer, g_scr)
        acc[...] = jnp.zeros_like(acc)
        gain_acc[...] = jnp.zeros_like(gain_acc)

    weights = (Near(out_ref, inner_ref, outer_ref), Far(far_scr))
    for j in range(2):
        d_scr[sides[j]] = g_ref[j, 0]
    g = join(d_scr[...])
    normal = join(n2_ref[0]).astype(f32)
    gain_acc[1] += lane_sum(g * normal)
    d_second = normalize_back(g, wide_gain(g_scr, 1, tokens), normal, r2_ref[0])
    d_scr[...] = split(d_second)
    b_scr[...] = split(d_second.astype(bf16))
    normal = join(n1_ref[0]).astype(f32)
    gain = wide_gain(g_scr, 0, tokens)
    f_scr[...] = split((normal * gain).astype(bf16))
    down(
        place,
        weights,
        acc,
        d_scr,
        b_scr,
        f_scr,
        lambda j, group: act_ref[0, j, group],
        lambda j, group: slope_ref[0, j, group],
    )
    d_first = join(d_scr[...])
    gain_acc[0] += lane_sum(d_first * normal)
    d_before = normalize_back(d_first, gain, normal, r1_ref[0])
    dz1_ref[0] = split(d_before)
    into_attention(d_before, weights, acc, ct_ref, dc_ref)

    @pl.when(step == pl.num_programs(0) - 1)
    def _():
        hand_out(place, acc, keep_ref, send_ref)
        hand_out_gains(gain_acc, gain_ref)


def lane_sum(values):
    chunks = [values[:, at : at + 128] for at in range(0, values.shape[1], 128)]
    return functools.reduce(jnp.add, chunks)


def placed_pieces(place, parts, size):
    mine, row, core = parts
    for c, y, value in ((0, 0, mine[...]), (0, 1, row[...]), (1, 0, core[0]), (1, 1, core[1])):
        yield ((place[CORE] ^ c) * 2 + (place[ROW] ^ y)) * size, value


def rows_at(at, size):
    return pl.ds(pl.multiple_of(at, size), size)


def finish_ffn_kernel(place, *refs):
    out_ref, inner_ref, outer_ref = refs[-3:]
    half, wide = out_ref.shape[1:]
    size = half // 8
    for at, value in placed_pieces(place, refs[:3], size):
        value = value.astype(f32)
        for s in range(2):
            low = s * (half // 2) + at
            out_ref[0, rows_at(low, size), :] = value[s, 0]
            inner_ref[0, rows_at(at, size), s * wide : (s + 1) * wide] = value[s, 1]
            outer_ref[0, rows_at(low, size), :] = value[s, 2][:, :half]
            outer_ref[0, rows_at(half + low, size), :] = value[s, 2][:, half:]


def finish_qkv_kernel(place, mine, row, core, qkv_ref, gain_ref):
    half = qkv_ref.shape[3]
    size = qkv_ref.shape[2] // 4
    for at, value in placed_pieces(place, (mine, row, core), size):
        for layer in range(2):
            for s in range(3):
                index = (layer * 3 + s) * size
                qkv_ref[layer, s, rows_at(at, size), :] = value[index : index + size].astype(f32)
    gains = mine[6 * size : 6 * size + 16].astype(f32)
    for layer in range(2):
        for i in range(2):
            at = layer * 4 + i
            gain_ref[layer, i : i + 1, :half] = gains[at : at + 1]
            gain_ref[layer, i : i + 1, half:] = gains[8 + at : 9 + at]


def pack_kernel(place, out_ref, inner_ref, low_ref, high_ref, qkv_ref, piece_ref, part_ref):
    half = low_ref.shape[2]
    piece_ref[0] = out_ref[0]
    piece_ref[1] = inner_ref[0]
    piece_ref[2, :, :half] = low_ref[0]
    piece_ref[2, :, half:] = high_ref[0]
    part_ref[...] = qkv_ref[0]


def whole(shape):
    return pl.BlockSpec(shape, lambda r, place: (0,) * len(shape))


def per_row(shape):
    rest = (0,) * (len(shape) - 1)
    return pl.BlockSpec((1,) + tuple(shape[1:]), lambda r, place: (r,) + rest)


def struct(shape, dtype):
    return jax.ShapeDtypeStruct(shape, dtype)


def call(
    kernel, rows, place, operands, in_specs, outs, out_specs, scratch, name, us, aliases=None, after=()
):
    count = len(operands)
    in_specs = list(in_specs) + [pl.BlockSpec(memory_space=pl.ANY)] * len(after)
    operands = tuple(operands) + tuple(after)

    def body(place, *refs):
        kernel(place, *refs[:count], *refs[count + len(after) :])

    results = pl.pallas_call(
        body,
        out_shape=outs,
        grid_spec=pltpu.PrefetchScalarGridSpec(
            num_scalar_prefetch=1,
            grid=(rows,),
            in_specs=in_specs,
            out_specs=out_specs,
            scratch_shapes=scratch,
        ),
        compiler_params=pltpu.CompilerParams(vmem_limit_bytes=64 * 2**20 - 2**16),
        cost_estimate=pl.CostEstimate(
            flops=int(us * 5e9), bytes_accessed=int(us * 1e7), transcendentals=0
        ),
        input_output_aliases=aliases or {},
        name=name,
    )(place, *operands)
    return list(results)


def per_side(shape, side):
    rest = (0,) * (len(shape) - 2)
    return pl.BlockSpec((1, 1) + tuple(shape[2:]), lambda r, place: (side, r) + rest)


def both_sides(shape, parts=1):
    middle = (0,) * (len(shape) - 3)
    return pl.BlockSpec(
        (2, 1) + tuple(shape[2:-1]) + (shape[-1] // parts,),
        lambda t, place: (0, t // parts, *middle, t % parts),
    )


def attend(x_tok, w, segments, place, rows, j, layer, us, held=(), after=()):
    row_total, seq_len = segments.shape
    far = j == 1
    channels = w[0].shape[-1]
    width = channels // 2
    heads = width // HEAD_DIM
    groups = channels // width
    tiles = seq_len // QUERY_TILE
    window = QUERY_TILE + REACH
    outs = [
        struct((2, rows, channels, seq_len), bf16),
        struct((2, rows, channels, seq_len), bf16),
        struct((2, rows, channels, seq_len), bf16),
        struct((2, rows, groups, seq_len, width), bf16),
        struct((2, rows, groups, tiles, window, heads * QUERY_TILE), bf16),
        struct((2, rows, channels, seq_len), bf16),
    ]
    if layer == 0:
        x_spec = pl.BlockSpec((seq_len, channels), lambda r, place: (place[OFFSET] + r, place[j]))
    else:
        x_spec = pl.BlockSpec((seq_len, channels), lambda r, place: (r, place[j]))
    operands = (x_tok, *w, segments)
    return call(
        functools.partial(attend_kernel, far),
        rows,
        place,
        operands + tuple(held),
        [x_spec, *weight_blocks(w, far, layer), whole(segments.shape)]
        + [pl.BlockSpec(memory_space=pl.ANY)] * len(held),
        outs,
        [per_side(o.shape, j) for o in outs],
        weight_scratch(w, far),
        "attend",
        us,
        {len(operands) + 1 + i: i for i in range(len(held))},
        after,
    )


def weight_blocks(w, far, layer):
    return [whole(o.shape) for o in w] if far else [layer_block(w[0].shape, layer)]


def weight_scratch(w, far):
    if not far:
        return []
    three, depth, channels = w[0].shape
    return [pltpu.VMEM((three, 2, depth, channels), bf16)]


def layer_block(shape, layer):
    rest = (0,) * (len(shape) - 1)
    return pl.BlockSpec((None,) + tuple(shape[1:]), lambda r, place: (layer,) + rest)


def attend_back(d_context, saved, w, d_before, place, rows, sides, layer, extra, us, after=()):
    xt, qt, kt, values, probs, ct = saved
    channels, seq_len = xt.shape[2:]
    window = QUERY_TILE + REACH
    width = values.shape[-1]
    heads = width // HEAD_DIM
    operands = (d_context, ct, probs, qt, kt, values, xt)
    scratch = [pltpu.VMEM((window, heads * QUERY_TILE), bf16)]
    grad = (3, width, channels)
    if len(sides) == 2:
        near, *far = w
        w_specs = [layer_block4(near.shape, layer)] + [whole(o.shape) for o in far]
        scratch += [pltpu.VMEM((2, 3, 2, width // 2, channels), bf16)]
    else:
        w_specs = weight_blocks(w, sides[0] == 1, layer)
        scratch += weight_scratch(w, sides[0] == 1)

    def side(t):
        return t // rows if len(sides) == 2 else sides[0]

    def one(shape):
        rest = (0,) * (len(shape) - 2)
        return pl.BlockSpec(
            (1, 1) + tuple(shape[2:]), lambda t, place: (side(t), t % rows) + rest
        )

    in_specs = [one(o.shape) for o in operands] + [
        pl.BlockSpec(
            (1, 1, channels, seq_len), lambda t, place: (t % rows, place[side(t)], 0, 0)
        ),
        *w_specs,
    ]
    operands += (d_before, *w)
    aliases = {}
    if extra is None:
        outs = [struct((2, rows, channels, seq_len), f32), struct((2,) + grad, f32)]
        out_specs = [
            one(outs[0].shape),
            pl.BlockSpec((1,) + grad, lambda t, place: (side(t), 0, 0, 0)),
        ]
    else:
        later, gain0, gain1, full = extra
        operands += (later, gain0, gain1)
        in_specs += [one_layer(later.shape, sides[0]), whole(gain0.shape), whole(gain1.shape)]
        if full is not None:
            aliases = {len(operands) + 1: 1}
            operands += (full,)
            in_specs.append(pl.BlockSpec(memory_space=pl.ANY))
        piece = struct((2, 6 * (width // 4) + 16, channels), bf16)
        outs = [
            struct((rows * seq_len, channels), bf16),
            struct((2 * rows * seq_len, 2 * channels), bf16),
            piece,
            piece,
        ]
        out_specs = [
            pl.BlockSpec((seq_len, channels), lambda r, place: (r, 0)),
            pl.BlockSpec(
                (seq_len, channels), lambda r, place: (place[OFFSET] + r, place[sides[0]])
            ),
            whole(piece.shape),
            whole(piece.shape),
        ]
        scratch = [pltpu.VMEM(grad, f32)] + scratch
    return call(
        functools.partial(attend_back_kernel, extra is not None, bool(aliases), sides, rows),
        len(sides) * rows,
        place,
        operands,
        in_specs,
        outs,
        out_specs,
        scratch,
        "attend_back",
        us,
        aliases,
        after,
    )


def layer_block4(shape, layer):
    rest = (0,) * (len(shape) - 1)
    return pl.BlockSpec((1,) + tuple(shape[1:]), lambda t, place: (layer,) + rest)


def per_part(shape, parts):
    middle = (0,) * (len(shape) - 2)
    return pl.BlockSpec(
        (1,) + tuple(shape[1:-1]) + (shape[-1] // parts,),
        lambda t, place: (t // parts, *middle, t % parts),
    )


def weight_specs(weights, layer):
    return [one_layer(o.shape, layer) for o in weights[:3]] + [whole(o.shape) for o in weights[3:]]


def ffn(xts, contexts, weights, gains, place, rows, layer, us):
    half, seq_len = contexts.shape[2:]
    parts = 1
    tokens = seq_len // parts
    stream = (rows, 2, half, seq_len)
    acts = (rows, 2, 2, 2 * half, seq_len)
    outs = [
        struct(stream, bf16),
        struct((rows, 1, seq_len), f32),
        struct(acts, bf16),
        struct(acts, bf16),
        struct(stream, bf16),
        struct((rows, 1, seq_len), f32),
        struct((rows * seq_len, 2 * half), bf16),
        struct(stream, f32),
    ]
    out_specs = [per_part(o.shape, parts) for o in outs]
    out_specs[6] = pl.BlockSpec((tokens, 2 * half), lambda t, place: (t, 0))
    return call(
        functools.partial(ffn_kernel, layer),
        rows * parts,
        place,
        (xts, contexts, *weights, gains),
        [both_sides(xts.shape, parts), both_sides(contexts.shape, parts)]
        + weight_specs(weights, layer)
        + [whole(gains.shape)],
        outs,
        out_specs,
        [
            pltpu.VMEM((2, half, tokens), f32),
            pltpu.VMEM((2, half, tokens), bf16),
            pltpu.VMEM((2,) + weights[3].shape, bf16),
            pltpu.VMEM((2, 2 * half, 128), f32),
        ],
        "ffn",
        us,
    )


def sum_shapes(half):
    piece = struct((2, 2, 2, 3, half // 8, 2 * half), bf16)
    return [piece, piece, struct((4, 2 * half), f32)]


def sum_scratch(weights, half):
    return [
        pltpu.VMEM((2,) + weights[3].shape, bf16),
        pltpu.VMEM((2, 2 * half, 128), f32),
        pltpu.VMEM((2, 3, half, 2 * half), f32),
        pltpu.VMEM((2, 2 * half, 128), f32),
    ]


def ffn_last(x, contexts, cotangent, weights, gains, place, rows, layer, us):
    half, seq_len = contexts.shape[2:]
    wide = 2 * half
    outs = [
        struct((rows * seq_len, wide), bf16),
        struct((2 * rows * seq_len, wide), bf16),
        struct((rows, 2, half, seq_len), f32),
        struct(contexts.shape, bf16),
        *sum_shapes(half),
    ]
    own = pl.BlockSpec((seq_len, wide), lambda r, place: (place[OFFSET] + r, 0))
    out_specs = (
        [pl.BlockSpec((seq_len, wide), lambda r, place: (r, 0)), own]
        + [per_row(outs[2].shape), both_sides(outs[3].shape)]
        + [whole(o.shape) for o in outs[4:]]
    )
    stream = (2, half, seq_len)
    acts = (2, 2, wide, seq_len)
    return call(
        functools.partial(ffn_last_kernel, layer),
        rows,
        place,
        (x, contexts, cotangent, *weights, gains),
        [per_row(x.shape), both_sides(contexts.shape), own]
        + weight_specs(weights, layer)
        + [whole(gains.shape)],
        outs,
        out_specs,
        [
            pltpu.VMEM(stream, f32),
            pltpu.VMEM(stream, bf16),
            pltpu.VMEM(stream, bf16),
            pltpu.VMEM((wide, seq_len), f32),
            pltpu.VMEM(acts, bf16),
            pltpu.VMEM(acts, bf16),
            *sum_scratch(weights, half),
        ],
        "ffn_last",
        us,
    )


def ffn_back(g, saved, contexts, weights, gains, place, rows, layer, us, after=()):
    half, seq_len = contexts.shape[2:]
    stream = (2, half, seq_len)
    outs = [
        struct((rows,) + stream, f32),
        struct(contexts.shape, bf16),
        *sum_shapes(half),
    ]
    out_specs = [per_row(outs[0].shape), both_sides(outs[1].shape)] + [
        whole(o.shape) for o in outs[2:]
    ]
    return call(
        functools.partial(ffn_back_kernel, layer),
        rows,
        place,
        (g, *saved, contexts, *weights, gains),
        [both_sides(g.shape)]
        + [per_row(o.shape) for o in saved]
        + [both_sides(contexts.shape)]
        + weight_specs(weights, layer)
        + [whole(gains.shape)],
        outs,
        out_specs,
        [
            pltpu.VMEM(stream, f32),
            pltpu.VMEM(stream, bf16),
            pltpu.VMEM(stream, bf16),
            *sum_scratch(weights, half),
        ],
        "ffn_back",
        us,
        after=after,
    )


def one_layer(shape, layer):
    rest = (0,) * (len(shape) - 1)
    return pl.BlockSpec((1,) + tuple(shape[1:]), lambda r, place: (layer,) + rest)


def finish_ffn(parts, place, layer, layers, held=()):
    operands = list(parts)
    half = operands[0].shape[-1] // 2
    outs = [
        struct((layers, half, 2 * half), f32),
        struct((layers, half // 2, 4 * half), f32),
        struct((layers, 2 * half, half), f32),
    ]
    return call(
        finish_ffn_kernel,
        1,
        place,
        operands + list(held),
        [whole(o.shape) for o in operands] + [pl.BlockSpec(memory_space=pl.ANY)] * len(held),
        outs,
        [one_layer(o.shape, layer) for o in outs],
        [],
        "finish_ffn",
        3,
        {4 + i: i for i in range(len(held))},
    )


def finish_qkv(parts, place, layers, width):
    half = parts[0].shape[-1]
    outs = [struct((layers, 3, width, half), f32), struct((layers, 2, 2 * half), f32)]
    return call(
        finish_qkv_kernel,
        1,
        place,
        parts,
        [whole(o.shape) for o in parts],
        outs,
        [whole(o.shape) for o in outs],
        [],
        "finish_qkv",
        3,
    )


def pack(weights, place, layer, after=()):
    out_w, inner_w, outer_w, qkv_w = weights
    half, wide = out_w.shape[1:]
    three, depth, channels = qkv_w.shape[1:]
    rows = half // 2
    outs = [struct((3, rows, wide), bf16), struct((three, depth // 2, channels), bf16)]
    return call(
        pack_kernel,
        1,
        place,
        (out_w, inner_w, outer_w, outer_w, qkv_w),
        [
            pl.BlockSpec((1, rows, wide), lambda r, place: (layer, place[CORE], 0)),
            pl.BlockSpec((1, depth, wide), lambda r, place: (layer, 0, place[CORE])),
            pl.BlockSpec((1, rows, half), lambda r, place: (layer, place[CORE], 0)),
            pl.BlockSpec((1, rows, half), lambda r, place: (layer, 2 + place[CORE], 0)),
            pl.BlockSpec((1, three, depth // 2, channels), lambda r, place: (layer, 0, place[CORE], 0)),
        ],
        outs,
        [whole(o.shape) for o in outs],
        [],
        "pack",
        3,
        after=after,
    )


def hold(values, place, after):
    anywhere = pl.BlockSpec(memory_space=pl.ANY)
    return call(
        lambda place, *refs: None,
        1,
        place,
        values,
        [anywhere] * len(values),
        [struct(v.shape, v.dtype) for v in values],
        [anywhere] * len(values),
        [],
        "hold",
        1,
        {i + 1: i for i in range(len(values))},
        after,
    )


def fill_input_kernel(place, full_ref, own_ref, far_ref, out_ref):
    column = pl.program_id(1)

    @pl.when(column == 0)
    def _():
        out_ref[...] = own_ref[...]

    @pl.when(column == 1)
    def _():
        out_ref[...] = far_ref[...]


def fill_input(full, from_own, from_far, place, rows, seq_len):
    half = from_own.shape[1]
    block = pl.BlockSpec((seq_len, half), lambda r, j, place: (r, 0))
    return pl.pallas_call(
        fill_input_kernel,
        out_shape=struct(full.shape, full.dtype),
        grid_spec=pltpu.PrefetchScalarGridSpec(
            num_scalar_prefetch=1,
            grid=(rows, 2),
            in_specs=[pl.BlockSpec(memory_space=pl.ANY), block, block],
            out_specs=pl.BlockSpec(
                (seq_len, half),
                lambda r, j, place: (rows - place[OFFSET] + r, (1 - place[SELF]) ^ j),
            ),
        ),
        input_output_aliases={1: 0},
        name="fill_input",
    )(place, full, from_own, from_far)


def swap(values):
    return lax.ppermute(values, "head", [(0, 1), (1, 0)])


def cross(values):
    count = lax.axis_size("dp")
    return lax.ppermute(
        values, ("dp", "head"), [(2 * a + h, 2 * (a ^ 2) + 1 - h) for a in range(count) for h in range(2)]
    )


def scatter(parts):
    return [swap(parts[0]), trade(parts[1], 2), cross(parts[2])]


SHARES = ((1, 0), (0, 1), (1, 1))


def trade(values, stride):
    count = lax.axis_size("dp")
    return lax.ppermute(values, "dp", [(a, a ^ stride) for a in range(count)])


def far_strides():
    count = lax.axis_size("dp")
    strides = []
    stride = 4
    while stride < count:
        strides.append(stride)
        stride *= 2
    return strides


def sums(groups, place, after=(), casts=None):
    operands = []
    plan = []
    for group in groups:
        terms = []
        for term in group:
            value, *index = term if isinstance(term, tuple) else (term,)
            terms.append((len(operands), tuple(index)))
            operands.append(value)
        plan.append(terms)
    outs = [
        struct(operands[terms[0][0]].shape[len(terms[0][1]) :], operands[terms[0][0]].dtype)
        for terms in plan
    ]

    def kernel(place, *refs):
        for terms, out in zip(plan, refs[len(operands) :]):
            out[...] = functools.reduce(
                jnp.add, [refs[at][...].astype(f32) for at, _ in terms]
            ).astype(out.dtype)

    def spec(value, index):
        shape = value.shape[len(index) :]
        return pl.BlockSpec(
            (None,) * len(index) + tuple(shape),
            lambda r, place: tuple(index) + (0,) * len(shape),
        )

    return call(
        kernel,
        1,
        place,
        operands,
        [spec(operands[at], index) for terms in plan for at, index in terms],
        outs,
        [whole(o.shape) for o in outs],
        [],
        "sums",
        2,
        after=after,
    )


def add(*terms):
    return functools.reduce(jnp.add, [t.astype(f32) for t in terms]).astype(bf16)


def shards(
    tokens, segments, qkv_weight, out_weight, inner_weight, outer_weight, norm_gains, cotangent
):
    side = lax.axis_index("head").astype(jnp.int32)
    spot = lax.axis_index("dp").astype(jnp.int32)
    layers = qkv_weight.shape[0]
    row_total, seq_len = segments.shape
    rows = row_total // 2
    width = qkv_weight.shape[2]
    place = jnp.stack([side, 1 - side, side * rows, spot & 1, (spot >> 1) & 1])
    weights = (out_weight, inner_weight, outer_weight)
    one = (qkv_weight,)
    far_qkv = [None, None]
    ffn_weights = [None, None]

    piece, part = pack((*weights, qkv_weight), place, 0)
    part, piece = swap(part), swap(piece)
    near = attend(tokens, one, segments, place, rows, 0, 0, 9)
    (part,) = hold([part], place, [near[5]])
    far_qkv[0] = (part, trade(part, 1))
    next_piece, next_part = pack((*weights, qkv_weight), place, 1, [near[5]])
    held = attend(tokens, far_qkv[0], segments, place, rows, 1, 0, 0.2, near, [next_piece])
    piece, next_piece, next_part = hold([piece, next_piece, next_part], place, [held[5]])
    ffn_weights[0] = (*weights, piece, trade(piece, 1))
    part, piece = swap(next_part), swap(next_piece)
    ffn_weights[1] = (*weights, piece, trade(piece, 1))
    saved_attend = [held]
    n1, r1, act, slope, n2, r2, x_tok, x_stream = ffn(
        held[0], held[5], ffn_weights[0], norm_gains, place, rows, 0, 20
    )
    saved_ffn = (n2, r2, act, slope, n1, r1)
    (part,) = hold([part], place, [x_tok])
    far_qkv[1] = (part, trade(part, 1))
    near = attend(x_tok, one, segments, place, rows, 0, 1, 9)
    held = attend(x_tok, far_qkv[1], segments, place, rows, 1, 1, 9, near)
    saved_attend.append(held)
    x_tok, activations, d_before, d_context, keep, send, gain1 = ffn_last(
        x_stream, held[5], cotangent, ffn_weights[1], norm_gains, place, rows, 1, 40
    )

    strides = far_strides()
    far_tok = swap(x_tok)
    got = trade(send, 1)
    dx, later = attend_back(
        d_context, held, one + far_qkv[1], d_before, place, rows, (0, 1), 1, None, 0.2
    )
    parts = sums([[(keep, *at), (got, *at)] for at in SHARES], place, [dx])
    crossed = scatter(parts)
    d_before, d_context, next_keep, next_send, gain0 = ffn_back(
        dx, saved_ffn, saved_attend[0][5], ffn_weights[0], norm_gains, place, rows, 0, 0.2, parts
    )
    (late,) = sums([[(keep, 0, 0), (got, 0, 0), *crossed]], place, [d_before])
    late_got = trade(late, strides[0])
    keep, send = next_keep, next_send
    got = trade(send, 1)
    dx1, full, keep1, send1 = attend_back(
        d_context,
        saved_attend[0],
        far_qkv[0],
        d_before,
        place,
        rows,
        (1,),
        0,
        (later, gain0, gain1, None),
        13,
        [late, far_tok],
    )
    core1 = trade(send1, 1)
    *parts, late = sums(
        [[(keep, *at), (got, *at)] for at in SHARES] + [[late, late_got]], place, [dx1]
    )
    crossed = scatter(parts)
    late_got = trade(late, strides[1])
    dx0, full, keep0, send0 = attend_back(
        d_context,
        saved_attend[0],
        one,
        d_before,
        place,
        rows,
        (0,),
        0,
        (later, gain0, gain1, full),
        13,
        parts + [late],
    )
    core0 = trade(send0, 1)
    (core1,) = hold([core1], place, [dx0])
    shares = [add(keep1[0], core1[0]), add(keep0[1], core0[1]), add(keep1[1], core1[1])]
    shares = scatter(shares)
    total = add(keep0[0], core0[0], *shares)
    early = [add(keep[0, 0, s], got[0, 0, s], *[c[s] for c in crossed]) for s in range(2)]
    orders = (strides, strides[::-1])
    late = add(late, late_got)
    for stride in strides[2:]:
        late = add(late, trade(late, stride))
    late_row = trade(late, 2)
    late_core = trade(jnp.stack([late, late_row]), 1)
    dx0, dx1 = hold([dx0, dx1], place, early)
    far_dx0, far_dx1 = swap(dx0), swap(dx1)
    for at in range(len(strides)):
        early = [add(early[s], trade(early[s], orders[s][at])) for s in range(2)]
        total = add(total, trade(total, strides[at]))
    early = jnp.stack(early)
    grads = finish_ffn([late, late_row, late_core], place, 1, layers)
    early, total = hold([early, total], place, [grads[0]])
    early_row = trade(early, 2)
    row = trade(total, 2)
    input_grad = fill_input(full, far_dx0, far_dx1, place, rows, seq_len)
    both = jnp.stack([early, early_row])
    (both,) = hold([both], place, [input_grad])
    early_core = trade(both, 1)
    core_part = trade(jnp.stack([total, row]), 1)
    other_rows = (1 - side) * rows * seq_len
    activations = lax.dynamic_update_slice(activations, far_tok, (other_rows, jnp.int32(0)))
    out_grad, inner_grad, outer_grad = finish_ffn(
        [early, early_row, early_core], place, 0, layers, grads
    )
    qkv_grad, gain_grad = finish_qkv([total, row, core_part], place, layers, width)
    return (activations, input_grad, qkv_grad, out_grad, inner_grad, outer_grad, gain_grad)


def solution(mesh):
    return jax.shard_map(
        shards,
        mesh=mesh,
        in_specs=(
            P("dp", None),
            P("dp", None),
            P(None, None, None, "head"),
            P(None, "head", None),
            P(None, None, "head"),
            P(None, None, "head"),
            P(),
            P("dp", None),
        ),
        out_specs=(
            P("dp", None),
            P("dp", None),
            P(None, None, None, "head"),
            P(None, "head", None),
            P(None, None, "head"),
            P(None, None, "head"),
            P(),
        ),
        check_vma=False,
    )
```

```python
import functools
import jax
import jax.numpy as jnp
from jax import lax
from jax.experimental import pallas as pl
from jax.experimental.pallas import tpu as pltpu
from jax.sharding import PartitionSpec as P

HEAD_DIM = 64
QUERY_TILE = 256
REACH = 128

SELF, OTHER, OFFSET, CORE, ROW = range(5)

epsilon = 1e-12
masked_score = -1e30
f32 = jnp.float32
bf16 = jnp.bfloat16

NN = (((1,), (0,)), ((), ()))
NT = (((1,), (1,)), ((), ()))
TN = (((0,), (0,)), ((), ()))


def mm(left, right, dims):
    return lax.dot_general(left, right, dims, preferred_element_type=f32)


def key_start(tile, seq_len):
    return min(max(tile * QUERY_TILE - REACH, 0), seq_len - QUERY_TILE - REACH)


def live_keys(tile, piece, seq_len):
    window = QUERY_TILE + REACH
    first_query = tile * QUERY_TILE + piece * REACH
    start = key_start(tile, seq_len)
    low = max(first_query - REACH - start, 0)
    high = min(first_query + 2 * REACH - start, window)
    return low, high


def block_diagonal(parts):
    rows = []
    for index, part in enumerate(parts):
        empty = jnp.zeros_like(part)
        rows.append(
            jnp.concatenate([part if at == index else empty for at in range(len(parts))], axis=1)
        )
    return jnp.concatenate(rows, axis=0)


def fill_rows(middle, low, high, total):
    pieces = []
    if low > 0:
        pieces.append(jnp.zeros((low, middle.shape[1]), middle.dtype))
    pieces.append(middle)
    if high < total:
        pieces.append(jnp.zeros((total - high, middle.shape[1]), middle.dtype))
    return jnp.concatenate(pieces, axis=0) if len(pieces) > 1 else middle


def across(row):
    return jnp.broadcast_to(row, (128, row.shape[1])).T


def take_weights(place, far, refs):
    if not far:
        return (lambda s: refs[0][s]), refs[1:]
    crossed, traded, *refs = refs
    scr = refs.pop()

    @pl.when(pl.program_id(0) == 0)
    def _():
        scr[:, place[CORE]] = crossed[...]
        scr[:, 1 - place[CORE]] = traded[...]

    return (lambda s: scr[s].reshape(2 * scr.shape[2], scr.shape[3])), refs


def attend_kernel(far, place, x_ref, *refs):
    weight, refs = take_weights(place, far, refs)
    seg_ref, *refs = refs
    xt_ref, qt_ref, kt_ref, v_ref, p_ref, ct_ref = refs[-6:]
    seq_len, channels = x_ref.shape
    width = v_ref.shape[-1]
    window = QUERY_TILE + REACH
    heads = width // HEAD_DIM
    tiles = seq_len // QUERY_TILE
    x = x_ref[...]
    xt = x.T
    xt_ref[0, 0] = xt
    segq = seg_ref[pl.ds(place[OFFSET] + pl.program_id(0), 1), :].astype(f32)
    segk = across(segq)
    masks = {}
    for tile in range(tiles):
        start = key_start(tile, seq_len)
        for piece in range(QUERY_TILE // REACH):
            low, high = live_keys(tile, piece, seq_len)
            at = tile * QUERY_TILE + piece * REACH
            same = segk[start + low : start + high] == segq[:, at : at + REACH]
            masks[tile, piece] = jnp.where(same, 0.0, masked_score)
    for group in range(channels // width):
        span = slice(group * width, (group + 1) * width)
        xg = x[:, span]
        xtg = xt[span]
        wq, wk, wv = (weight(s)[:, span] for s in range(3))
        qt = mm(wq, xtg, TN).astype(bf16) * jnp.asarray(HEAD_DIM**-0.5, bf16)
        kt = mm(wk, xtg, TN).astype(bf16)
        vt = mm(wv, xtg, TN).astype(bf16)
        keys = mm(xg, wk, NN).astype(bf16)
        values = mm(xg, wv, NN).astype(bf16)
        qt_ref[0, 0, span] = qt
        kt_ref[0, 0, span] = kt * jnp.asarray(HEAD_DIM**-0.5, bf16)
        v_ref[0, 0, group] = values
        for tile in range(tiles):
            start = key_start(tile, seq_len)
            asked = slice(tile * QUERY_TILE, (tile + 1) * QUERY_TILE)
            spread = block_diagonal(
                [qt[i * HEAD_DIM : (i + 1) * HEAD_DIM, asked] for i in range(heads)]
            )
            scores = mm(keys[start : start + window], spread, NN)
            for i in range(heads):
                probs = []
                for piece in range(QUERY_TILE // REACH):
                    low, high = live_keys(tile, piece, seq_len)
                    at = i * QUERY_TILE + piece * REACH
                    s = scores[low:high, at : at + REACH] + masks[tile, piece]
                    top = jnp.max(s, axis=0, keepdims=True)
                    e = jnp.exp(s - top)
                    total = jnp.sum(e, axis=0, keepdims=True)
                    p = (e * (1.0 / total)).astype(bf16)
                    probs.append(fill_rows(p, low, high, window))
                probs = jnp.concatenate(probs, axis=1)
                p_ref[0, 0, group, tile, :, i * QUERY_TILE : (i + 1) * QUERY_TILE] = probs
                context = mm(
                    vt[i * HEAD_DIM : (i + 1) * HEAD_DIM, start : start + window], probs, NN
                )
                at = group * width + i * HEAD_DIM
                ct_ref[0, 0, at : at + HEAD_DIM, asked] = context.astype(bf16)


def attend_back_kernel(
    last,
    aliased,
    sides,
    rows,
    place,
    dc_ref,
    ct_ref,
    p_ref,
    qt_ref,
    kt_ref,
    v_ref,
    xt_ref,
    dz_ref,
    *refs,
):
    step = pl.program_id(0)
    row = step % rows
    if len(sides) == 2:
        near_ref, crossed, traded, *refs = refs
        scr = refs.pop()

        @pl.when(step == 0)
        def _():
            scr[0] = near_ref[0].reshape(scr.shape[1:])
            scr[1, :, place[CORE]] = crossed[...]
            scr[1, :, 1 - place[CORE]] = traded[...]

        def weight(s):
            rows_of = scr[step // rows, s]
            return rows_of.reshape(2 * rows_of.shape[1], rows_of.shape[2])

    else:
        weight, refs = take_weights(place, sides[0] == 1, refs)
    if last:
        later_ref, gain0_ref, gain1_ref, *refs = refs
        if aliased:
            _, *refs = refs
        dx_ref, full_ref, keep_ref, send_ref, grad_ref, ds_ref = refs
    else:
        dx_ref, grad_ref, ds_ref = refs
        grad_ref = grad_ref.at[0]
    channels, seq_len = xt_ref.shape[2:]
    width = v_ref.shape[-1]
    window = QUERY_TILE + REACH
    heads = width // HEAD_DIM
    tiles = seq_len // QUERY_TILE
    grads = [[], [], []]
    d_inputs = []
    for group in range(channels // width):
        span = slice(group * width, (group + 1) * width)
        dq_tiles = []
        dk_tiles = []
        dv_tiles = []
        for tile in range(tiles):
            start = key_start(tile, seq_len)
            asked = slice(tile * QUERY_TILE, (tile + 1) * QUERY_TILE)
            d_context = dc_ref[0, 0, span, asked]
            context = ct_ref[0, 0, span, asked]
            both = d_context.astype(f32) * context.astype(f32)
            spread_dc = block_diagonal(
                [d_context[i * HEAD_DIM : (i + 1) * HEAD_DIM] for i in range(heads)]
            )
            qt = qt_ref[0, 0, span, asked]
            spread_q = block_diagonal(
                [qt[i * HEAD_DIM : (i + 1) * HEAD_DIM] for i in range(heads)]
            )
            d_probs = mm(v_ref[0, 0, group, start : start + window], spread_dc, NN)
            dq_heads = []
            for i in range(heads):
                shared = jnp.sum(both[i * HEAD_DIM : (i + 1) * HEAD_DIM], axis=0, keepdims=True)
                for piece in range(QUERY_TILE // REACH):
                    low, high = live_keys(tile, piece, seq_len)
                    at = i * QUERY_TILE + piece * REACH
                    p = p_ref[0, 0, group, tile, low:high, at : at + REACH].astype(f32)
                    dp = d_probs[low:high, at : at + REACH]
                    ds = (p * (dp - shared[:, piece * REACH : (piece + 1) * REACH])).astype(bf16)
                    ds_ref[:, at : at + REACH] = fill_rows(ds, low, high, window)
                of_head = slice(group * width + i * HEAD_DIM, group * width + (i + 1) * HEAD_DIM)
                dq_heads.append(
                    mm(
                        kt_ref[0, 0, of_head, start : start + window],
                        ds_ref[:, i * QUERY_TILE : (i + 1) * QUERY_TILE],
                        NN,
                    )
                )
            dq_tiles.append(jnp.concatenate(dq_heads, axis=0))
            dk_tiles.append(mm(ds_ref[...], spread_q, NT))
            dv_tiles.append(mm(p_ref[0, 0, group, tile], spread_dc, NT))
        dq = jnp.concatenate(dq_tiles, axis=1).astype(bf16)
        dk = join_windows(dk_tiles, seq_len).astype(bf16)
        dv = join_windows(dv_tiles, seq_len).astype(bf16)
        xtg = xt_ref[0, 0, span]
        grads[0].append(mm(xtg, dq, NT))
        grads[1].append(mm(xtg, dk, NN))
        grads[2].append(mm(xtg, dv, NN))
        wq, wk, wv = (weight(s)[:, span] for s in range(3))
        d_inputs.append(
            dz_ref[0, 0, span] + mm(wq, dq, NN) + mm(wk, dk, NT) + mm(wv, dv, NT)
        )
    joined = [jnp.concatenate(parts, axis=1) for parts in grads]

    @pl.when(row == 0)
    def _():
        for s in range(3):
            grad_ref[s] = joined[s]

    @pl.when(row > 0)
    def _():
        for s in range(3):
            grad_ref[s] += joined[s]

    d_input = jnp.concatenate(d_inputs, axis=0)
    if not last:
        dx_ref[0, 0] = d_input
        return
    tok = d_input.astype(bf16).T
    dx_ref[...] = tok
    full_ref[...] = tok

    @pl.when(step == pl.num_programs(0) - 1)
    def _():
        piece = width // 4
        gain_rows = jnp.concatenate([gain0_ref[...], gain1_ref[...]], axis=0).astype(bf16)
        gain_rows = jnp.concatenate([gain_rows[:, :channels], gain_rows[:, channels:]], axis=0)
        for c, out_ref in enumerate((keep_ref, send_ref)):
            for y in range(2):
                at = ((place[CORE] ^ c) * 2 + (place[ROW] ^ y)) * piece
                at_rows = pl.ds(pl.multiple_of(at, piece), piece)
                for layer, source in enumerate((grad_ref, later_ref.at[0])):
                    for s in range(3):
                        out_ref[y, pl.ds((layer * 3 + s) * piece, piece)] = source[
                            s, at_rows
                        ].astype(bf16)
                out_ref[y, pl.ds(6 * piece, 16)] = gain_rows


def join_windows(pieces, seq_len):
    window = QUERY_TILE + REACH
    rows = []
    for at in range(0, seq_len, REACH):
        held = []
        for tile, piece in enumerate(pieces):
            start = key_start(tile, seq_len)
            if start <= at < start + window:
                held.append(piece[at - start : at - start + REACH])
        rows.append(functools.reduce(jnp.add, held))
    return jnp.concatenate(rows, axis=0)


def feature_mean(values):
    return jnp.sum(values, axis=0, keepdims=True) * (1.0 / values.shape[0])


def normalize(before):
    centered = before - feature_mean(before)
    inverse = lax.rsqrt(feature_mean(centered * centered) + epsilon)
    return centered * inverse, inverse


def normalize_back(gradient, gains, normal, inverse):
    scaled = gradient * gains
    return inverse * (scaled - feature_mean(scaled) - normal * feature_mean(scaled * normal))


def gather_far(place, x_ref, c_ref, scr):
    scr[place[CORE]] = x_ref[...]
    scr[1 - place[CORE]] = c_ref[...]


class Near:
    def __init__(self, out_ref, inner_ref, outer_ref):
        self.refs = out_ref, inner_ref, outer_ref

    def out(self):
        return self.refs[0][0]

    def inner(self, group):
        hidden = self.refs[1].shape[2] // 2
        return self.refs[1][0, :, group * hidden : (group + 1) * hidden]

    def outer(self, group):
        width = self.refs[2].shape[2] // 2
        return self.refs[2][0, :, group * width : (group + 1) * width]


class Far:
    def __init__(self, pack):
        self.pack = pack

    def rows(self, k):
        rows = self.pack[:, k]
        return rows.reshape(2 * rows.shape[1], rows.shape[2])

    def out(self):
        return self.rows(0)

    def inner(self, group):
        return self.pack[group, 1]

    def outer(self, group):
        rows = self.rows(2)
        half = rows.shape[1] // 2
        width = half // 2
        at = group * width
        return jnp.concatenate(
            [rows[:, at : at + width], rows[:, half + at : half + at + width]], axis=0
        )


def spread_gains(gains_ref, layer, g_scr):
    for i in range(2):
        g_scr[i] = across(gains_ref[layer, i : i + 1, :])


def wide_gain(g_scr, i, seq_len):
    return jnp.concatenate([g_scr[i]] * (seq_len // 128), axis=1)


def split(values):
    return values.reshape(2, values.shape[0] // 2, values.shape[1])


def join(values):
    return values.reshape(2 * values.shape[1], values.shape[2])


def up(first, weights, group):
    pre = mm(weights.inner(group), first, TN)
    below = 0.5 + 0.5 * lax.erf(pre * 0.7071067811865476)
    slope = below + pre * (jnp.exp(-0.5 * pre * pre) * 0.3989422804014327)
    return (pre * below).astype(bf16), slope.astype(bf16)


def ffn_kernel(layer, place, *refs):
    (xt_ref, ct_ref, out_ref, inner_ref, outer_ref, farx_ref, farc_ref, gains_ref, *refs) = refs
    (n1_ref, r1_ref, act_ref, slope_ref, n2_ref, r2_ref, tok_ref, next_ref, *refs) = refs
    z_scr, fb_scr, far_scr, g_scr = refs
    half, tokens = z_scr.shape[1:]
    width = half // 2
    sides = (place[SELF], place[OTHER])

    @pl.when(pl.program_id(0) == 0)
    def _():
        gather_far(place, farx_ref, farc_ref, far_scr)
        spread_gains(gains_ref, layer, g_scr)

    weights = (Near(out_ref, inner_ref, outer_ref), Far(far_scr))
    z_scr[...] = split(sum(mm(weights[j].out(), ct_ref[j, 0], TN) for j in range(2)))
    for j in range(2):
        z_scr[sides[j]] += xt_ref[j, 0].astype(f32)
    normal, inverse = normalize(join(z_scr[...]))
    n1_ref[0] = split(normal.astype(bf16))
    r1_ref[0] = inverse
    first = normal * wide_gain(g_scr, 0, tokens)
    z_scr[...] = split(first)
    fb_scr[...] = split(first.astype(bf16))
    for j in range(2):
        for group in range(2):
            span = slice(group * width, (group + 1) * width)
            act, slope = up(fb_scr[sides[j], span], weights[j], group)
            act_ref[0, j, group] = act
            slope_ref[0, j, group] = slope
            z_scr[sides[j], span] += mm(weights[j].outer(group), act, TN)
    normal, inverse = normalize(join(z_scr[...]))
    n2_ref[0] = split(normal.astype(bf16))
    r2_ref[0] = inverse
    output = normal * wide_gain(g_scr, 1, tokens)
    tok_ref[...] = output.astype(bf16).T
    next_ref[0] = split(output)


def down(place, weights, acc, d_scr, b_scr, f_scr, act_of, slope_of):
    half = d_scr.shape[1]
    width = half // 2
    sides = (place[SELF], place[OTHER])
    for j in range(2):
        outers = []
        for group in range(2):
            span = slice(group * width, (group + 1) * width)
            d_branch = b_scr[sides[j], span]
            outers.append(mm(act_of(j, group), d_branch, NT))
            d_act = mm(weights[j].outer(group), d_branch, NN)
            d_pre = (d_act * slope_of(j, group).astype(f32)).astype(bf16)
            acc[j, 1, span] += mm(f_scr[sides[j], span], d_pre, NT)
            d_scr[sides[j], span] += mm(weights[j].inner(group), d_pre, NN)
        acc[j, 2] += jnp.concatenate(
            [o[:half] for o in outers] + [o[half:] for o in outers], axis=1
        )


def into_attention(d_before, weights, acc, ct_ref, dc_ref):
    d_attention = d_before.astype(bf16)
    for j in range(2):
        acc[j, 0] += mm(ct_ref[j, 0], d_attention, NT)
        dc_ref[j, 0] = mm(weights[j].out(), d_attention, NN).astype(bf16)


def hand_out(place, acc, keep_ref, send_ref):
    piece = acc.shape[2] // 8
    for c, out_ref in enumerate((keep_ref, send_ref)):
        for s in range(2):
            for j in range(2):
                for y in range(2):
                    at = ((s * 2 + (place[CORE] ^ c)) * 2 + (place[ROW] ^ y)) * piece
                    rows = pl.ds(pl.multiple_of(at, piece), piece)
                    spot = j, y, s
                    for k in range(3):
                        out_ref[(*spot, k)] = acc[j, k, rows].astype(bf16)


def hand_out_gains(gain_acc, gain_ref):
    sums = [jnp.sum(gain_acc[i], axis=1, keepdims=True) for i in range(2)]
    lane = lax.broadcasted_iota(jnp.int32, gain_acc.shape[1:], 1)
    gain_ref[...] = jnp.where(lane == 0, sums[0], sums[1]).T[:4]


def ffn_last_kernel(layer, place, *refs):
    (x_ref, ct_ref, cot_ref, out_ref, inner_ref, outer_ref, *refs) = refs
    (farx_ref, farc_ref, gains_ref, tok_ref, full_ref, *refs) = refs
    (dz1_ref, dc_ref, keep_ref, send_ref, gain_ref, *refs) = refs
    (z_scr, fb_scr, b_scr, n_scr, act_scr, slope_scr, far_scr, g_scr, acc, gain_acc) = refs
    half, tokens = z_scr.shape[1:]
    width = half // 2
    sides = (place[SELF], place[OTHER])
    step = pl.program_id(0)

    @pl.when(step == 0)
    def _():
        gather_far(place, farx_ref, farc_ref, far_scr)
        spread_gains(gains_ref, layer, g_scr)
        acc[...] = jnp.zeros_like(acc)
        gain_acc[...] = jnp.zeros_like(gain_acc)

    weights = (Near(out_ref, inner_ref, outer_ref), Far(far_scr))
    attention = sum(mm(weights[j].out(), ct_ref[j, 0], TN) for j in range(2))
    normal, inverse1 = normalize(attention + join(x_ref[0]))
    n_scr[...] = normal
    first = normal * wide_gain(g_scr, 0, tokens)
    z_scr[...] = split(first)
    fb_scr[...] = split(first.astype(bf16))
    for j in range(2):
        for group in range(2):
            span = slice(group * width, (group + 1) * width)
            act, slope = up(fb_scr[sides[j], span], weights[j], group)
            act_scr[j, group] = act
            slope_scr[j, group] = slope
            z_scr[sides[j], span] += mm(weights[j].outer(group), act, TN)
    normal, inverse = normalize(join(z_scr[...]))
    gain = wide_gain(g_scr, 1, tokens)
    tok = (normal * gain).astype(bf16).T
    tok_ref[...] = tok
    full_ref[...] = tok

    g = cot_ref[...].T.astype(f32)
    gain_acc[1] += lane_sum(g * normal)
    d_second = normalize_back(g, gain, normal, inverse)
    z_scr[...] = split(d_second)
    b_scr[...] = split(d_second.astype(bf16))
    down(
        place,
        weights,
        acc,
        z_scr,
        b_scr,
        fb_scr,
        lambda j, group: act_scr[j, group],
        lambda j, group: slope_scr[j, group],
    )
    d_first = join(z_scr[...])
    normal = n_scr[...]
    gain_acc[0] += lane_sum(d_first * normal)
    d_before = normalize_back(d_first, wide_gain(g_scr, 0, tokens), normal, inverse1)
    dz1_ref[0] = split(d_before)
    into_attention(d_before, weights, acc, ct_ref, dc_ref)

    @pl.when(step == pl.num_programs(0) - 1)
    def _():
        hand_out(place, acc, keep_ref, send_ref)
        hand_out_gains(gain_acc, gain_ref)


def ffn_back_kernel(layer, place, *refs):
    (g_ref, n2_ref, r2_ref, act_ref, slope_ref, n1_ref, r1_ref, ct_ref, *refs) = refs
    (out_ref, inner_ref, outer_ref, farx_ref, farc_ref, gains_ref, *refs) = refs
    (dz1_ref, dc_ref, keep_ref, send_ref, gain_ref, *refs) = refs
    d_scr, b_scr, f_scr, far_scr, g_scr, acc, gain_acc = refs
    tokens = d_scr.shape[2]
    sides = (place[SELF], place[OTHER])
    step = pl.program_id(0)

    @pl.when(step == 0)
    def _():
        gather_far(place, farx_ref, farc_ref, far_scr)
        spread_gains(gains_ref, layer, g_scr)
        acc[...] = jnp.zeros_like(acc)
        gain_acc[...] = jnp.zeros_like(gain_acc)

    weights = (Near(out_ref, inner_ref, outer_ref), Far(far_scr))
    for j in range(2):
        d_scr[sides[j]] = g_ref[j, 0]
    g = join(d_scr[...])
    normal = join(n2_ref[0]).astype(f32)
    gain_acc[1] += lane_sum(g * normal)
    d_second = normalize_back(g, wide_gain(g_scr, 1, tokens), normal, r2_ref[0])
    d_scr[...] = split(d_second)
    b_scr[...] = split(d_second.astype(bf16))
    normal = join(n1_ref[0]).astype(f32)
    gain = wide_gain(g_scr, 0, tokens)
    f_scr[...] = split((normal * gain).astype(bf16))
    down(
        place,
        weights,
        acc,
        d_scr,
        b_scr,
        f_scr,
        lambda j, group: act_ref[0, j, group],
        lambda j, group: slope_ref[0, j, group],
    )
    d_first = join(d_scr[...])
    gain_acc[0] += lane_sum(d_first * normal)
    d_before = normalize_back(d_first, gain, normal, r1_ref[0])
    dz1_ref[0] = split(d_before)
    into_attention(d_before, weights, acc, ct_ref, dc_ref)

    @pl.when(step == pl.num_programs(0) - 1)
    def _():
        hand_out(place, acc, keep_ref, send_ref)
        hand_out_gains(gain_acc, gain_ref)


def lane_sum(values):
    chunks = [values[:, at : at + 128] for at in range(0, values.shape[1], 128)]
    return functools.reduce(jnp.add, chunks)


def placed_pieces(place, parts, size):
    mine, row, core = parts
    for c, y, value in ((0, 0, mine[...]), (0, 1, row[...]), (1, 0, core[0]), (1, 1, core[1])):
        yield ((place[CORE] ^ c) * 2 + (place[ROW] ^ y)) * size, value


def rows_at(at, size):
    return pl.ds(pl.multiple_of(at, size), size)


def finish_ffn_kernel(place, *refs):
    out_ref, inner_ref, outer_ref = refs[-3:]
    half, wide = out_ref.shape[1:]
    size = half // 8
    for at, value in placed_pieces(place, refs[:3], size):
        value = value.astype(f32)
        for s in range(2):
            low = s * (half // 2) + at
            out_ref[0, rows_at(low, size), :] = value[s, 0]
            inner_ref[0, rows_at(at, size), s * wide : (s + 1) * wide] = value[s, 1]
            outer_ref[0, rows_at(low, size), :] = value[s, 2][:, :half]
            outer_ref[0, rows_at(half + low, size), :] = value[s, 2][:, half:]


def finish_qkv_kernel(place, mine, row, core, qkv_ref, gain_ref):
    half = qkv_ref.shape[3]
    size = qkv_ref.shape[2] // 4
    for at, value in placed_pieces(place, (mine, row, core), size):
        for layer in range(2):
            for s in range(3):
                index = (layer * 3 + s) * size
                qkv_ref[layer, s, rows_at(at, size), :] = value[index : index + size].astype(f32)
    gains = mine[6 * size : 6 * size + 16].astype(f32)
    for layer in range(2):
        for i in range(2):
            at = layer * 4 + i
            gain_ref[layer, i : i + 1, :half] = gains[at : at + 1]
            gain_ref[layer, i : i + 1, half:] = gains[8 + at : 9 + at]


def pack_kernel(place, out_ref, inner_ref, low_ref, high_ref, qkv_ref, piece_ref, part_ref):
    half = low_ref.shape[2]
    piece_ref[0] = out_ref[0]
    piece_ref[1] = inner_ref[0]
    piece_ref[2, :, :half] = low_ref[0]
    piece_ref[2, :, half:] = high_ref[0]
    part_ref[...] = qkv_ref[0]


def whole(shape):
    return pl.BlockSpec(shape, lambda r, place: (0,) * len(shape))


def per_row(shape):
    rest = (0,) * (len(shape) - 1)
    return pl.BlockSpec((1,) + tuple(shape[1:]), lambda r, place: (r,) + rest)


def struct(shape, dtype):
    return jax.ShapeDtypeStruct(shape, dtype)


def call(
    kernel, rows, place, operands, in_specs, outs, out_specs, scratch, name, us, aliases=None, after=()
):
    count = len(operands)
    in_specs = list(in_specs) + [pl.BlockSpec(memory_space=pl.ANY)] * len(after)
    operands = tuple(operands) + tuple(after)

    def body(place, *refs):
        kernel(place, *refs[:count], *refs[count + len(after) :])

    results = pl.pallas_call(
        body,
        out_shape=outs,
        grid_spec=pltpu.PrefetchScalarGridSpec(
            num_scalar_prefetch=1,
            grid=(rows,),
            in_specs=in_specs,
            out_specs=out_specs,
            scratch_shapes=scratch,
        ),
        compiler_params=pltpu.CompilerParams(vmem_limit_bytes=64 * 2**20 - 2**16),
        cost_estimate=pl.CostEstimate(
            flops=int(us * 5e9), bytes_accessed=int(us * 1e7), transcendentals=0
        ),
        input_output_aliases=aliases or {},
        name=name,
    )(place, *operands)
    return list(results)


def per_side(shape, side):
    rest = (0,) * (len(shape) - 2)
    return pl.BlockSpec((1, 1) + tuple(shape[2:]), lambda r, place: (side, r) + rest)


def both_sides(shape, parts=1):
    middle = (0,) * (len(shape) - 3)
    return pl.BlockSpec(
        (2, 1) + tuple(shape[2:-1]) + (shape[-1] // parts,),
        lambda t, place: (0, t // parts, *middle, t % parts),
    )


def attend(x_tok, w, segments, place, rows, j, layer, us, held=(), after=()):
    row_total, seq_len = segments.shape
    far = j == 1
    channels = w[0].shape[-1]
    width = channels // 2
    heads = width // HEAD_DIM
    groups = channels // width
    tiles = seq_len // QUERY_TILE
    window = QUERY_TILE + REACH
    outs = [
        struct((2, rows, channels, seq_len), bf16),
        struct((2, rows, channels, seq_len), bf16),
        struct((2, rows, channels, seq_len), bf16),
        struct((2, rows, groups, seq_len, width), bf16),
        struct((2, rows, groups, tiles, window, heads * QUERY_TILE), bf16),
        struct((2, rows, channels, seq_len), bf16),
    ]
    if layer == 0:
        x_spec = pl.BlockSpec((seq_len, channels), lambda r, place: (place[OFFSET] + r, place[j]))
    else:
        x_spec = pl.BlockSpec((seq_len, channels), lambda r, place: (r, place[j]))
    operands = (x_tok, *w, segments)
    return call(
        functools.partial(attend_kernel, far),
        rows,
        place,
        operands + tuple(held),
        [x_spec, *weight_blocks(w, far, layer), whole(segments.shape)]
        + [pl.BlockSpec(memory_space=pl.ANY)] * len(held),
        outs,
        [per_side(o.shape, j) for o in outs],
        weight_scratch(w, far),
        "attend",
        us,
        {len(operands) + 1 + i: i for i in range(len(held))},
        after,
    )


def weight_blocks(w, far, layer):
    return [whole(o.shape) for o in w] if far else [layer_block(w[0].shape, layer)]


def weight_scratch(w, far):
    if not far:
        return []
    three, depth, channels = w[0].shape
    return [pltpu.VMEM((three, 2, depth, channels), bf16)]


def layer_block(shape, layer):
    rest = (0,) * (len(shape) - 1)
    return pl.BlockSpec((None,) + tuple(shape[1:]), lambda r, place: (layer,) + rest)


def attend_back(d_context, saved, w, d_before, place, rows, sides, layer, extra, us, after=()):
    xt, qt, kt, values, probs, ct = saved
    channels, seq_len = xt.shape[2:]
    window = QUERY_TILE + REACH
    width = values.shape[-1]
    heads = width // HEAD_DIM
    operands = (d_context, ct, probs, qt, kt, values, xt)
    scratch = [pltpu.VMEM((window, heads * QUERY_TILE), bf16)]
    grad = (3, width, channels)
    if len(sides) == 2:
        near, *far = w
        w_specs = [layer_block4(near.shape, layer)] + [whole(o.shape) for o in far]
        scratch += [pltpu.VMEM((2, 3, 2, width // 2, channels), bf16)]
    else:
        w_specs = weight_blocks(w, sides[0] == 1, layer)
        scratch += weight_scratch(w, sides[0] == 1)

    def side(t):
        return t // rows if len(sides) == 2 else sides[0]

    def one(shape):
        rest = (0,) * (len(shape) - 2)
        return pl.BlockSpec(
            (1, 1) + tuple(shape[2:]), lambda t, place: (side(t), t % rows) + rest
        )

    in_specs = [one(o.shape) for o in operands] + [
        pl.BlockSpec(
            (1, 1, channels, seq_len), lambda t, place: (t % rows, place[side(t)], 0, 0)
        ),
        *w_specs,
    ]
    operands += (d_before, *w)
    aliases = {}
    if extra is None:
        outs = [struct((2, rows, channels, seq_len), f32), struct((2,) + grad, f32)]
        out_specs = [
            one(outs[0].shape),
            pl.BlockSpec((1,) + grad, lambda t, place: (side(t), 0, 0, 0)),
        ]
    else:
        later, gain0, gain1, full = extra
        operands += (later, gain0, gain1)
        in_specs += [one_layer(later.shape, sides[0]), whole(gain0.shape), whole(gain1.shape)]
        if full is not None:
            aliases = {len(operands) + 1: 1}
            operands += (full,)
            in_specs.append(pl.BlockSpec(memory_space=pl.ANY))
        piece = struct((2, 6 * (width // 4) + 16, channels), bf16)
        outs = [
            struct((rows * seq_len, channels), bf16),
            struct((2 * rows * seq_len, 2 * channels), bf16),
            piece,
            piece,
        ]
        out_specs = [
            pl.BlockSpec((seq_len, channels), lambda r, place: (r, 0)),
            pl.BlockSpec(
                (seq_len, channels), lambda r, place: (place[OFFSET] + r, place[sides[0]])
            ),
            whole(piece.shape),
            whole(piece.shape),
        ]
        scratch = [pltpu.VMEM(grad, f32)] + scratch
    return call(
        functools.partial(attend_back_kernel, extra is not None, bool(aliases), sides, rows),
        len(sides) * rows,
        place,
        operands,
        in_specs,
        outs,
        out_specs,
        scratch,
        "attend_back",
        us,
        aliases,
        after,
    )


def layer_block4(shape, layer):
    rest = (0,) * (len(shape) - 1)
    return pl.BlockSpec((1,) + tuple(shape[1:]), lambda t, place: (layer,) + rest)


def per_part(shape, parts):
    middle = (0,) * (len(shape) - 2)
    return pl.BlockSpec(
        (1,) + tuple(shape[1:-1]) + (shape[-1] // parts,),
        lambda t, place: (t // parts, *middle, t % parts),
    )


def weight_specs(weights, layer):
    return [one_layer(o.shape, layer) for o in weights[:3]] + [whole(o.shape) for o in weights[3:]]


def ffn(xts, contexts, weights, gains, place, rows, layer, us):
    half, seq_len = contexts.shape[2:]
    parts = 1
    tokens = seq_len // parts
    stream = (rows, 2, half, seq_len)
    acts = (rows, 2, 2, 2 * half, seq_len)
    outs = [
        struct(stream, bf16),
        struct((rows, 1, seq_len), f32),
        struct(acts, bf16),
        struct(acts, bf16),
        struct(stream, bf16),
        struct((rows, 1, seq_len), f32),
        struct((rows * seq_len, 2 * half), bf16),
        struct(stream, f32),
    ]
    out_specs = [per_part(o.shape, parts) for o in outs]
    out_specs[6] = pl.BlockSpec((tokens, 2 * half), lambda t, place: (t, 0))
    return call(
        functools.partial(ffn_kernel, layer),
        rows * parts,
        place,
        (xts, contexts, *weights, gains),
        [both_sides(xts.shape, parts), both_sides(contexts.shape, parts)]
        + weight_specs(weights, layer)
        + [whole(gains.shape)],
        outs,
        out_specs,
        [
            pltpu.VMEM((2, half, tokens), f32),
            pltpu.VMEM((2, half, tokens), bf16),
            pltpu.VMEM((2,) + weights[3].shape, bf16),
            pltpu.VMEM((2, 2 * half, 128), f32),
        ],
        "ffn",
        us,
    )


def sum_shapes(half):
    piece = struct((2, 2, 2, 3, half // 8, 2 * half), bf16)
    return [piece, piece, struct((4, 2 * half), f32)]


def sum_scratch(weights, half):
    return [
        pltpu.VMEM((2,) + weights[3].shape, bf16),
        pltpu.VMEM((2, 2 * half, 128), f32),
        pltpu.VMEM((2, 3, half, 2 * half), f32),
        pltpu.VMEM((2, 2 * half, 128), f32),
    ]


def ffn_last(x, contexts, cotangent, weights, gains, place, rows, layer, us):
    half, seq_len = contexts.shape[2:]
    wide = 2 * half
    outs = [
        struct((rows * seq_len, wide), bf16),
        struct((2 * rows * seq_len, wide), bf16),
        struct((rows, 2, half, seq_len), f32),
        struct(contexts.shape, bf16),
        *sum_shapes(half),
    ]
    own = pl.BlockSpec((seq_len, wide), lambda r, place: (place[OFFSET] + r, 0))
    out_specs = (
        [pl.BlockSpec((seq_len, wide), lambda r, place: (r, 0)), own]
        + [per_row(outs[2].shape), both_sides(outs[3].shape)]
        + [whole(o.shape) for o in outs[4:]]
    )
    stream = (2, half, seq_len)
    acts = (2, 2, wide, seq_len)
    return call(
        functools.partial(ffn_last_kernel, layer),
        rows,
        place,
        (x, contexts, cotangent, *weights, gains),
        [per_row(x.shape), both_sides(contexts.shape), own]
        + weight_specs(weights, layer)
        + [whole(gains.shape)],
        outs,
        out_specs,
        [
            pltpu.VMEM(stream, f32),
            pltpu.VMEM(stream, bf16),
            pltpu.VMEM(stream, bf16),
            pltpu.VMEM((wide, seq_len), f32),
            pltpu.VMEM(acts, bf16),
            pltpu.VMEM(acts, bf16),
            *sum_scratch(weights, half),
        ],
        "ffn_last",
        us,
    )


def ffn_back(g, saved, contexts, weights, gains, place, rows, layer, us, after=()):
    half, seq_len = contexts.shape[2:]
    stream = (2, half, seq_len)
    outs = [
        struct((rows,) + stream, f32),
        struct(contexts.shape, bf16),
        *sum_shapes(half),
    ]
    out_specs = [per_row(outs[0].shape), both_sides(outs[1].shape)] + [
        whole(o.shape) for o in outs[2:]
    ]
    return call(
        functools.partial(ffn_back_kernel, layer),
        rows,
        place,
        (g, *saved, contexts, *weights, gains),
        [both_sides(g.shape)]
        + [per_row(o.shape) for o in saved]
        + [both_sides(contexts.shape)]
        + weight_specs(weights, layer)
        + [whole(gains.shape)],
        outs,
        out_specs,
        [
            pltpu.VMEM(stream, f32),
            pltpu.VMEM(stream, bf16),
            pltpu.VMEM(stream, bf16),
            *sum_scratch(weights, half),
        ],
        "ffn_back",
        us,
        after=after,
    )


def one_layer(shape, layer):
    rest = (0,) * (len(shape) - 1)
    return pl.BlockSpec((1,) + tuple(shape[1:]), lambda r, place: (layer,) + rest)


def finish_ffn(parts, place, layer, layers, held=()):
    operands = list(parts)
    half = operands[0].shape[-1] // 2
    outs = [
        struct((layers, half, 2 * half), f32),
        struct((layers, half // 2, 4 * half), f32),
        struct((layers, 2 * half, half), f32),
    ]
    return call(
        finish_ffn_kernel,
        1,
        place,
        operands + list(held),
        [whole(o.shape) for o in operands] + [pl.BlockSpec(memory_space=pl.ANY)] * len(held),
        outs,
        [one_layer(o.shape, layer) for o in outs],
        [],
        "finish_ffn",
        3,
        {4 + i: i for i in range(len(held))},
    )


def finish_qkv(parts, place, layers, width):
    half = parts[0].shape[-1]
    outs = [struct((layers, 3, width, half), f32), struct((layers, 2, 2 * half), f32)]
    return call(
        finish_qkv_kernel,
        1,
        place,
        parts,
        [whole(o.shape) for o in parts],
        outs,
        [whole(o.shape) for o in outs],
        [],
        "finish_qkv",
        3,
    )


def pack(weights, place, layer, after=()):
    out_w, inner_w, outer_w, qkv_w = weights
    half, wide = out_w.shape[1:]
    three, depth, channels = qkv_w.shape[1:]
    rows = half // 2
    outs = [struct((3, rows, wide), bf16), struct((three, depth // 2, channels), bf16)]
    return call(
        pack_kernel,
        1,
        place,
        (out_w, inner_w, outer_w, outer_w, qkv_w),
        [
            pl.BlockSpec((1, rows, wide), lambda r, place: (layer, place[CORE], 0)),
            pl.BlockSpec((1, depth, wide), lambda r, place: (layer, 0, place[CORE])),
            pl.BlockSpec((1, rows, half), lambda r, place: (layer, place[CORE], 0)),
            pl.BlockSpec((1, rows, half), lambda r, place: (layer, 2 + place[CORE], 0)),
            pl.BlockSpec((1, three, depth // 2, channels), lambda r, place: (layer, 0, place[CORE], 0)),
        ],
        outs,
        [whole(o.shape) for o in outs],
        [],
        "pack",
        3,
        after=after,
    )


def hold(values, place, after):
    anywhere = pl.BlockSpec(memory_space=pl.ANY)
    return call(
        lambda place, *refs: None,
        1,
        place,
        values,
        [anywhere] * len(values),
        [struct(v.shape, v.dtype) for v in values],
        [anywhere] * len(values),
        [],
        "hold",
        1,
        {i + 1: i for i in range(len(values))},
        after,
    )


def fill_input_kernel(place, full_ref, own_ref, far_ref, out_ref):
    column = pl.program_id(0)

    @pl.when(column == 0)
    def _():
        out_ref[...] = own_ref[...]

    @pl.when(column == 1)
    def _():
        out_ref[...] = far_ref[...]


def fill_input(full, from_own, from_far, place, rows, seq_len):
    half = from_own.shape[1]
    count = rows * seq_len
    block = pl.BlockSpec((count, half), lambda j, place: (0, 0))
    return pl.pallas_call(
        fill_input_kernel,
        out_shape=struct(full.shape, full.dtype),
        grid_spec=pltpu.PrefetchScalarGridSpec(
            num_scalar_prefetch=1,
            grid=(2,),
            in_specs=[pl.BlockSpec(memory_space=pl.ANY), block, block],
            out_specs=pl.BlockSpec(
                (count, half), lambda j, place: (place[OTHER], (1 - place[SELF]) ^ j)
            ),
        ),
        input_output_aliases={1: 0},
        name="fill_input",
    )(place, full, from_own, from_far)


def swap(values):
    return lax.ppermute(values, "head", [(0, 1), (1, 0)])


def cross(values):
    count = lax.axis_size("dp")
    return lax.ppermute(
        values, ("dp", "head"), [(2 * a + h, 2 * (a ^ 2) + 1 - h) for a in range(count) for h in range(2)]
    )


def scatter(parts):
    return [swap(parts[0]), trade(parts[1], 2), cross(parts[2])]


SHARES = ((1, 0), (0, 1), (1, 1))


def trade(values, stride):
    count = lax.axis_size("dp")
    return lax.ppermute(values, "dp", [(a, a ^ stride) for a in range(count)])


def far_strides():
    count = lax.axis_size("dp")
    strides = []
    stride = 4
    while stride < count:
        strides.append(stride)
        stride *= 2
    return strides


def sums(groups, place, after=(), casts=None):
    operands = []
    plan = []
    for group in groups:
        terms = []
        for term in group:
            value, *index = term if isinstance(term, tuple) else (term,)
            terms.append((len(operands), tuple(index)))
            operands.append(value)
        plan.append(terms)
    outs = [
        struct(operands[terms[0][0]].shape[len(terms[0][1]) :], operands[terms[0][0]].dtype)
        for terms in plan
    ]

    def kernel(place, *refs):
        for terms, out in zip(plan, refs[len(operands) :]):
            out[...] = functools.reduce(
                jnp.add, [refs[at][...].astype(f32) for at, _ in terms]
            ).astype(out.dtype)

    def spec(value, index):
        shape = value.shape[len(index) :]
        return pl.BlockSpec(
            (None,) * len(index) + tuple(shape),
            lambda r, place: tuple(index) + (0,) * len(shape),
        )

    return call(
        kernel,
        1,
        place,
        operands,
        [spec(operands[at], index) for terms in plan for at, index in terms],
        outs,
        [whole(o.shape) for o in outs],
        [],
        "sums",
        2,
        after=after,
    )


def add(*terms):
    return functools.reduce(jnp.add, [t.astype(f32) for t in terms]).astype(bf16)


def shards(
    tokens, segments, qkv_weight, out_weight, inner_weight, outer_weight, norm_gains, cotangent
):
    side = lax.axis_index("head").astype(jnp.int32)
    spot = lax.axis_index("dp").astype(jnp.int32)
    layers = qkv_weight.shape[0]
    row_total, seq_len = segments.shape
    rows = row_total // 2
    width = qkv_weight.shape[2]
    place = jnp.stack([side, 1 - side, side * rows, spot & 1, (spot >> 1) & 1])
    weights = (out_weight, inner_weight, outer_weight)
    one = (qkv_weight,)
    far_qkv = [None, None]
    ffn_weights = [None, None]

    piece, part = pack((*weights, qkv_weight), place, 0)
    part, piece = swap(part), swap(piece)
    near = attend(tokens, one, segments, place, rows, 0, 0, 9)
    (part,) = hold([part], place, [near[5]])
    far_qkv[0] = (part, trade(part, 1))
    next_piece, next_part = pack((*weights, qkv_weight), place, 1, [near[5]])
    held = attend(tokens, far_qkv[0], segments, place, rows, 1, 0, 0.2, near, [next_piece])
    piece, next_piece, next_part = hold([piece, next_piece, next_part], place, [held[5]])
    ffn_weights[0] = (*weights, piece, trade(piece, 1))
    part, piece = swap(next_part), swap(next_piece)
    ffn_weights[1] = (*weights, piece, trade(piece, 1))
    saved_attend = [held]
    n1, r1, act, slope, n2, r2, x_tok, x_stream = ffn(
        held[0], held[5], ffn_weights[0], norm_gains, place, rows, 0, 20
    )
    saved_ffn = (n2, r2, act, slope, n1, r1)
    (part,) = hold([part], place, [x_tok])
    far_qkv[1] = (part, trade(part, 1))
    near = attend(x_tok, one, segments, place, rows, 0, 1, 9)
    held = attend(x_tok, far_qkv[1], segments, place, rows, 1, 1, 9, near)
    saved_attend.append(held)
    x_tok, activations, d_before, d_context, keep, send, gain1 = ffn_last(
        x_stream, held[5], cotangent, ffn_weights[1], norm_gains, place, rows, 1, 40
    )

    strides = far_strides()
    far_tok = swap(x_tok)
    got = trade(send, 1)
    dx, later = attend_back(
        d_context, held, one + far_qkv[1], d_before, place, rows, (0, 1), 1, None, 0.2
    )
    parts = sums([[(keep, *at), (got, *at)] for at in SHARES], place, [dx])
    crossed = scatter(parts)
    d_before, d_context, next_keep, next_send, gain0 = ffn_back(
        dx, saved_ffn, saved_attend[0][5], ffn_weights[0], norm_gains, place, rows, 0, 0.2, parts
    )
    (late,) = sums([[(keep, 0, 0), (got, 0, 0), *crossed]], place, [d_before])
    late_got = trade(late, strides[0])
    keep, send = next_keep, next_send
    got = trade(send, 1)
    dx1, full, keep1, send1 = attend_back(
        d_context,
        saved_attend[0],
        far_qkv[0],
        d_before,
        place,
        rows,
        (1,),
        0,
        (later, gain0, gain1, None),
        13,
        [late, far_tok],
    )
    core1 = trade(send1, 1)
    *parts, late = sums(
        [[(keep, *at), (got, *at)] for at in SHARES] + [[late, late_got]], place, [dx1]
    )
    crossed = scatter(parts)
    late_got = trade(late, strides[1])
    dx0, full, keep0, send0 = attend_back(
        d_context,
        saved_attend[0],
        one,
        d_before,
        place,
        rows,
        (0,),
        0,
        (later, gain0, gain1, full),
        13,
        parts + [late],
    )
    core0 = trade(send0, 1)
    (core1,) = hold([core1], place, [dx0])
    shares = [add(keep1[0], core1[0]), add(keep0[1], core0[1]), add(keep1[1], core1[1])]
    shares = scatter(shares)
    total = add(keep0[0], core0[0], *shares)
    early = [add(keep[0, 0, s], got[0, 0, s], *[c[s] for c in crossed]) for s in range(2)]
    orders = (strides, strides[::-1])
    late = add(late, late_got)
    for stride in strides[2:]:
        late = add(late, trade(late, stride))
    late_row = trade(late, 2)
    late_core = trade(jnp.stack([late, late_row]), 1)
    dx0, dx1 = hold([dx0, dx1], place, early)
    far_dx0, far_dx1 = swap(dx0), swap(dx1)
    for at in range(len(strides)):
        early = [add(early[s], trade(early[s], orders[s][at])) for s in range(2)]
        total = add(total, trade(total, strides[at]))
    early = jnp.stack(early)
    grads = finish_ffn([late, late_row, late_core], place, 1, layers)
    early_row = trade(early, 2)
    row = trade(total, 2)
    input_grad = fill_input(full, far_dx0, far_dx1, place, rows, seq_len)
    both = jnp.stack([early, early_row])
    (both,) = hold([both], place, [input_grad, grads[0]])
    early_core = trade(both, 1)
    core_part = trade(jnp.stack([total, row]), 1)
    other_rows = (1 - side) * rows * seq_len
    activations = lax.dynamic_update_slice(activations, far_tok, (other_rows, jnp.int32(0)))
    out_grad, inner_grad, outer_grad = finish_ffn(
        [early, early_row, early_core], place, 0, layers, grads
    )
    qkv_grad, gain_grad = finish_qkv([total, row, core_part], place, layers, width)
    return (activations, input_grad, qkv_grad, out_grad, inner_grad, outer_grad, gain_grad)


def solution(mesh):
    return jax.shard_map(
        shards,
        mesh=mesh,
        in_specs=(
            P("dp", None),
            P("dp", None),
            P(None, None, None, "head"),
            P(None, "head", None),
            P(None, None, "head"),
            P(None, None, "head"),
            P(),
            P("dp", None),
        ),
        out_specs=(
            P("dp", None),
            P("dp", None),
            P(None, None, None, "head"),
            P(None, "head", None),
            P(None, None, "head"),
            P(None, None, "head"),
            P(),
        ),
        check_vma=False,
    )
```

```python
import functools
import jax
import jax.numpy as jnp
from jax import lax
from jax.experimental import pallas as pl
from jax.experimental.pallas import tpu as pltpu
from jax.sharding import PartitionSpec as P

HEAD_DIM = 64
QUERY_TILE = 256
REACH = 128

SELF, OTHER, OFFSET, CORE, ROW = range(5)

epsilon = 1e-12
masked_score = -1e30
f32 = jnp.float32
bf16 = jnp.bfloat16

NN = (((1,), (0,)), ((), ()))
NT = (((1,), (1,)), ((), ()))
TN = (((0,), (0,)), ((), ()))


def mm(left, right, dims):
    return lax.dot_general(left, right, dims, preferred_element_type=f32)


def key_start(tile, seq_len):
    return min(max(tile * QUERY_TILE - REACH, 0), seq_len - QUERY_TILE - REACH)


def live_keys(tile, piece, seq_len):
    window = QUERY_TILE + REACH
    first_query = tile * QUERY_TILE + piece * REACH
    start = key_start(tile, seq_len)
    low = max(first_query - REACH - start, 0)
    high = min(first_query + 2 * REACH - start, window)
    return low, high


def block_diagonal(parts):
    rows = []
    for index, part in enumerate(parts):
        empty = jnp.zeros_like(part)
        rows.append(
            jnp.concatenate([part if at == index else empty for at in range(len(parts))], axis=1)
        )
    return jnp.concatenate(rows, axis=0)


def fill_rows(middle, low, high, total):
    pieces = []
    if low > 0:
        pieces.append(jnp.zeros((low, middle.shape[1]), middle.dtype))
    pieces.append(middle)
    if high < total:
        pieces.append(jnp.zeros((total - high, middle.shape[1]), middle.dtype))
    return jnp.concatenate(pieces, axis=0) if len(pieces) > 1 else middle


def across(row):
    return jnp.broadcast_to(row, (128, row.shape[1])).T


def take_weights(place, far, refs):
    if not far:
        return (lambda s: refs[0][s]), refs[1:]
    crossed, traded, *refs = refs
    scr = refs.pop()

    @pl.when(pl.program_id(0) == 0)
    def _():
        scr[:, place[CORE]] = crossed[...]
        scr[:, 1 - place[CORE]] = traded[...]

    return (lambda s: scr[s].reshape(2 * scr.shape[2], scr.shape[3])), refs


def attend_kernel(far, place, x_ref, *refs):
    weight, refs = take_weights(place, far, refs)
    seg_ref, *refs = refs
    xt_ref, qt_ref, kt_ref, v_ref, p_ref, ct_ref = refs[-6:]
    seq_len, channels = x_ref.shape
    width = v_ref.shape[-1]
    window = QUERY_TILE + REACH
    heads = width // HEAD_DIM
    tiles = seq_len // QUERY_TILE
    x = x_ref[...]
    xt = x.T
    xt_ref[0, 0] = xt
    segq = seg_ref[pl.ds(place[OFFSET] + pl.program_id(0), 1), :].astype(f32)
    segk = across(segq)
    masks = {}
    for tile in range(tiles):
        start = key_start(tile, seq_len)
        for piece in range(QUERY_TILE // REACH):
            low, high = live_keys(tile, piece, seq_len)
            at = tile * QUERY_TILE + piece * REACH
            same = segk[start + low : start + high] == segq[:, at : at + REACH]
            masks[tile, piece] = jnp.where(same, 0.0, masked_score)
    for group in range(channels // width):
        span = slice(group * width, (group + 1) * width)
        xg = x[:, span]
        xtg = xt[span]
        wq, wk, wv = (weight(s)[:, span] for s in range(3))
        qt = mm(wq, xtg, TN).astype(bf16) * jnp.asarray(HEAD_DIM**-0.5, bf16)
        kt = mm(wk, xtg, TN).astype(bf16)
        vt = mm(wv, xtg, TN).astype(bf16)
        keys = mm(xg, wk, NN).astype(bf16)
        values = mm(xg, wv, NN).astype(bf16)
        qt_ref[0, 0, span] = qt
        kt_ref[0, 0, span] = kt * jnp.asarray(HEAD_DIM**-0.5, bf16)
        v_ref[0, 0, group] = values
        for tile in range(tiles):
            start = key_start(tile, seq_len)
            asked = slice(tile * QUERY_TILE, (tile + 1) * QUERY_TILE)
            spread = block_diagonal(
                [qt[i * HEAD_DIM : (i + 1) * HEAD_DIM, asked] for i in range(heads)]
            )
            scores = mm(keys[start : start + window], spread, NN)
            for i in range(heads):
                probs = []
                for piece in range(QUERY_TILE // REACH):
                    low, high = live_keys(tile, piece, seq_len)
                    at = i * QUERY_TILE + piece * REACH
                    s = scores[low:high, at : at + REACH] + masks[tile, piece]
                    top = jnp.max(s, axis=0, keepdims=True)
                    e = jnp.exp(s - top)
                    total = jnp.sum(e, axis=0, keepdims=True)
                    p = (e * (1.0 / total)).astype(bf16)
                    probs.append(fill_rows(p, low, high, window))
                probs = jnp.concatenate(probs, axis=1)
                p_ref[0, 0, group, tile, :, i * QUERY_TILE : (i + 1) * QUERY_TILE] = probs
                context = mm(
                    vt[i * HEAD_DIM : (i + 1) * HEAD_DIM, start : start + window], probs, NN
                )
                at = group * width + i * HEAD_DIM
                ct_ref[0, 0, at : at + HEAD_DIM, asked] = context.astype(bf16)


def attend_back_kernel(
    last,
    aliased,
    sides,
    rows,
    place,
    dc_ref,
    ct_ref,
    p_ref,
    qt_ref,
    kt_ref,
    v_ref,
    xt_ref,
    dz_ref,
    *refs,
):
    step = pl.program_id(0)
    row = step % rows
    if len(sides) == 2:
        near_ref, crossed, traded, *refs = refs
        scr = refs.pop()

        @pl.when(step == 0)
        def _():
            scr[0] = near_ref[0].reshape(scr.shape[1:])
            scr[1, :, place[CORE]] = crossed[...]
            scr[1, :, 1 - place[CORE]] = traded[...]

        def weight(s):
            rows_of = scr[step // rows, s]
            return rows_of.reshape(2 * rows_of.shape[1], rows_of.shape[2])

    else:
        weight, refs = take_weights(place, sides[0] == 1, refs)
    if last:
        later_ref, gain0_ref, gain1_ref, *refs = refs
        if aliased:
            _, *refs = refs
        dx_ref, full_ref, keep_ref, send_ref, grad_ref, ds_ref = refs
    else:
        dx_ref, grad_ref, ds_ref = refs
        grad_ref = grad_ref.at[0]
    channels, seq_len = xt_ref.shape[2:]
    width = v_ref.shape[-1]
    window = QUERY_TILE + REACH
    heads = width // HEAD_DIM
    tiles = seq_len // QUERY_TILE
    grads = [[], [], []]
    d_inputs = []
    for group in range(channels // width):
        span = slice(group * width, (group + 1) * width)
        dq_tiles = []
        dk_tiles = []
        dv_tiles = []
        for tile in range(tiles):
            start = key_start(tile, seq_len)
            asked = slice(tile * QUERY_TILE, (tile + 1) * QUERY_TILE)
            d_context = dc_ref[0, 0, span, asked]
            context = ct_ref[0, 0, span, asked]
            both = d_context.astype(f32) * context.astype(f32)
            spread_dc = block_diagonal(
                [d_context[i * HEAD_DIM : (i + 1) * HEAD_DIM] for i in range(heads)]
            )
            qt = qt_ref[0, 0, span, asked]
            spread_q = block_diagonal(
                [qt[i * HEAD_DIM : (i + 1) * HEAD_DIM] for i in range(heads)]
            )
            d_probs = mm(v_ref[0, 0, group, start : start + window], spread_dc, NN)
            dq_heads = []
            for i in range(heads):
                shared = jnp.sum(both[i * HEAD_DIM : (i + 1) * HEAD_DIM], axis=0, keepdims=True)
                for piece in range(QUERY_TILE // REACH):
                    low, high = live_keys(tile, piece, seq_len)
                    at = i * QUERY_TILE + piece * REACH
                    p = p_ref[0, 0, group, tile, low:high, at : at + REACH].astype(f32)
                    dp = d_probs[low:high, at : at + REACH]
                    ds = (p * (dp - shared[:, piece * REACH : (piece + 1) * REACH])).astype(bf16)
                    ds_ref[:, at : at + REACH] = fill_rows(ds, low, high, window)
                of_head = slice(group * width + i * HEAD_DIM, group * width + (i + 1) * HEAD_DIM)
                dq_heads.append(
                    mm(
                        kt_ref[0, 0, of_head, start : start + window],
                        ds_ref[:, i * QUERY_TILE : (i + 1) * QUERY_TILE],
                        NN,
                    )
                )
            dq_tiles.append(jnp.concatenate(dq_heads, axis=0))
            dk_tiles.append(mm(ds_ref[...], spread_q, NT))
            dv_tiles.append(mm(p_ref[0, 0, group, tile], spread_dc, NT))
        dq = jnp.concatenate(dq_tiles, axis=1).astype(bf16)
        dk = join_windows(dk_tiles, seq_len).astype(bf16)
        dv = join_windows(dv_tiles, seq_len).astype(bf16)
        xtg = xt_ref[0, 0, span]
        grads[0].append(mm(xtg, dq, NT))
        grads[1].append(mm(xtg, dk, NN))
        grads[2].append(mm(xtg, dv, NN))
        wq, wk, wv = (weight(s)[:, span] for s in range(3))
        d_inputs.append(
            dz_ref[0, 0, span] + mm(wq, dq, NN) + mm(wk, dk, NT) + mm(wv, dv, NT)
        )
    joined = [jnp.concatenate(parts, axis=1) for parts in grads]

    @pl.when(row == 0)
    def _():
        for s in range(3):
            grad_ref[s] = joined[s]

    @pl.when(row > 0)
    def _():
        for s in range(3):
            grad_ref[s] += joined[s]

    d_input = jnp.concatenate(d_inputs, axis=0)
    if not last:
        dx_ref[0, 0] = d_input
        return
    tok = d_input.astype(bf16).T
    dx_ref[...] = tok
    full_ref[...] = tok

    @pl.when(step == pl.num_programs(0) - 1)
    def _():
        piece = width // 4
        gain_rows = jnp.concatenate([gain0_ref[...], gain1_ref[...]], axis=0).astype(bf16)
        gain_rows = jnp.concatenate([gain_rows[:, :channels], gain_rows[:, channels:]], axis=0)
        for c, out_ref in enumerate((keep_ref, send_ref)):
            for y in range(2):
                at = ((place[CORE] ^ c) * 2 + (place[ROW] ^ y)) * piece
                at_rows = pl.ds(pl.multiple_of(at, piece), piece)
                for layer, source in enumerate((grad_ref, later_ref.at[0])):
                    for s in range(3):
                        out_ref[y, pl.ds((layer * 3 + s) * piece, piece)] = source[
                            s, at_rows
                        ].astype(bf16)
                out_ref[y, pl.ds(6 * piece, 16)] = gain_rows


def join_windows(pieces, seq_len):
    window = QUERY_TILE + REACH
    rows = []
    for at in range(0, seq_len, REACH):
        held = []
        for tile, piece in enumerate(pieces):
            start = key_start(tile, seq_len)
            if start <= at < start + window:
                held.append(piece[at - start : at - start + REACH])
        rows.append(functools.reduce(jnp.add, held))
    return jnp.concatenate(rows, axis=0)


def feature_mean(values):
    return jnp.sum(values, axis=0, keepdims=True) * (1.0 / values.shape[0])


def normalize(before):
    centered = before - feature_mean(before)
    inverse = lax.rsqrt(feature_mean(centered * centered) + epsilon)
    return centered * inverse, inverse


def normalize_back(gradient, gains, normal, inverse):
    scaled = gradient * gains
    return inverse * (scaled - feature_mean(scaled) - normal * feature_mean(scaled * normal))


def gather_far(place, x_ref, c_ref, scr):
    scr[place[CORE]] = x_ref[...]
    scr[1 - place[CORE]] = c_ref[...]


class Near:
    def __init__(self, out_ref, inner_ref, outer_ref):
        self.refs = out_ref, inner_ref, outer_ref

    def out(self):
        return self.refs[0][0]

    def inner(self, group):
        hidden = self.refs[1].shape[2] // 2
        return self.refs[1][0, :, group * hidden : (group + 1) * hidden]

    def outer(self, group):
        width = self.refs[2].shape[2] // 2
        return self.refs[2][0, :, group * width : (group + 1) * width]


class Far:
    def __init__(self, pack):
        self.pack = pack

    def rows(self, k):
        rows = self.pack[:, k]
        return rows.reshape(2 * rows.shape[1], rows.shape[2])

    def out(self):
        return self.rows(0)

    def inner(self, group):
        return self.pack[group, 1]

    def outer(self, group):
        rows = self.rows(2)
        half = rows.shape[1] // 2
        width = half // 2
        at = group * width
        return jnp.concatenate(
            [rows[:, at : at + width], rows[:, half + at : half + at + width]], axis=0
        )


def spread_gains(gains_ref, layer, g_scr):
    for i in range(2):
        g_scr[i] = across(gains_ref[layer, i : i + 1, :])


def wide_gain(g_scr, i, seq_len):
    return jnp.concatenate([g_scr[i]] * (seq_len // 128), axis=1)


def split(values):
    return values.reshape(2, values.shape[0] // 2, values.shape[1])


def join(values):
    return values.reshape(2 * values.shape[1], values.shape[2])


def up(first, weights, group):
    pre = mm(weights.inner(group), first, TN)
    below = 0.5 + 0.5 * lax.erf(pre * 0.7071067811865476)
    slope = below + pre * (jnp.exp(-0.5 * pre * pre) * 0.3989422804014327)
    return (pre * below).astype(bf16), slope.astype(bf16)


def ffn_kernel(layer, place, *refs):
    (xt_ref, ct_ref, out_ref, inner_ref, outer_ref, farx_ref, farc_ref, gains_ref, *refs) = refs
    (n1_ref, r1_ref, act_ref, slope_ref, n2_ref, r2_ref, tok_ref, next_ref, *refs) = refs
    z_scr, fb_scr, far_scr, g_scr = refs
    half, tokens = z_scr.shape[1:]
    width = half // 2
    sides = (place[SELF], place[OTHER])

    @pl.when(pl.program_id(0) == 0)
    def _():
        gather_far(place, farx_ref, farc_ref, far_scr)
        spread_gains(gains_ref, layer, g_scr)

    weights = (Near(out_ref, inner_ref, outer_ref), Far(far_scr))
    z_scr[...] = split(sum(mm(weights[j].out(), ct_ref[j, 0], TN) for j in range(2)))
    for j in range(2):
        z_scr[sides[j]] += xt_ref[j, 0].astype(f32)
    normal, inverse = normalize(join(z_scr[...]))
    n1_ref[0] = split(normal.astype(bf16))
    r1_ref[0] = inverse
    first = normal * wide_gain(g_scr, 0, tokens)
    z_scr[...] = split(first)
    fb_scr[...] = split(first.astype(bf16))
    for j in range(2):
        for group in range(2):
            span = slice(group * width, (group + 1) * width)
            act, slope = up(fb_scr[sides[j], span], weights[j], group)
            act_ref[0, j, group] = act
            slope_ref[0, j, group] = slope
            z_scr[sides[j], span] += mm(weights[j].outer(group), act, TN)
    normal, inverse = normalize(join(z_scr[...]))
    n2_ref[0] = split(normal.astype(bf16))
    r2_ref[0] = inverse
    output = normal * wide_gain(g_scr, 1, tokens)
    tok_ref[...] = output.astype(bf16).T
    next_ref[0] = split(output)


def down(place, weights, acc, d_scr, b_scr, f_scr, act_of, slope_of):
    half = d_scr.shape[1]
    width = half // 2
    sides = (place[SELF], place[OTHER])
    for j in range(2):
        outers = []
        for group in range(2):
            span = slice(group * width, (group + 1) * width)
            d_branch = b_scr[sides[j], span]
            outers.append(mm(act_of(j, group), d_branch, NT))
            d_act = mm(weights[j].outer(group), d_branch, NN)
            d_pre = (d_act * slope_of(j, group).astype(f32)).astype(bf16)
            acc[j, 1, span] += mm(f_scr[sides[j], span], d_pre, NT)
            d_scr[sides[j], span] += mm(weights[j].inner(group), d_pre, NN)
        acc[j, 2] += jnp.concatenate(
            [o[:half] for o in outers] + [o[half:] for o in outers], axis=1
        )


def into_attention(d_before, weights, acc, ct_ref, dc_ref):
    d_attention = d_before.astype(bf16)
    for j in range(2):
        acc[j, 0] += mm(ct_ref[j, 0], d_attention, NT)
        dc_ref[j, 0] = mm(weights[j].out(), d_attention, NN).astype(bf16)


def hand_out(place, acc, keep_ref, send_ref):
    piece = acc.shape[2] // 8
    for c, out_ref in enumerate((keep_ref, send_ref)):
        for s in range(2):
            for j in range(2):
                for y in range(2):
                    at = ((s * 2 + (place[CORE] ^ c)) * 2 + (place[ROW] ^ y)) * piece
                    rows = pl.ds(pl.multiple_of(at, piece), piece)
                    spot = j, y, s
                    for k in range(3):
                        out_ref[(*spot, k)] = acc[j, k, rows].astype(bf16)


def hand_out_gains(gain_acc, gain_ref):
    sums = [jnp.sum(gain_acc[i], axis=1, keepdims=True) for i in range(2)]
    lane = lax.broadcasted_iota(jnp.int32, gain_acc.shape[1:], 1)
    gain_ref[...] = jnp.where(lane == 0, sums[0], sums[1]).T[:4]


def ffn_last_kernel(layer, place, *refs):
    (x_ref, ct_ref, cot_ref, out_ref, inner_ref, outer_ref, *refs) = refs
    (farx_ref, farc_ref, gains_ref, tok_ref, full_ref, *refs) = refs
    (dz1_ref, dc_ref, keep_ref, send_ref, gain_ref, *refs) = refs
    (z_scr, fb_scr, b_scr, n_scr, act_scr, slope_scr, far_scr, g_scr, acc, gain_acc) = refs
    half, tokens = z_scr.shape[1:]
    width = half // 2
    sides = (place[SELF], place[OTHER])
    step = pl.program_id(0)

    @pl.when(step == 0)
    def _():
        gather_far(place, farx_ref, farc_ref, far_scr)
        spread_gains(gains_ref, layer, g_scr)
        acc[...] = jnp.zeros_like(acc)
        gain_acc[...] = jnp.zeros_like(gain_acc)

    weights = (Near(out_ref, inner_ref, outer_ref), Far(far_scr))
    attention = sum(mm(weights[j].out(), ct_ref[j, 0], TN) for j in range(2))
    normal, inverse1 = normalize(attention + join(x_ref[0]))
    n_scr[...] = normal
    first = normal * wide_gain(g_scr, 0, tokens)
    z_scr[...] = split(first)
    fb_scr[...] = split(first.astype(bf16))
    for j in range(2):
        for group in range(2):
            span = slice(group * width, (group + 1) * width)
            act, slope = up(fb_scr[sides[j], span], weights[j], group)
            act_scr[j, group] = act
            slope_scr[j, group] = slope
            z_scr[sides[j], span] += mm(weights[j].outer(group), act, TN)
    normal, inverse = normalize(join(z_scr[...]))
    gain = wide_gain(g_scr, 1, tokens)
    tok = (normal * gain).astype(bf16).T
    tok_ref[...] = tok
    full_ref[...] = tok

    g = cot_ref[...].T.astype(f32)
    gain_acc[1] += lane_sum(g * normal)
    d_second = normalize_back(g, gain, normal, inverse)
    z_scr[...] = split(d_second)
    b_scr[...] = split(d_second.astype(bf16))
    down(
        place,
        weights,
        acc,
        z_scr,
        b_scr,
        fb_scr,
        lambda j, group: act_scr[j, group],
        lambda j, group: slope_scr[j, group],
    )
    d_first = join(z_scr[...])
    normal = n_scr[...]
    gain_acc[0] += lane_sum(d_first * normal)
    d_before = normalize_back(d_first, wide_gain(g_scr, 0, tokens), normal, inverse1)
    dz1_ref[0] = split(d_before)
    into_attention(d_before, weights, acc, ct_ref, dc_ref)

    @pl.when(step == pl.num_programs(0) - 1)
    def _():
        hand_out(place, acc, keep_ref, send_ref)
        hand_out_gains(gain_acc, gain_ref)


def ffn_back_kernel(layer, place, *refs):
    (g_ref, n2_ref, r2_ref, act_ref, slope_ref, n1_ref, r1_ref, ct_ref, *refs) = refs
    (out_ref, inner_ref, outer_ref, farx_ref, farc_ref, gains_ref, *refs) = refs
    (dz1_ref, dc_ref, keep_ref, send_ref, gain_ref, *refs) = refs
    d_scr, b_scr, f_scr, far_scr, g_scr, acc, gain_acc = refs
    tokens = d_scr.shape[2]
    sides = (place[SELF], place[OTHER])
    step = pl.program_id(0)

    @pl.when(step == 0)
    def _():
        gather_far(place, farx_ref, farc_ref, far_scr)
        spread_gains(gains_ref, layer, g_scr)
        acc[...] = jnp.zeros_like(acc)
        gain_acc[...] = jnp.zeros_like(gain_acc)

    weights = (Near(out_ref, inner_ref, outer_ref), Far(far_scr))
    for j in range(2):
        d_scr[sides[j]] = g_ref[j, 0]
    g = join(d_scr[...])
    normal = join(n2_ref[0]).astype(f32)
    gain_acc[1] += lane_sum(g * normal)
    d_second = normalize_back(g, wide_gain(g_scr, 1, tokens), normal, r2_ref[0])
    d_scr[...] = split(d_second)
    b_scr[...] = split(d_second.astype(bf16))
    normal = join(n1_ref[0]).astype(f32)
    gain = wide_gain(g_scr, 0, tokens)
    f_scr[...] = split((normal * gain).astype(bf16))
    down(
        place,
        weights,
        acc,
        d_scr,
        b_scr,
        f_scr,
        lambda j, group: act_ref[0, j, group],
        lambda j, group: slope_ref[0, j, group],
    )
    d_first = join(d_scr[...])
    gain_acc[0] += lane_sum(d_first * normal)
    d_before = normalize_back(d_first, gain, normal, r1_ref[0])
    dz1_ref[0] = split(d_before)
    into_attention(d_before, weights, acc, ct_ref, dc_ref)

    @pl.when(step == pl.num_programs(0) - 1)
    def _():
        hand_out(place, acc, keep_ref, send_ref)
        hand_out_gains(gain_acc, gain_ref)


def lane_sum(values):
    chunks = [values[:, at : at + 128] for at in range(0, values.shape[1], 128)]
    return functools.reduce(jnp.add, chunks)


def placed_pieces(place, parts, size):
    mine, row, core = parts
    for c, y, value in ((0, 0, mine[...]), (0, 1, row[...]), (1, 0, core[0]), (1, 1, core[1])):
        yield ((place[CORE] ^ c) * 2 + (place[ROW] ^ y)) * size, value


def rows_at(at, size):
    return pl.ds(pl.multiple_of(at, size), size)


def finish_kernel(place, *refs):
    count = 6 if len(refs) > 9 else 3
    out_ref, inner_ref, outer_ref, *rest = refs[-3:] if count == 3 else refs[-5:]
    half = outer_ref.shape[4]
    size = half // 8
    for at, value in placed_pieces(place, [r.at[0] if r.ndim == 4 else r.at[:, 0] for r in refs[:3]], size):
        value = value.astype(f32)
        rows = rows_at(at, size)
        out_ref[0, rows, :] = value[0]
        inner_ref[0, rows, :] = value[1]
        outer_ref[0, 0, 0, rows, :] = value[2][:, :half]
        outer_ref[0, 1, 0, rows, :] = value[2][:, half:]
    if count == 3:
        return
    qkv_ref, gain_ref = rest
    layer = pl.program_id(0)
    size = qkv_ref.shape[2] // 4
    mine, row, core = refs[3:6]
    pieces = ((0, 0, mine), (0, 1, row), (1, 0, core.at[0]), (1, 1, core.at[1]))
    for c, y, ref in pieces:
        at = ((place[CORE] ^ c) * 2 + (place[ROW] ^ y)) * size
        for s in range(3):
            qkv_ref[0, s, rows_at(at, size), :] = ref[
                rows_at((layer * 3 + s) * size, size), :
            ].astype(f32)
    gains = mine[6 * size : 6 * size + 16].astype(f32)
    for at_layer in range(2):
        for i in range(2):
            at = at_layer * 4 + i
            gain_ref[at_layer, i : i + 1, :half] = gains[at : at + 1]
            gain_ref[at_layer, i : i + 1, half:] = gains[8 + at : 9 + at]


def pack_kernel(place, out_ref, inner_ref, low_ref, high_ref, qkv_ref, piece_ref, part_ref):
    half = low_ref.shape[2]
    piece_ref[0] = out_ref[0]
    piece_ref[1] = inner_ref[0]
    piece_ref[2, :, :half] = low_ref[0]
    piece_ref[2, :, half:] = high_ref[0]
    part_ref[...] = qkv_ref[0]


def whole(shape):
    return pl.BlockSpec(shape, lambda r, place: (0,) * len(shape))


def per_row(shape):
    rest = (0,) * (len(shape) - 1)
    return pl.BlockSpec((1,) + tuple(shape[1:]), lambda r, place: (r,) + rest)


def struct(shape, dtype):
    return jax.ShapeDtypeStruct(shape, dtype)


def call(
    kernel, rows, place, operands, in_specs, outs, out_specs, scratch, name, us, aliases=None, after=()
):
    count = len(operands)
    in_specs = list(in_specs) + [pl.BlockSpec(memory_space=pl.ANY)] * len(after)
    operands = tuple(operands) + tuple(after)

    def body(place, *refs):
        kernel(place, *refs[:count], *refs[count + len(after) :])

    results = pl.pallas_call(
        body,
        out_shape=outs,
        grid_spec=pltpu.PrefetchScalarGridSpec(
            num_scalar_prefetch=1,
            grid=(rows,),
            in_specs=in_specs,
            out_specs=out_specs,
            scratch_shapes=scratch,
        ),
        compiler_params=pltpu.CompilerParams(vmem_limit_bytes=64 * 2**20 - 2**16),
        cost_estimate=pl.CostEstimate(
            flops=int(us * 5e9), bytes_accessed=int(us * 1e7), transcendentals=0
        ),
        input_output_aliases=aliases or {},
        name=name,
    )(place, *operands)
    return list(results)


def per_side(shape, side):
    rest = (0,) * (len(shape) - 2)
    return pl.BlockSpec((1, 1) + tuple(shape[2:]), lambda r, place: (side, r) + rest)


def both_sides(shape, parts=1):
    middle = (0,) * (len(shape) - 3)
    return pl.BlockSpec(
        (2, 1) + tuple(shape[2:-1]) + (shape[-1] // parts,),
        lambda t, place: (0, t // parts, *middle, t % parts),
    )


def attend(x_tok, w, segments, place, rows, j, layer, us, held=(), after=()):
    row_total, seq_len = segments.shape
    far = j == 1
    channels = w[0].shape[-1]
    width = channels // 2
    heads = width // HEAD_DIM
    groups = channels // width
    tiles = seq_len // QUERY_TILE
    window = QUERY_TILE + REACH
    outs = [
        struct((2, rows, channels, seq_len), bf16),
        struct((2, rows, channels, seq_len), bf16),
        struct((2, rows, channels, seq_len), bf16),
        struct((2, rows, groups, seq_len, width), bf16),
        struct((2, rows, groups, tiles, window, heads * QUERY_TILE), bf16),
        struct((2, rows, channels, seq_len), bf16),
    ]
    if layer == 0:
        x_spec = pl.BlockSpec((seq_len, channels), lambda r, place: (place[OFFSET] + r, place[j]))
    else:
        x_spec = pl.BlockSpec((seq_len, channels), lambda r, place: (r, place[j]))
    operands = (x_tok, *w, segments)
    return call(
        functools.partial(attend_kernel, far),
        rows,
        place,
        operands + tuple(held),
        [x_spec, *weight_blocks(w, far, layer), whole(segments.shape)]
        + [pl.BlockSpec(memory_space=pl.ANY)] * len(held),
        outs,
        [per_side(o.shape, j) for o in outs],
        weight_scratch(w, far),
        "attend",
        us,
        {len(operands) + 1 + i: i for i in range(len(held))},
        after,
    )


def weight_blocks(w, far, layer):
    return [whole(o.shape) for o in w] if far else [layer_block(w[0].shape, layer)]


def weight_scratch(w, far):
    if not far:
        return []
    three, depth, channels = w[0].shape
    return [pltpu.VMEM((three, 2, depth, channels), bf16)]


def layer_block(shape, layer):
    rest = (0,) * (len(shape) - 1)
    return pl.BlockSpec((None,) + tuple(shape[1:]), lambda r, place: (layer,) + rest)


def attend_back(d_context, saved, w, d_before, place, rows, sides, layer, extra, us, after=()):
    xt, qt, kt, values, probs, ct = saved
    channels, seq_len = xt.shape[2:]
    window = QUERY_TILE + REACH
    width = values.shape[-1]
    heads = width // HEAD_DIM
    operands = (d_context, ct, probs, qt, kt, values, xt)
    scratch = [pltpu.VMEM((window, heads * QUERY_TILE), bf16)]
    grad = (3, width, channels)
    if len(sides) == 2:
        near, *far = w
        w_specs = [layer_block4(near.shape, layer)] + [whole(o.shape) for o in far]
        scratch += [pltpu.VMEM((2, 3, 2, width // 2, channels), bf16)]
    else:
        w_specs = weight_blocks(w, sides[0] == 1, layer)
        scratch += weight_scratch(w, sides[0] == 1)

    def side(t):
        return t // rows if len(sides) == 2 else sides[0]

    def one(shape):
        rest = (0,) * (len(shape) - 2)
        return pl.BlockSpec(
            (1, 1) + tuple(shape[2:]), lambda t, place: (side(t), t % rows) + rest
        )

    in_specs = [one(o.shape) for o in operands] + [
        pl.BlockSpec(
            (1, 1, channels, seq_len), lambda t, place: (t % rows, place[side(t)], 0, 0)
        ),
        *w_specs,
    ]
    operands += (d_before, *w)
    aliases = {}
    if extra is None:
        outs = [struct((2, rows, channels, seq_len), f32), struct((2,) + grad, f32)]
        out_specs = [
            one(outs[0].shape),
            pl.BlockSpec((1,) + grad, lambda t, place: (side(t), 0, 0, 0)),
        ]
    else:
        later, gain0, gain1, full = extra
        operands += (later, gain0, gain1)
        in_specs += [one_layer(later.shape, sides[0]), whole(gain0.shape), whole(gain1.shape)]
        if full is not None:
            aliases = {len(operands) + 1: 1}
            operands += (full,)
            in_specs.append(pl.BlockSpec(memory_space=pl.ANY))
        piece = struct((2, 6 * (width // 4) + 16, channels), bf16)
        outs = [
            struct((rows * seq_len, channels), bf16),
            struct((2 * rows * seq_len, 2 * channels), bf16),
            piece,
            piece,
        ]
        out_specs = [
            pl.BlockSpec((seq_len, channels), lambda r, place: (r, 0)),
            pl.BlockSpec(
                (seq_len, channels), lambda r, place: (place[OFFSET] + r, place[sides[0]])
            ),
            whole(piece.shape),
            whole(piece.shape),
        ]
        scratch = [pltpu.VMEM(grad, f32)] + scratch
    return call(
        functools.partial(attend_back_kernel, extra is not None, bool(aliases), sides, rows),
        len(sides) * rows,
        place,
        operands,
        in_specs,
        outs,
        out_specs,
        scratch,
        "attend_back",
        us,
        aliases,
        after,
    )


def layer_block4(shape, layer):
    rest = (0,) * (len(shape) - 1)
    return pl.BlockSpec((1,) + tuple(shape[1:]), lambda t, place: (layer,) + rest)


def per_part(shape, parts):
    middle = (0,) * (len(shape) - 2)
    return pl.BlockSpec(
        (1,) + tuple(shape[1:-1]) + (shape[-1] // parts,),
        lambda t, place: (t // parts, *middle, t % parts),
    )


def weight_specs(weights, layer):
    return [one_layer(o.shape, layer) for o in weights[:3]] + [whole(o.shape) for o in weights[3:]]


def ffn(xts, contexts, weights, gains, place, rows, layer, us):
    half, seq_len = contexts.shape[2:]
    parts = 1
    tokens = seq_len // parts
    stream = (rows, 2, half, seq_len)
    acts = (rows, 2, 2, 2 * half, seq_len)
    outs = [
        struct(stream, bf16),
        struct((rows, 1, seq_len), f32),
        struct(acts, bf16),
        struct(acts, bf16),
        struct(stream, bf16),
        struct((rows, 1, seq_len), f32),
        struct((rows * seq_len, 2 * half), bf16),
        struct(stream, f32),
    ]
    out_specs = [per_part(o.shape, parts) for o in outs]
    out_specs[6] = pl.BlockSpec((tokens, 2 * half), lambda t, place: (t, 0))
    return call(
        functools.partial(ffn_kernel, layer),
        rows * parts,
        place,
        (xts, contexts, *weights, gains),
        [both_sides(xts.shape, parts), both_sides(contexts.shape, parts)]
        + weight_specs(weights, layer)
        + [whole(gains.shape)],
        outs,
        out_specs,
        [
            pltpu.VMEM((2, half, tokens), f32),
            pltpu.VMEM((2, half, tokens), bf16),
            pltpu.VMEM((2,) + weights[3].shape, bf16),
            pltpu.VMEM((2, 2 * half, 128), f32),
        ],
        "ffn",
        us,
    )


def sum_shapes(half):
    piece = struct((2, 2, 2, 3, half // 8, 2 * half), bf16)
    return [piece, piece, struct((4, 2 * half), f32)]


def sum_scratch(weights, half):
    return [
        pltpu.VMEM((2,) + weights[3].shape, bf16),
        pltpu.VMEM((2, 2 * half, 128), f32),
        pltpu.VMEM((2, 3, half, 2 * half), f32),
        pltpu.VMEM((2, 2 * half, 128), f32),
    ]


def ffn_last(x, contexts, cotangent, weights, gains, place, rows, layer, us):
    half, seq_len = contexts.shape[2:]
    wide = 2 * half
    outs = [
        struct((rows * seq_len, wide), bf16),
        struct((2 * rows * seq_len, wide), bf16),
        struct((rows, 2, half, seq_len), f32),
        struct(contexts.shape, bf16),
        *sum_shapes(half),
    ]
    own = pl.BlockSpec((seq_len, wide), lambda r, place: (place[OFFSET] + r, 0))
    out_specs = (
        [pl.BlockSpec((seq_len, wide), lambda r, place: (r, 0)), own]
        + [per_row(outs[2].shape), both_sides(outs[3].shape)]
        + [whole(o.shape) for o in outs[4:]]
    )
    stream = (2, half, seq_len)
    acts = (2, 2, wide, seq_len)
    return call(
        functools.partial(ffn_last_kernel, layer),
        rows,
        place,
        (x, contexts, cotangent, *weights, gains),
        [per_row(x.shape), both_sides(contexts.shape), own]
        + weight_specs(weights, layer)
        + [whole(gains.shape)],
        outs,
        out_specs,
        [
            pltpu.VMEM(stream, f32),
            pltpu.VMEM(stream, bf16),
            pltpu.VMEM(stream, bf16),
            pltpu.VMEM((wide, seq_len), f32),
            pltpu.VMEM(acts, bf16),
            pltpu.VMEM(acts, bf16),
            *sum_scratch(weights, half),
        ],
        "ffn_last",
        us,
    )


def ffn_back(g, saved, contexts, weights, gains, place, rows, layer, us, after=()):
    half, seq_len = contexts.shape[2:]
    stream = (2, half, seq_len)
    outs = [
        struct((rows,) + stream, f32),
        struct(contexts.shape, bf16),
        *sum_shapes(half),
    ]
    out_specs = [per_row(outs[0].shape), both_sides(outs[1].shape)] + [
        whole(o.shape) for o in outs[2:]
    ]
    return call(
        functools.partial(ffn_back_kernel, layer),
        rows,
        place,
        (g, *saved, contexts, *weights, gains),
        [both_sides(g.shape)]
        + [per_row(o.shape) for o in saved]
        + [both_sides(contexts.shape)]
        + weight_specs(weights, layer)
        + [whole(gains.shape)],
        outs,
        out_specs,
        [
            pltpu.VMEM(stream, f32),
            pltpu.VMEM(stream, bf16),
            pltpu.VMEM(stream, bf16),
            *sum_scratch(weights, half),
        ],
        "ffn_back",
        us,
        after=after,
    )


def one_layer(shape, layer):
    rest = (0,) * (len(shape) - 1)
    return pl.BlockSpec((1,) + tuple(shape[1:]), lambda r, place: (layer,) + rest)


def finish(parts, place, layer, layers, qkv_parts=(), held=()):
    operands = [*parts, *qkv_parts]
    half = parts[0].shape[-1] // 2
    width = half // 2
    outs = [
        struct((layers, half, 2 * half), f32),
        struct((layers, width, 4 * half), f32),
        struct((layers, 2, 2, width, half), f32),
    ]
    out_specs = [
        pl.BlockSpec((1, width, 2 * half), lambda s, place: (layer, s, 0)),
        pl.BlockSpec((1, width, 2 * half), lambda s, place: (layer, 0, s)),
        pl.BlockSpec((1, 2, 1, width, half), lambda s, place: (layer, 0, s, 0, 0)),
    ]
    piece = parts[0].shape[1:]
    one = pl.BlockSpec((1,) + piece, lambda s, place: (s, 0, 0, 0))
    two = pl.BlockSpec((2, 1) + piece, lambda s, place: (0, s, 0, 0, 0))
    if qkv_parts:
        outs += [struct((layers, 3, width, half), f32), struct((layers, 2, 2 * half), f32)]
        out_specs += [
            pl.BlockSpec((1, 3, width, half), lambda s, place: (s, 0, 0, 0)),
            whole(outs[-1].shape),
        ]
    return call(
        finish_kernel,
        2,
        place,
        operands + list(held),
        [one, one, two]
        + [whole(o.shape) for o in qkv_parts]
        + [pl.BlockSpec(memory_space=pl.ANY)] * len(held),
        outs,
        out_specs,
        [],
        "finish",
        3,
        {len(operands) + 1 + i: i for i in range(len(held))},
    )


def pack(weights, place, layer, after=()):
    out_w, inner_w, outer_w, qkv_w = weights
    half, wide = out_w.shape[1:]
    three, depth, channels = qkv_w.shape[1:]
    rows = half // 2
    outs = [struct((3, rows, wide), bf16), struct((three, depth // 2, channels), bf16)]
    return call(
        pack_kernel,
        1,
        place,
        (out_w, inner_w, outer_w, outer_w, qkv_w),
        [
            pl.BlockSpec((1, rows, wide), lambda r, place: (layer, place[CORE], 0)),
            pl.BlockSpec((1, depth, wide), lambda r, place: (layer, 0, place[CORE])),
            pl.BlockSpec((1, rows, half), lambda r, place: (layer, place[CORE], 0)),
            pl.BlockSpec((1, rows, half), lambda r, place: (layer, 2 + place[CORE], 0)),
            pl.BlockSpec((1, three, depth // 2, channels), lambda r, place: (layer, 0, place[CORE], 0)),
        ],
        outs,
        [whole(o.shape) for o in outs],
        [],
        "pack",
        3,
        after=after,
    )


def hold(values, place, after):
    anywhere = pl.BlockSpec(memory_space=pl.ANY)
    return call(
        lambda place, *refs: None,
        1,
        place,
        values,
        [anywhere] * len(values),
        [struct(v.shape, v.dtype) for v in values],
        [anywhere] * len(values),
        [],
        "hold",
        1,
        {i + 1: i for i in range(len(values))},
        after,
    )


def fill_input_kernel(place, full_ref, own_ref, far_ref, out_ref):
    column = pl.program_id(0)

    @pl.when(column == 0)
    def _():
        out_ref[...] = own_ref[...]

    @pl.when(column == 1)
    def _():
        out_ref[...] = far_ref[...]


def fill_input(full, from_own, from_far, place, rows, seq_len):
    half = from_own.shape[1]
    count = rows * seq_len
    block = pl.BlockSpec((count, half), lambda j, place: (0, 0))
    return pl.pallas_call(
        fill_input_kernel,
        out_shape=struct(full.shape, full.dtype),
        grid_spec=pltpu.PrefetchScalarGridSpec(
            num_scalar_prefetch=1,
            grid=(2,),
            in_specs=[pl.BlockSpec(memory_space=pl.ANY), block, block],
            out_specs=pl.BlockSpec(
                (count, half), lambda j, place: (place[OTHER], (1 - place[SELF]) ^ j)
            ),
        ),
        input_output_aliases={1: 0},
        name="fill_input",
    )(place, full, from_own, from_far)


def swap(values):
    return lax.ppermute(values, "head", [(0, 1), (1, 0)])


def cross(values):
    count = lax.axis_size("dp")
    return lax.ppermute(
        values, ("dp", "head"), [(2 * a + h, 2 * (a ^ 2) + 1 - h) for a in range(count) for h in range(2)]
    )


def scatter(parts):
    return [swap(parts[0]), trade(parts[1], 2), cross(parts[2])]


SHARES = ((1, 0), (0, 1), (1, 1))


def trade(values, stride):
    count = lax.axis_size("dp")
    return lax.ppermute(values, "dp", [(a, a ^ stride) for a in range(count)])


def far_strides():
    count = lax.axis_size("dp")
    strides = []
    stride = 4
    while stride < count:
        strides.append(stride)
        stride *= 2
    return strides


def sums(groups, place, after=(), casts=None):
    operands = []
    plan = []
    for group in groups:
        terms = []
        for term in group:
            value, *index = term if isinstance(term, tuple) else (term,)
            terms.append((len(operands), tuple(index)))
            operands.append(value)
        plan.append(terms)
    outs = [
        struct(operands[terms[0][0]].shape[len(terms[0][1]) :], operands[terms[0][0]].dtype)
        for terms in plan
    ]

    steps = 2 if all(o.shape[0] == 2 for o in outs) else 1

    def kernel(place, *refs):
        for terms, out in zip(plan, refs[len(operands) :]):
            out[...] = functools.reduce(
                jnp.add, [refs[at][...].astype(f32) for at, _ in terms]
            ).astype(out.dtype)

    def spec(value, index):
        shape = value.shape[len(index) :]
        return pl.BlockSpec(
            (None,) * len(index) + (shape[0] // steps,) + tuple(shape[1:]),
            lambda r, place: tuple(index) + (r,) + (0,) * (len(shape) - 1),
        )

    return call(
        kernel,
        steps,
        place,
        operands,
        [spec(operands[at], index) for terms in plan for at, index in terms],
        outs,
        [spec(o, ()) for o in outs],
        [],
        "sums",
        2,
        after=after,
    )


def add(*terms):
    return functools.reduce(jnp.add, [t.astype(f32) for t in terms]).astype(bf16)


def shards(
    tokens, segments, qkv_weight, out_weight, inner_weight, outer_weight, norm_gains, cotangent
):
    side = lax.axis_index("head").astype(jnp.int32)
    spot = lax.axis_index("dp").astype(jnp.int32)
    layers = qkv_weight.shape[0]
    row_total, seq_len = segments.shape
    rows = row_total // 2
    width = qkv_weight.shape[2]
    place = jnp.stack([side, 1 - side, side * rows, spot & 1, (spot >> 1) & 1])
    weights = (out_weight, inner_weight, outer_weight)
    one = (qkv_weight,)
    far_qkv = [None, None]
    ffn_weights = [None, None]

    piece, part = pack((*weights, qkv_weight), place, 0)
    part, piece = swap(part), swap(piece)
    near = attend(tokens, one, segments, place, rows, 0, 0, 9)
    (part,) = hold([part], place, [near[5]])
    far_qkv[0] = (part, trade(part, 1))
    next_piece, next_part = pack((*weights, qkv_weight), place, 1, [near[5]])
    held = attend(tokens, far_qkv[0], segments, place, rows, 1, 0, 0.2, near, [next_piece])
    piece, next_piece, next_part = hold([piece, next_piece, next_part], place, [held[5]])
    ffn_weights[0] = (*weights, piece, trade(piece, 1))
    part, piece = swap(next_part), swap(next_piece)
    ffn_weights[1] = (*weights, piece, trade(piece, 1))
    saved_attend = [held]
    n1, r1, act, slope, n2, r2, x_tok, x_stream = ffn(
        held[0], held[5], ffn_weights[0], norm_gains, place, rows, 0, 20
    )
    saved_ffn = (n2, r2, act, slope, n1, r1)
    (part,) = hold([part], place, [x_tok])
    far_qkv[1] = (part, trade(part, 1))
    near = attend(x_tok, one, segments, place, rows, 0, 1, 9)
    held = attend(x_tok, far_qkv[1], segments, place, rows, 1, 1, 9, near)
    saved_attend.append(held)
    x_tok, activations, d_before, d_context, keep, send, gain1 = ffn_last(
        x_stream, held[5], cotangent, ffn_weights[1], norm_gains, place, rows, 1, 40
    )

    strides = far_strides()
    far_tok = swap(x_tok)
    got = trade(send, 1)
    dx, later = attend_back(
        d_context, held, one + far_qkv[1], d_before, place, rows, (0, 1), 1, None, 0.2
    )
    parts = sums([[(keep, *at), (got, *at)] for at in SHARES], place, [dx])
    crossed = scatter(parts)
    d_before, d_context, next_keep, next_send, gain0 = ffn_back(
        dx, saved_ffn, saved_attend[0][5], ffn_weights[0], norm_gains, place, rows, 0, 0.2, parts
    )
    (late,) = sums([[(keep, 0, 0), (got, 0, 0), *crossed]], place, [d_before])
    late_got = trade(late, strides[0])
    keep, send = next_keep, next_send
    got = trade(send, 1)
    dx1, full, keep1, send1 = attend_back(
        d_context,
        saved_attend[0],
        far_qkv[0],
        d_before,
        place,
        rows,
        (1,),
        0,
        (later, gain0, gain1, None),
        13,
        [late, far_tok],
    )
    core1 = trade(send1, 1)
    *parts, late = sums(
        [[(keep, *at), (got, *at)] for at in SHARES] + [[late, late_got]], place, [dx1]
    )
    crossed = scatter(parts)
    late_got = trade(late, strides[1])
    dx0, full, keep0, send0 = attend_back(
        d_context,
        saved_attend[0],
        one,
        d_before,
        place,
        rows,
        (0,),
        0,
        (later, gain0, gain1, full),
        13,
        parts + [late],
    )
    core0 = trade(send0, 1)
    (core1,) = hold([core1], place, [dx0])
    shares = [add(keep1[0], core1[0]), add(keep0[1], core0[1]), add(keep1[1], core1[1])]
    shares = scatter(shares)
    total = add(keep0[0], core0[0], *shares)
    early = [add(keep[0, 0, s], got[0, 0, s], *[c[s] for c in crossed]) for s in range(2)]
    orders = (strides, strides[::-1])
    late = add(late, late_got)
    for stride in strides[2:]:
        late = add(late, trade(late, stride))
    late_row = trade(late, 2)
    late_core = trade(jnp.stack([late, late_row]), 1)
    dx0, dx1 = hold([dx0, dx1], place, early)
    far_dx0, far_dx1 = swap(dx0), swap(dx1)
    for at in range(len(strides)):
        early = [add(early[s], trade(early[s], orders[s][at])) for s in range(2)]
        total = add(total, trade(total, strides[at]))
    early = jnp.stack(early)
    grads = finish([late, late_row, late_core], place, 1, layers)
    early_row = trade(early, 2)
    row = trade(total, 2)
    input_grad = fill_input(full, far_dx0, far_dx1, place, rows, seq_len)
    both = jnp.stack([early, early_row])
    early_core = trade(both, 1)
    (pair,) = hold([jnp.stack([total, row])], place, [input_grad, grads[0]])
    core_part = trade(pair, 1)
    other_rows = (1 - side) * rows * seq_len
    activations = lax.dynamic_update_slice(activations, far_tok, (other_rows, jnp.int32(0)))
    out_grad, inner_grad, outer_grad, qkv_grad, gain_grad = finish(
        [early, early_row, early_core], place, 0, layers, [total, row, core_part], grads
    )
    outer_grad = outer_grad.reshape(outer_weight.shape)
    return (activations, input_grad, qkv_grad, out_grad, inner_grad, outer_grad, gain_grad)


def solution(mesh):
    return jax.shard_map(
        shards,
        mesh=mesh,
        in_specs=(
            P("dp", None),
            P("dp", None),
            P(None, None, None, "head"),
            P(None, "head", None),
            P(None, None, "head"),
            P(None, None, "head"),
            P(),
            P("dp", None),
        ),
        out_specs=(
            P("dp", None),
            P("dp", None),
            P(None, None, None, "head"),
            P(None, "head", None),
            P(None, None, "head"),
            P(None, None, "head"),
            P(),
        ),
        check_vma=False,
    )
```

```python
import functools
import jax
import jax.numpy as jnp
from jax import lax
from jax.experimental import pallas as pl
from jax.experimental.pallas import tpu as pltpu
from jax.sharding import PartitionSpec as P

HEAD_DIM = 64
QUERY_TILE = 256
REACH = 128

SELF, OTHER, OFFSET, CORE, ROW = range(5)

epsilon = 1e-12
masked_score = -1e30
f32 = jnp.float32
bf16 = jnp.bfloat16

NN = (((1,), (0,)), ((), ()))
NT = (((1,), (1,)), ((), ()))
TN = (((0,), (0,)), ((), ()))


def mm(left, right, dims):
    return lax.dot_general(left, right, dims, preferred_element_type=f32)


def key_start(tile, seq_len):
    return min(max(tile * QUERY_TILE - REACH, 0), seq_len - QUERY_TILE - REACH)


def live_keys(tile, piece, seq_len):
    window = QUERY_TILE + REACH
    first_query = tile * QUERY_TILE + piece * REACH
    start = key_start(tile, seq_len)
    low = max(first_query - REACH - start, 0)
    high = min(first_query + 2 * REACH - start, window)
    return low, high


def block_diagonal(parts):
    rows = []
    for index, part in enumerate(parts):
        empty = jnp.zeros_like(part)
        rows.append(
            jnp.concatenate([part if at == index else empty for at in range(len(parts))], axis=1)
        )
    return jnp.concatenate(rows, axis=0)


def fill_rows(middle, low, high, total):
    pieces = []
    if low > 0:
        pieces.append(jnp.zeros((low, middle.shape[1]), middle.dtype))
    pieces.append(middle)
    if high < total:
        pieces.append(jnp.zeros((total - high, middle.shape[1]), middle.dtype))
    return jnp.concatenate(pieces, axis=0) if len(pieces) > 1 else middle


def across(row):
    return jnp.broadcast_to(row, (128, row.shape[1])).T


def take_weights(place, far, refs):
    if not far:
        return (lambda s: refs[0][s]), refs[1:]
    crossed, traded, *refs = refs
    scr = refs.pop()

    @pl.when(pl.program_id(0) == 0)
    def _():
        scr[:, place[CORE]] = crossed[...]
        scr[:, 1 - place[CORE]] = traded[...]

    return (lambda s: scr[s].reshape(2 * scr.shape[2], scr.shape[3])), refs


def attend_kernel(far, place, x_ref, *refs):
    weight, refs = take_weights(place, far, refs)
    seg_ref, *refs = refs
    xt_ref, qt_ref, kt_ref, v_ref, p_ref, ct_ref, inv_ref = refs[-7:]
    seq_len, channels = x_ref.shape
    width = v_ref.shape[-1]
    window = QUERY_TILE + REACH
    heads = width // HEAD_DIM
    tiles = seq_len // QUERY_TILE
    x = x_ref[...]
    xt = x.T
    xt_ref[0, 0] = xt
    segq = seg_ref[pl.ds(place[OFFSET] + pl.program_id(0), 1), :].astype(f32)
    segk = across(segq)
    masks = {}
    for tile in range(tiles):
        start = key_start(tile, seq_len)
        for piece in range(QUERY_TILE // REACH):
            low, high = live_keys(tile, piece, seq_len)
            at = tile * QUERY_TILE + piece * REACH
            same = segk[start + low : start + high] == segq[:, at : at + REACH]
            masks[tile, piece] = jnp.where(same, 0.0, masked_score)
    for group in range(channels // width):
        span = slice(group * width, (group + 1) * width)
        xg = x[:, span]
        xtg = xt[span]
        wq, wk, wv = (weight(s)[:, span] for s in range(3))
        qt = mm(wq, xtg, TN).astype(bf16) * jnp.asarray(HEAD_DIM**-0.5, bf16)
        kt = mm(wk, xtg, TN).astype(bf16)
        vt = mm(wv, xtg, TN).astype(bf16)
        keys = mm(xg, wk, NN).astype(bf16)
        values = mm(xg, wv, NN).astype(bf16)
        qt_ref[0, 0, span] = qt
        kt_ref[0, 0, span] = kt * jnp.asarray(HEAD_DIM**-0.5, bf16)
        v_ref[0, 0, group] = values
        for tile in range(tiles):
            start = key_start(tile, seq_len)
            asked = slice(tile * QUERY_TILE, (tile + 1) * QUERY_TILE)
            spread = block_diagonal(
                [qt[i * HEAD_DIM : (i + 1) * HEAD_DIM, asked] for i in range(heads)]
            )
            scores = mm(keys[start : start + window], spread, NN)
            for i in range(heads):
                probs = []
                for piece in range(QUERY_TILE // REACH):
                    low, high = live_keys(tile, piece, seq_len)
                    at = i * QUERY_TILE + piece * REACH
                    s = scores[low:high, at : at + REACH] + masks[tile, piece]
                    top = jnp.max(s, axis=0, keepdims=True)
                    e = jnp.exp(s - top).astype(bf16)
                    probs.append(fill_rows(e, low, high, window))
                probs = jnp.concatenate(probs, axis=1)
                p_ref[0, 0, group, tile, :, i * QUERY_TILE : (i + 1) * QUERY_TILE] = probs
                values_t = vt[i * HEAD_DIM : (i + 1) * HEAD_DIM, start : start + window]
                ones = jnp.ones((16, window), bf16)
                context = mm(jnp.concatenate([values_t, ones], axis=0), probs, NN)
                inverse = 1.0 / context[HEAD_DIM : HEAD_DIM + 1]
                inv_ref[0, 0, group, i : i + 1, asked] = inverse
                at = group * width + i * HEAD_DIM
                ct_ref[0, 0, at : at + HEAD_DIM, asked] = (context[:HEAD_DIM] * inverse).astype(bf16)


def attend_back_kernel(
    last,
    aliased,
    sides,
    rows,
    place,
    dc_ref,
    ct_ref,
    p_ref,
    qt_ref,
    kt_ref,
    v_ref,
    xt_ref,
    inv_ref,
    dz_ref,
    *refs,
):
    step = pl.program_id(0)
    row = step % rows
    if len(sides) == 2:
        near_ref, crossed, traded, *refs = refs
        scr = refs.pop()

        @pl.when(step == 0)
        def _():
            scr[0] = near_ref[0].reshape(scr.shape[1:])
            scr[1, :, place[CORE]] = crossed[...]
            scr[1, :, 1 - place[CORE]] = traded[...]

        def weight(s):
            rows_of = scr[step // rows, s]
            return rows_of.reshape(2 * rows_of.shape[1], rows_of.shape[2])

    else:
        weight, refs = take_weights(place, sides[0] == 1, refs)
    if last:
        later_ref, gain0_ref, gain1_ref, *refs = refs
        if aliased:
            _, *refs = refs
        dx_ref, full_ref, keep_ref, send_ref, grad_ref, ds_ref = refs
    else:
        dx_ref, grad_ref, ds_ref = refs
        grad_ref = grad_ref.at[0]
    channels, seq_len = xt_ref.shape[2:]
    width = v_ref.shape[-1]
    window = QUERY_TILE + REACH
    heads = width // HEAD_DIM
    tiles = seq_len // QUERY_TILE
    grads = [[], [], []]
    d_inputs = []
    for group in range(channels // width):
        span = slice(group * width, (group + 1) * width)
        dq_tiles = []
        dk_tiles = []
        dv_tiles = []
        for tile in range(tiles):
            start = key_start(tile, seq_len)
            asked = slice(tile * QUERY_TILE, (tile + 1) * QUERY_TILE)
            d_context = jnp.concatenate(
                [
                    dc_ref[
                        0, 0, group * width + i * HEAD_DIM : group * width + (i + 1) * HEAD_DIM, asked
                    ].astype(f32)
                    * inv_ref[0, 0, group, i : i + 1, asked]
                    for i in range(heads)
                ],
                axis=0,
            )
            both = d_context * ct_ref[0, 0, span, asked].astype(f32)
            d_context = d_context.astype(bf16)
            spread_dc = block_diagonal(
                [d_context[i * HEAD_DIM : (i + 1) * HEAD_DIM] for i in range(heads)]
            )
            qt = qt_ref[0, 0, span, asked]
            spread_q = block_diagonal(
                [qt[i * HEAD_DIM : (i + 1) * HEAD_DIM] for i in range(heads)]
            )
            d_probs = mm(v_ref[0, 0, group, start : start + window], spread_dc, NN)
            dq_heads = []
            for i in range(heads):
                shared = jnp.sum(both[i * HEAD_DIM : (i + 1) * HEAD_DIM], axis=0, keepdims=True)
                for piece in range(QUERY_TILE // REACH):
                    low, high = live_keys(tile, piece, seq_len)
                    at = i * QUERY_TILE + piece * REACH
                    p = p_ref[0, 0, group, tile, low:high, at : at + REACH].astype(f32)
                    dp = d_probs[low:high, at : at + REACH]
                    ds = (p * (dp - shared[:, piece * REACH : (piece + 1) * REACH])).astype(bf16)
                    ds_ref[:, at : at + REACH] = fill_rows(ds, low, high, window)
                of_head = slice(group * width + i * HEAD_DIM, group * width + (i + 1) * HEAD_DIM)
                dq_heads.append(
                    mm(
                        kt_ref[0, 0, of_head, start : start + window],
                        ds_ref[:, i * QUERY_TILE : (i + 1) * QUERY_TILE],
                        NN,
                    )
                )
            dq_tiles.append(jnp.concatenate(dq_heads, axis=0))
            dk_tiles.append(mm(ds_ref[...], spread_q, NT))
            dv_tiles.append(mm(p_ref[0, 0, group, tile], spread_dc, NT))
        dq = jnp.concatenate(dq_tiles, axis=1).astype(bf16)
        dk = join_windows(dk_tiles, seq_len).astype(bf16)
        dv = join_windows(dv_tiles, seq_len).astype(bf16)
        xtg = xt_ref[0, 0, span]
        grads[0].append(mm(xtg, dq, NT))
        grads[1].append(mm(xtg, dk, NN))
        grads[2].append(mm(xtg, dv, NN))
        wq, wk, wv = (weight(s)[:, span] for s in range(3))
        d_inputs.append(
            dz_ref[0, 0, span] + mm(wq, dq, NN) + mm(wk, dk, NT) + mm(wv, dv, NT)
        )
    joined = [jnp.concatenate(parts, axis=1) for parts in grads]

    @pl.when(row == 0)
    def _():
        for s in range(3):
            grad_ref[s] = joined[s]

    @pl.when(row > 0)
    def _():
        for s in range(3):
            grad_ref[s] += joined[s]

    d_input = jnp.concatenate(d_inputs, axis=0)
    if not last:
        dx_ref[0, 0] = d_input
        return
    tok = d_input.astype(bf16).T
    dx_ref[...] = tok
    full_ref[...] = tok

    @pl.when(step == pl.num_programs(0) - 1)
    def _():
        piece = width // 4
        gain_rows = jnp.concatenate([gain0_ref[...], gain1_ref[...]], axis=0).astype(bf16)
        gain_rows = jnp.concatenate([gain_rows[:, :channels], gain_rows[:, channels:]], axis=0)
        for c, out_ref in enumerate((keep_ref, send_ref)):
            for y in range(2):
                at = ((place[CORE] ^ c) * 2 + (place[ROW] ^ y)) * piece
                at_rows = pl.ds(pl.multiple_of(at, piece), piece)
                for layer, source in enumerate((grad_ref, later_ref.at[0])):
                    for s in range(3):
                        out_ref[y, pl.ds((layer * 3 + s) * piece, piece)] = source[
                            s, at_rows
                        ].astype(bf16)
                out_ref[y, pl.ds(6 * piece, 16)] = gain_rows


def join_windows(pieces, seq_len):
    window = QUERY_TILE + REACH
    rows = []
    for at in range(0, seq_len, REACH):
        held = []
        for tile, piece in enumerate(pieces):
            start = key_start(tile, seq_len)
            if start <= at < start + window:
                held.append(piece[at - start : at - start + REACH])
        rows.append(functools.reduce(jnp.add, held))
    return jnp.concatenate(rows, axis=0)


def feature_mean(values):
    return jnp.sum(values, axis=0, keepdims=True) * (1.0 / values.shape[0])


def normalize(before):
    centered = before - feature_mean(before)
    inverse = lax.rsqrt(feature_mean(centered * centered) + epsilon)
    return centered * inverse, inverse


def normalize_back(gradient, gains, normal, inverse):
    scaled = gradient * gains
    return inverse * (scaled - feature_mean(scaled) - normal * feature_mean(scaled * normal))


def gather_far(place, x_ref, c_ref, scr):
    scr[place[CORE]] = x_ref[...]
    scr[1 - place[CORE]] = c_ref[...]


class Near:
    def __init__(self, out_ref, inner_ref, outer_ref):
        self.refs = out_ref, inner_ref, outer_ref

    def out(self):
        return self.refs[0][0]

    def inner(self, group):
        hidden = self.refs[1].shape[2] // 2
        return self.refs[1][0, :, group * hidden : (group + 1) * hidden]

    def outer(self, group):
        width = self.refs[2].shape[2] // 2
        return self.refs[2][0, :, group * width : (group + 1) * width]


class Far:
    def __init__(self, pack):
        self.pack = pack

    def rows(self, k):
        rows = self.pack[:, k]
        return rows.reshape(2 * rows.shape[1], rows.shape[2])

    def out(self):
        return self.rows(0)

    def inner(self, group):
        return self.pack[group, 1]

    def outer(self, group):
        rows = self.rows(2)
        half = rows.shape[1] // 2
        width = half // 2
        at = group * width
        return jnp.concatenate(
            [rows[:, at : at + width], rows[:, half + at : half + at + width]], axis=0
        )


def spread_gains(gains_ref, layer, g_scr):
    for i in range(2):
        g_scr[i] = across(gains_ref[layer, i : i + 1, :])


def wide_gain(g_scr, i, seq_len):
    return jnp.concatenate([g_scr[i]] * (seq_len // 128), axis=1)


def split(values):
    return values.reshape(2, values.shape[0] // 2, values.shape[1])


def join(values):
    return values.reshape(2 * values.shape[1], values.shape[2])


def up(first, weights, group):
    pre = mm(weights.inner(group), first, TN)
    below = 0.5 + 0.5 * lax.erf(pre * 0.7071067811865476)
    slope = below + pre * (jnp.exp(-0.5 * pre * pre) * 0.3989422804014327)
    return (pre * below).astype(bf16), slope.astype(bf16)


def ffn_kernel(layer, place, *refs):
    (xt_ref, ct_ref, out_ref, inner_ref, outer_ref, farx_ref, farc_ref, gains_ref, *refs) = refs
    (n1_ref, r1_ref, act_ref, slope_ref, n2_ref, r2_ref, tok_ref, next_ref, *refs) = refs
    z_scr, fb_scr, far_scr, g_scr = refs
    half, tokens = z_scr.shape[1:]
    width = half // 2
    sides = (place[SELF], place[OTHER])

    @pl.when(pl.program_id(0) == 0)
    def _():
        gather_far(place, farx_ref, farc_ref, far_scr)
        spread_gains(gains_ref, layer, g_scr)

    weights = (Near(out_ref, inner_ref, outer_ref), Far(far_scr))
    z_scr[...] = split(sum(mm(weights[j].out(), ct_ref[j, 0], TN) for j in range(2)))
    for j in range(2):
        z_scr[sides[j]] += xt_ref[j, 0].astype(f32)
    normal, inverse = normalize(join(z_scr[...]))
    n1_ref[0] = split(normal.astype(bf16))
    r1_ref[0] = inverse
    first = normal * wide_gain(g_scr, 0, tokens)
    z_scr[...] = split(first)
    fb_scr[...] = split(first.astype(bf16))
    for j in range(2):
        for group in range(2):
            span = slice(group * width, (group + 1) * width)
            act, slope = up(fb_scr[sides[j], span], weights[j], group)
            act_ref[0, j, group] = act
            slope_ref[0, j, group] = slope
            z_scr[sides[j], span] += mm(weights[j].outer(group), act, TN)
    normal, inverse = normalize(join(z_scr[...]))
    n2_ref[0] = split(normal.astype(bf16))
    r2_ref[0] = inverse
    output = normal * wide_gain(g_scr, 1, tokens)
    tok_ref[...] = output.astype(bf16).T
    next_ref[0] = split(output)


def down(place, weights, acc, d_scr, b_scr, f_scr, act_of, slope_of):
    half = d_scr.shape[1]
    width = half // 2
    sides = (place[SELF], place[OTHER])
    for j in range(2):
        outers = []
        for group in range(2):
            span = slice(group * width, (group + 1) * width)
            d_branch = b_scr[sides[j], span]
            outers.append(mm(act_of(j, group), d_branch, NT))
            d_act = mm(weights[j].outer(group), d_branch, NN)
            d_pre = (d_act * slope_of(j, group).astype(f32)).astype(bf16)
            acc[j, 1, span] += mm(f_scr[sides[j], span], d_pre, NT)
            d_scr[sides[j], span] += mm(weights[j].inner(group), d_pre, NN)
        acc[j, 2] += jnp.concatenate(
            [o[:half] for o in outers] + [o[half:] for o in outers], axis=1
        )


def into_attention(d_before, weights, acc, ct_ref, dc_ref):
    d_attention = d_before.astype(bf16)
    for j in range(2):
        acc[j, 0] += mm(ct_ref[j, 0], d_attention, NT)
        dc_ref[j, 0] = mm(weights[j].out(), d_attention, NN).astype(bf16)


def hand_out(place, acc, keep_ref, send_ref):
    piece = acc.shape[2] // 8
    for c, out_ref in enumerate((keep_ref, send_ref)):
        for s in range(2):
            for j in range(2):
                for y in range(2):
                    at = ((s * 2 + (place[CORE] ^ c)) * 2 + (place[ROW] ^ y)) * piece
                    rows = pl.ds(pl.multiple_of(at, piece), piece)
                    spot = j, y, s
                    for k in range(3):
                        out_ref[(*spot, k)] = acc[j, k, rows].astype(bf16)


def hand_out_gains(gain_acc, gain_ref):
    sums = [jnp.sum(gain_acc[i], axis=1, keepdims=True) for i in range(2)]
    lane = lax.broadcasted_iota(jnp.int32, gain_acc.shape[1:], 1)
    gain_ref[...] = jnp.where(lane == 0, sums[0], sums[1]).T[:4]


def ffn_last_kernel(layer, place, *refs):
    (x_ref, ct_ref, cot_ref, out_ref, inner_ref, outer_ref, *refs) = refs
    (farx_ref, farc_ref, gains_ref, tok_ref, full_ref, *refs) = refs
    (dz1_ref, dc_ref, keep_ref, send_ref, gain_ref, *refs) = refs
    (z_scr, fb_scr, b_scr, n_scr, act_scr, slope_scr, far_scr, g_scr, acc, gain_acc) = refs
    half, tokens = z_scr.shape[1:]
    width = half // 2
    sides = (place[SELF], place[OTHER])
    step = pl.program_id(0)

    @pl.when(step == 0)
    def _():
        gather_far(place, farx_ref, farc_ref, far_scr)
        spread_gains(gains_ref, layer, g_scr)
        acc[...] = jnp.zeros_like(acc)
        gain_acc[...] = jnp.zeros_like(gain_acc)

    weights = (Near(out_ref, inner_ref, outer_ref), Far(far_scr))
    attention = sum(mm(weights[j].out(), ct_ref[j, 0], TN) for j in range(2))
    normal, inverse1 = normalize(attention + join(x_ref[0]))
    n_scr[...] = normal
    first = normal * wide_gain(g_scr, 0, tokens)
    z_scr[...] = split(first)
    fb_scr[...] = split(first.astype(bf16))
    for j in range(2):
        for group in range(2):
            span = slice(group * width, (group + 1) * width)
            act, slope = up(fb_scr[sides[j], span], weights[j], group)
            act_scr[j, group] = act
            slope_scr[j, group] = slope
            z_scr[sides[j], span] += mm(weights[j].outer(group), act, TN)
    normal, inverse = normalize(join(z_scr[...]))
    gain = wide_gain(g_scr, 1, tokens)
    tok = (normal * gain).astype(bf16).T
    tok_ref[...] = tok
    full_ref[...] = tok

    g = cot_ref[...].T.astype(f32)
    gain_acc[1] += lane_sum(g * normal)
    d_second = normalize_back(g, gain, normal, inverse)
    z_scr[...] = split(d_second)
    b_scr[...] = split(d_second.astype(bf16))
    down(
        place,
        weights,
        acc,
        z_scr,
        b_scr,
        fb_scr,
        lambda j, group: act_scr[j, group],
        lambda j, group: slope_scr[j, group],
    )
    d_first = join(z_scr[...])
    normal = n_scr[...]
    gain_acc[0] += lane_sum(d_first * normal)
    d_before = normalize_back(d_first, wide_gain(g_scr, 0, tokens), normal, inverse1)
    dz1_ref[0] = split(d_before)
    into_attention(d_before, weights, acc, ct_ref, dc_ref)

    @pl.when(step == pl.num_programs(0) - 1)
    def _():
        hand_out(place, acc, keep_ref, send_ref)
        hand_out_gains(gain_acc, gain_ref)


def ffn_back_kernel(layer, place, *refs):
    (g_ref, n2_ref, r2_ref, act_ref, slope_ref, n1_ref, r1_ref, ct_ref, *refs) = refs
    (out_ref, inner_ref, outer_ref, farx_ref, farc_ref, gains_ref, *refs) = refs
    (dz1_ref, dc_ref, keep_ref, send_ref, gain_ref, *refs) = refs
    d_scr, b_scr, f_scr, far_scr, g_scr, acc, gain_acc = refs
    tokens = d_scr.shape[2]
    sides = (place[SELF], place[OTHER])
    step = pl.program_id(0)

    @pl.when(step == 0)
    def _():
        gather_far(place, farx_ref, farc_ref, far_scr)
        spread_gains(gains_ref, layer, g_scr)
        acc[...] = jnp.zeros_like(acc)
        gain_acc[...] = jnp.zeros_like(gain_acc)

    weights = (Near(out_ref, inner_ref, outer_ref), Far(far_scr))
    for j in range(2):
        d_scr[sides[j]] = g_ref[j, 0]
    g = join(d_scr[...])
    normal = join(n2_ref[0]).astype(f32)
    gain_acc[1] += lane_sum(g * normal)
    d_second = normalize_back(g, wide_gain(g_scr, 1, tokens), normal, r2_ref[0])
    d_scr[...] = split(d_second)
    b_scr[...] = split(d_second.astype(bf16))
    normal = join(n1_ref[0]).astype(f32)
    gain = wide_gain(g_scr, 0, tokens)
    f_scr[...] = split((normal * gain).astype(bf16))
    down(
        place,
        weights,
        acc,
        d_scr,
        b_scr,
        f_scr,
        lambda j, group: act_ref[0, j, group],
        lambda j, group: slope_ref[0, j, group],
    )
    d_first = join(d_scr[...])
    gain_acc[0] += lane_sum(d_first * normal)
    d_before = normalize_back(d_first, gain, normal, r1_ref[0])
    dz1_ref[0] = split(d_before)
    into_attention(d_before, weights, acc, ct_ref, dc_ref)

    @pl.when(step == pl.num_programs(0) - 1)
    def _():
        hand_out(place, acc, keep_ref, send_ref)
        hand_out_gains(gain_acc, gain_ref)


def lane_sum(values):
    chunks = [values[:, at : at + 128] for at in range(0, values.shape[1], 128)]
    return functools.reduce(jnp.add, chunks)


def placed_pieces(place, parts, size):
    mine, row, core = parts
    for c, y, value in ((0, 0, mine[...]), (0, 1, row[...]), (1, 0, core[0]), (1, 1, core[1])):
        yield ((place[CORE] ^ c) * 2 + (place[ROW] ^ y)) * size, value


def rows_at(at, size):
    return pl.ds(pl.multiple_of(at, size), size)


def finish_kernel(place, *refs):
    count = 6 if len(refs) > 9 else 3
    out_ref, inner_ref, outer_ref, *rest = refs[-3:] if count == 3 else refs[-5:]
    half = outer_ref.shape[4]
    size = half // 8
    for at, value in placed_pieces(place, [r.at[0] if r.ndim == 4 else r.at[:, 0] for r in refs[:3]], size):
        value = value.astype(f32)
        rows = rows_at(at, size)
        out_ref[0, rows, :] = value[0]
        inner_ref[0, rows, :] = value[1]
        outer_ref[0, 0, 0, rows, :] = value[2][:, :half]
        outer_ref[0, 1, 0, rows, :] = value[2][:, half:]
    if count == 3:
        return
    qkv_ref, gain_ref = rest
    layer = pl.program_id(0)
    size = qkv_ref.shape[2] // 4
    mine, row, core = refs[3:6]
    pieces = ((0, 0, mine), (0, 1, row), (1, 0, core.at[0]), (1, 1, core.at[1]))
    for c, y, ref in pieces:
        at = ((place[CORE] ^ c) * 2 + (place[ROW] ^ y)) * size
        for s in range(3):
            qkv_ref[0, s, rows_at(at, size), :] = ref[
                rows_at((layer * 3 + s) * size, size), :
            ].astype(f32)
    gains = mine[6 * size : 6 * size + 16].astype(f32)
    for at_layer in range(2):
        for i in range(2):
            at = at_layer * 4 + i
            gain_ref[at_layer, i : i + 1, :half] = gains[at : at + 1]
            gain_ref[at_layer, i : i + 1, half:] = gains[8 + at : 9 + at]


def pack_kernel(place, out_ref, inner_ref, low_ref, high_ref, qkv_ref, piece_ref, part_ref):
    half = low_ref.shape[2]
    piece_ref[0] = out_ref[0]
    piece_ref[1] = inner_ref[0]
    piece_ref[2, :, :half] = low_ref[0]
    piece_ref[2, :, half:] = high_ref[0]
    part_ref[...] = qkv_ref[0]


def whole(shape):
    return pl.BlockSpec(shape, lambda r, place: (0,) * len(shape))


def per_row(shape):
    rest = (0,) * (len(shape) - 1)
    return pl.BlockSpec((1,) + tuple(shape[1:]), lambda r, place: (r,) + rest)


def struct(shape, dtype):
    return jax.ShapeDtypeStruct(shape, dtype)


def call(
    kernel, rows, place, operands, in_specs, outs, out_specs, scratch, name, us, aliases=None, after=()
):
    count = len(operands)
    in_specs = list(in_specs) + [pl.BlockSpec(memory_space=pl.ANY)] * len(after)
    operands = tuple(operands) + tuple(after)

    def body(place, *refs):
        kernel(place, *refs[:count], *refs[count + len(after) :])

    results = pl.pallas_call(
        body,
        out_shape=outs,
        grid_spec=pltpu.PrefetchScalarGridSpec(
            num_scalar_prefetch=1,
            grid=(rows,),
            in_specs=in_specs,
            out_specs=out_specs,
            scratch_shapes=scratch,
        ),
        compiler_params=pltpu.CompilerParams(vmem_limit_bytes=64 * 2**20 - 2**16),
        cost_estimate=pl.CostEstimate(
            flops=int(us * 5e9), bytes_accessed=int(us * 1e7), transcendentals=0
        ),
        input_output_aliases=aliases or {},
        name=name,
    )(place, *operands)
    return list(results)


def per_side(shape, side):
    rest = (0,) * (len(shape) - 2)
    return pl.BlockSpec((1, 1) + tuple(shape[2:]), lambda r, place: (side, r) + rest)


def both_sides(shape, parts=1):
    middle = (0,) * (len(shape) - 3)
    return pl.BlockSpec(
        (2, 1) + tuple(shape[2:-1]) + (shape[-1] // parts,),
        lambda t, place: (0, t // parts, *middle, t % parts),
    )


def attend(x_tok, w, segments, place, rows, j, layer, us, held=(), after=()):
    row_total, seq_len = segments.shape
    far = j == 1
    channels = w[0].shape[-1]
    width = channels // 2
    heads = width // HEAD_DIM
    groups = channels // width
    tiles = seq_len // QUERY_TILE
    window = QUERY_TILE + REACH
    outs = [
        struct((2, rows, channels, seq_len), bf16),
        struct((2, rows, channels, seq_len), bf16),
        struct((2, rows, channels, seq_len), bf16),
        struct((2, rows, groups, seq_len, width), bf16),
        struct((2, rows, groups, tiles, window, heads * QUERY_TILE), bf16),
        struct((2, rows, channels, seq_len), bf16),
        struct((2, rows, groups, 8, seq_len), f32),
    ]
    if layer == 0:
        x_spec = pl.BlockSpec((seq_len, channels), lambda r, place: (place[OFFSET] + r, place[j]))
    else:
        x_spec = pl.BlockSpec((seq_len, channels), lambda r, place: (r, place[j]))
    operands = (x_tok, *w, segments)
    return call(
        functools.partial(attend_kernel, far),
        rows,
        place,
        operands + tuple(held),
        [x_spec, *weight_blocks(w, far, layer), whole(segments.shape)]
        + [pl.BlockSpec(memory_space=pl.ANY)] * len(held),
        outs,
        [per_side(o.shape, j) for o in outs],
        weight_scratch(w, far),
        "attend",
        us,
        {len(operands) + 1 + i: i for i in range(len(held))},
        after,
    )


def weight_blocks(w, far, layer):
    return [whole(o.shape) for o in w] if far else [layer_block(w[0].shape, layer)]


def weight_scratch(w, far):
    if not far:
        return []
    three, depth, channels = w[0].shape
    return [pltpu.VMEM((three, 2, depth, channels), bf16)]


def layer_block(shape, layer):
    rest = (0,) * (len(shape) - 1)
    return pl.BlockSpec((None,) + tuple(shape[1:]), lambda r, place: (layer,) + rest)


def attend_back(d_context, saved, w, d_before, place, rows, sides, layer, extra, us, after=()):
    xt, qt, kt, values, probs, ct, inverse = saved
    channels, seq_len = xt.shape[2:]
    window = QUERY_TILE + REACH
    width = values.shape[-1]
    heads = width // HEAD_DIM
    operands = (d_context, ct, probs, qt, kt, values, xt, inverse)
    scratch = [pltpu.VMEM((window, heads * QUERY_TILE), bf16)]
    grad = (3, width, channels)
    if len(sides) == 2:
        near, *far = w
        w_specs = [layer_block4(near.shape, layer)] + [whole(o.shape) for o in far]
        scratch += [pltpu.VMEM((2, 3, 2, width // 2, channels), bf16)]
    else:
        w_specs = weight_blocks(w, sides[0] == 1, layer)
        scratch += weight_scratch(w, sides[0] == 1)

    def side(t):
        return t // rows if len(sides) == 2 else sides[0]

    def one(shape):
        rest = (0,) * (len(shape) - 2)
        return pl.BlockSpec(
            (1, 1) + tuple(shape[2:]), lambda t, place: (side(t), t % rows) + rest
        )

    in_specs = [one(o.shape) for o in operands] + [
        pl.BlockSpec(
            (1, 1, channels, seq_len), lambda t, place: (t % rows, place[side(t)], 0, 0)
        ),
        *w_specs,
    ]
    operands += (d_before, *w)
    aliases = {}
    if extra is None:
        outs = [struct((2, rows, channels, seq_len), f32), struct((2,) + grad, f32)]
        out_specs = [
            one(outs[0].shape),
            pl.BlockSpec((1,) + grad, lambda t, place: (side(t), 0, 0, 0)),
        ]
    else:
        later, gain0, gain1, full = extra
        operands += (later, gain0, gain1)
        in_specs += [one_layer(later.shape, sides[0]), whole(gain0.shape), whole(gain1.shape)]
        if full is not None:
            aliases = {len(operands) + 1: 1}
            operands += (full,)
            in_specs.append(pl.BlockSpec(memory_space=pl.ANY))
        piece = struct((2, 6 * (width // 4) + 16, channels), bf16)
        outs = [
            struct((rows * seq_len, channels), bf16),
            struct((2 * rows * seq_len, 2 * channels), bf16),
            piece,
            piece,
        ]
        out_specs = [
            pl.BlockSpec((seq_len, channels), lambda r, place: (r, 0)),
            pl.BlockSpec(
                (seq_len, channels), lambda r, place: (place[OFFSET] + r, place[sides[0]])
            ),
            whole(piece.shape),
            whole(piece.shape),
        ]
        scratch = [pltpu.VMEM(grad, f32)] + scratch
    return call(
        functools.partial(attend_back_kernel, extra is not None, bool(aliases), sides, rows),
        len(sides) * rows,
        place,
        operands,
        in_specs,
        outs,
        out_specs,
        scratch,
        "attend_back",
        us,
        aliases,
        after,
    )


def layer_block4(shape, layer):
    rest = (0,) * (len(shape) - 1)
    return pl.BlockSpec((1,) + tuple(shape[1:]), lambda t, place: (layer,) + rest)


def per_part(shape, parts):
    middle = (0,) * (len(shape) - 2)
    return pl.BlockSpec(
        (1,) + tuple(shape[1:-1]) + (shape[-1] // parts,),
        lambda t, place: (t // parts, *middle, t % parts),
    )


def weight_specs(weights, layer):
    return [one_layer(o.shape, layer) for o in weights[:3]] + [whole(o.shape) for o in weights[3:]]


def ffn(xts, contexts, weights, gains, place, rows, layer, us):
    half, seq_len = contexts.shape[2:]
    parts = 1
    tokens = seq_len // parts
    stream = (rows, 2, half, seq_len)
    acts = (rows, 2, 2, 2 * half, seq_len)
    outs = [
        struct(stream, bf16),
        struct((rows, 1, seq_len), f32),
        struct(acts, bf16),
        struct(acts, bf16),
        struct(stream, bf16),
        struct((rows, 1, seq_len), f32),
        struct((rows * seq_len, 2 * half), bf16),
        struct(stream, f32),
    ]
    out_specs = [per_part(o.shape, parts) for o in outs]
    out_specs[6] = pl.BlockSpec((tokens, 2 * half), lambda t, place: (t, 0))
    return call(
        functools.partial(ffn_kernel, layer),
        rows * parts,
        place,
        (xts, contexts, *weights, gains),
        [both_sides(xts.shape, parts), both_sides(contexts.shape, parts)]
        + weight_specs(weights, layer)
        + [whole(gains.shape)],
        outs,
        out_specs,
        [
            pltpu.VMEM((2, half, tokens), f32),
            pltpu.VMEM((2, half, tokens), bf16),
            pltpu.VMEM((2,) + weights[3].shape, bf16),
            pltpu.VMEM((2, 2 * half, 128), f32),
        ],
        "ffn",
        us,
    )


def sum_shapes(half):
    piece = struct((2, 2, 2, 3, half // 8, 2 * half), bf16)
    return [piece, piece, struct((4, 2 * half), f32)]


def sum_scratch(weights, half):
    return [
        pltpu.VMEM((2,) + weights[3].shape, bf16),
        pltpu.VMEM((2, 2 * half, 128), f32),
        pltpu.VMEM((2, 3, half, 2 * half), f32),
        pltpu.VMEM((2, 2 * half, 128), f32),
    ]


def ffn_last(x, contexts, cotangent, weights, gains, place, rows, layer, us):
    half, seq_len = contexts.shape[2:]
    wide = 2 * half
    outs = [
        struct((rows * seq_len, wide), bf16),
        struct((2 * rows * seq_len, wide), bf16),
        struct((rows, 2, half, seq_len), f32),
        struct(contexts.shape, bf16),
        *sum_shapes(half),
    ]
    own = pl.BlockSpec((seq_len, wide), lambda r, place: (place[OFFSET] + r, 0))
    out_specs = (
        [pl.BlockSpec((seq_len, wide), lambda r, place: (r, 0)), own]
        + [per_row(outs[2].shape), both_sides(outs[3].shape)]
        + [whole(o.shape) for o in outs[4:]]
    )
    stream = (2, half, seq_len)
    acts = (2, 2, wide, seq_len)
    return call(
        functools.partial(ffn_last_kernel, layer),
        rows,
        place,
        (x, contexts, cotangent, *weights, gains),
        [per_row(x.shape), both_sides(contexts.shape), own]
        + weight_specs(weights, layer)
        + [whole(gains.shape)],
        outs,
        out_specs,
        [
            pltpu.VMEM(stream, f32),
            pltpu.VMEM(stream, bf16),
            pltpu.VMEM(stream, bf16),
            pltpu.VMEM((wide, seq_len), f32),
            pltpu.VMEM(acts, bf16),
            pltpu.VMEM(acts, bf16),
            *sum_scratch(weights, half),
        ],
        "ffn_last",
        us,
    )


def ffn_back(g, saved, contexts, weights, gains, place, rows, layer, us, after=()):
    half, seq_len = contexts.shape[2:]
    stream = (2, half, seq_len)
    outs = [
        struct((rows,) + stream, f32),
        struct(contexts.shape, bf16),
        *sum_shapes(half),
    ]
    out_specs = [per_row(outs[0].shape), both_sides(outs[1].shape)] + [
        whole(o.shape) for o in outs[2:]
    ]
    return call(
        functools.partial(ffn_back_kernel, layer),
        rows,
        place,
        (g, *saved, contexts, *weights, gains),
        [both_sides(g.shape)]
        + [per_row(o.shape) for o in saved]
        + [both_sides(contexts.shape)]
        + weight_specs(weights, layer)
        + [whole(gains.shape)],
        outs,
        out_specs,
        [
            pltpu.VMEM(stream, f32),
            pltpu.VMEM(stream, bf16),
            pltpu.VMEM(stream, bf16),
            *sum_scratch(weights, half),
        ],
        "ffn_back",
        us,
        after=after,
    )


def one_layer(shape, layer):
    rest = (0,) * (len(shape) - 1)
    return pl.BlockSpec((1,) + tuple(shape[1:]), lambda r, place: (layer,) + rest)


def finish(parts, place, layer, layers, qkv_parts=(), held=()):
    operands = [*parts, *qkv_parts]
    half = parts[0].shape[-1] // 2
    width = half // 2
    outs = [
        struct((layers, half, 2 * half), f32),
        struct((layers, width, 4 * half), f32),
        struct((layers, 2, 2, width, half), f32),
    ]
    out_specs = [
        pl.BlockSpec((1, width, 2 * half), lambda s, place: (layer, s, 0)),
        pl.BlockSpec((1, width, 2 * half), lambda s, place: (layer, 0, s)),
        pl.BlockSpec((1, 2, 1, width, half), lambda s, place: (layer, 0, s, 0, 0)),
    ]
    piece = parts[0].shape[1:]
    one = pl.BlockSpec((1,) + piece, lambda s, place: (s, 0, 0, 0))
    two = pl.BlockSpec((2, 1) + piece, lambda s, place: (0, s, 0, 0, 0))
    if qkv_parts:
        outs += [struct((layers, 3, width, half), f32), struct((layers, 2, 2 * half), f32)]
        out_specs += [
            pl.BlockSpec((1, 3, width, half), lambda s, place: (s, 0, 0, 0)),
            whole(outs[-1].shape),
        ]
    return call(
        finish_kernel,
        2,
        place,
        operands + list(held),
        [one, one, two]
        + [whole(o.shape) for o in qkv_parts]
        + [pl.BlockSpec(memory_space=pl.ANY)] * len(held),
        outs,
        out_specs,
        [],
        "finish",
        3,
        {len(operands) + 1 + i: i for i in range(len(held))},
    )


def pack(weights, place, layer, after=()):
    out_w, inner_w, outer_w, qkv_w = weights
    half, wide = out_w.shape[1:]
    three, depth, channels = qkv_w.shape[1:]
    rows = half // 2
    outs = [struct((3, rows, wide), bf16), struct((three, depth // 2, channels), bf16)]
    return call(
        pack_kernel,
        1,
        place,
        (out_w, inner_w, outer_w, outer_w, qkv_w),
        [
            pl.BlockSpec((1, rows, wide), lambda r, place: (layer, place[CORE], 0)),
            pl.BlockSpec((1, depth, wide), lambda r, place: (layer, 0, place[CORE])),
            pl.BlockSpec((1, rows, half), lambda r, place: (layer, place[CORE], 0)),
            pl.BlockSpec((1, rows, half), lambda r, place: (layer, 2 + place[CORE], 0)),
            pl.BlockSpec((1, three, depth // 2, channels), lambda r, place: (layer, 0, place[CORE], 0)),
        ],
        outs,
        [whole(o.shape) for o in outs],
        [],
        "pack",
        3,
        after=after,
    )


def hold(values, place, after):
    anywhere = pl.BlockSpec(memory_space=pl.ANY)
    return call(
        lambda place, *refs: None,
        1,
        place,
        values,
        [anywhere] * len(values),
        [struct(v.shape, v.dtype) for v in values],
        [anywhere] * len(values),
        [],
        "hold",
        1,
        {i + 1: i for i in range(len(values))},
        after,
    )


def fill_input_kernel(place, full_ref, own_ref, far_ref, out_ref):
    column = pl.program_id(0)

    @pl.when(column == 0)
    def _():
        out_ref[...] = own_ref[...]

    @pl.when(column == 1)
    def _():
        out_ref[...] = far_ref[...]


def fill_input(full, from_own, from_far, place, rows, seq_len):
    half = from_own.shape[1]
    count = rows * seq_len
    block = pl.BlockSpec((count, half), lambda j, place: (0, 0))
    return pl.pallas_call(
        fill_input_kernel,
        out_shape=struct(full.shape, full.dtype),
        grid_spec=pltpu.PrefetchScalarGridSpec(
            num_scalar_prefetch=1,
            grid=(2,),
            in_specs=[pl.BlockSpec(memory_space=pl.ANY), block, block],
            out_specs=pl.BlockSpec(
                (count, half), lambda j, place: (place[OTHER], (1 - place[SELF]) ^ j)
            ),
        ),
        input_output_aliases={1: 0},
        name="fill_input",
    )(place, full, from_own, from_far)


def swap(values):
    return lax.ppermute(values, "head", [(0, 1), (1, 0)])


def cross(values):
    count = lax.axis_size("dp")
    return lax.ppermute(
        values, ("dp", "head"), [(2 * a + h, 2 * (a ^ 2) + 1 - h) for a in range(count) for h in range(2)]
    )


def scatter(parts):
    return [swap(parts[0]), trade(parts[1], 2), cross(parts[2])]


SHARES = ((1, 0), (0, 1), (1, 1))


def trade(values, stride):
    count = lax.axis_size("dp")
    return lax.ppermute(values, "dp", [(a, a ^ stride) for a in range(count)])


def far_strides():
    count = lax.axis_size("dp")
    strides = []
    stride = 4
    while stride < count:
        strides.append(stride)
        stride *= 2
    return strides


def sums(groups, place, after=(), casts=None):
    operands = []
    plan = []
    for group in groups:
        terms = []
        for term in group:
            value, *index = term if isinstance(term, tuple) else (term,)
            terms.append((len(operands), tuple(index)))
            operands.append(value)
        plan.append(terms)
    outs = [
        struct(operands[terms[0][0]].shape[len(terms[0][1]) :], operands[terms[0][0]].dtype)
        for terms in plan
    ]

    steps = 2 if all(o.shape[0] == 2 for o in outs) else 1

    def kernel(place, *refs):
        for terms, out in zip(plan, refs[len(operands) :]):
            out[...] = functools.reduce(
                jnp.add, [refs[at][...].astype(f32) for at, _ in terms]
            ).astype(out.dtype)

    def spec(value, index):
        shape = value.shape[len(index) :]
        return pl.BlockSpec(
            (None,) * len(index) + (shape[0] // steps,) + tuple(shape[1:]),
            lambda r, place: tuple(index) + (r,) + (0,) * (len(shape) - 1),
        )

    return call(
        kernel,
        steps,
        place,
        operands,
        [spec(operands[at], index) for terms in plan for at, index in terms],
        outs,
        [spec(o, ()) for o in outs],
        [],
        "sums",
        2,
        after=after,
    )


def add(*terms):
    return functools.reduce(jnp.add, [t.astype(f32) for t in terms]).astype(bf16)


def shards(
    tokens, segments, qkv_weight, out_weight, inner_weight, outer_weight, norm_gains, cotangent
):
    side = lax.axis_index("head").astype(jnp.int32)
    spot = lax.axis_index("dp").astype(jnp.int32)
    layers = qkv_weight.shape[0]
    row_total, seq_len = segments.shape
    rows = row_total // 2
    width = qkv_weight.shape[2]
    place = jnp.stack([side, 1 - side, side * rows, spot & 1, (spot >> 1) & 1])
    weights = (out_weight, inner_weight, outer_weight)
    one = (qkv_weight,)
    far_qkv = [None, None]
    ffn_weights = [None, None]

    piece, part = pack((*weights, qkv_weight), place, 0)
    part, piece = swap(part), swap(piece)
    near = attend(tokens, one, segments, place, rows, 0, 0, 9)
    (part,) = hold([part], place, [near[5]])
    far_qkv[0] = (part, trade(part, 1))
    next_piece, next_part = pack((*weights, qkv_weight), place, 1, [near[5]])
    held = attend(tokens, far_qkv[0], segments, place, rows, 1, 0, 0.2, near, [next_piece])
    piece, next_piece, next_part = hold([piece, next_piece, next_part], place, [held[5]])
    ffn_weights[0] = (*weights, piece, trade(piece, 1))
    part, piece = swap(next_part), swap(next_piece)
    ffn_weights[1] = (*weights, piece, trade(piece, 1))
    saved_attend = [held]
    n1, r1, act, slope, n2, r2, x_tok, x_stream = ffn(
        held[0], held[5], ffn_weights[0], norm_gains, place, rows, 0, 20
    )
    saved_ffn = (n2, r2, act, slope, n1, r1)
    (part,) = hold([part], place, [x_tok])
    far_qkv[1] = (part, trade(part, 1))
    near = attend(x_tok, one, segments, place, rows, 0, 1, 9)
    held = attend(x_tok, far_qkv[1], segments, place, rows, 1, 1, 9, near)
    saved_attend.append(held)
    x_tok, activations, d_before, d_context, keep, send, gain1 = ffn_last(
        x_stream, held[5], cotangent, ffn_weights[1], norm_gains, place, rows, 1, 40
    )

    strides = far_strides()
    far_tok = swap(x_tok)
    got = trade(send, 1)
    dx, later = attend_back(
        d_context, held, one + far_qkv[1], d_before, place, rows, (0, 1), 1, None, 0.2
    )
    parts = sums([[(keep, *at), (got, *at)] for at in SHARES], place, [dx])
    crossed = scatter(parts)
    d_before, d_context, next_keep, next_send, gain0 = ffn_back(
        dx, saved_ffn, saved_attend[0][5], ffn_weights[0], norm_gains, place, rows, 0, 0.2, parts
    )
    (late,) = sums([[(keep, 0, 0), (got, 0, 0), *crossed]], place, [d_before])
    late_got = trade(late, strides[0])
    keep, send = next_keep, next_send
    got = trade(send, 1)
    dx1, full, keep1, send1 = attend_back(
        d_context,
        saved_attend[0],
        far_qkv[0],
        d_before,
        place,
        rows,
        (1,),
        0,
        (later, gain0, gain1, None),
        13,
        [late, far_tok],
    )
    core1 = trade(send1, 1)
    *parts, late = sums(
        [[(keep, *at), (got, *at)] for at in SHARES] + [[late, late_got]], place, [dx1]
    )
    crossed = scatter(parts)
    late_got = trade(late, strides[1])
    dx0, full, keep0, send0 = attend_back(
        d_context,
        saved_attend[0],
        one,
        d_before,
        place,
        rows,
        (0,),
        0,
        (later, gain0, gain1, full),
        13,
        parts + [late],
    )
    core0 = trade(send0, 1)
    (core1,) = hold([core1], place, [dx0])
    shares = [add(keep1[0], core1[0]), add(keep0[1], core0[1]), add(keep1[1], core1[1])]
    shares = scatter(shares)
    total = add(keep0[0], core0[0], *shares)
    early = [add(keep[0, 0, s], got[0, 0, s], *[c[s] for c in crossed]) for s in range(2)]
    orders = (strides, strides[::-1])
    late = add(late, late_got)
    for stride in strides[2:]:
        late = add(late, trade(late, stride))
    late_row = trade(late, 2)
    late_core = trade(jnp.stack([late, late_row]), 1)
    dx0, dx1 = hold([dx0, dx1], place, early)
    far_dx0, far_dx1 = swap(dx0), swap(dx1)
    for at in range(len(strides)):
        early = [add(early[s], trade(early[s], orders[s][at])) for s in range(2)]
        total = add(total, trade(total, strides[at]))
    early = jnp.stack(early)
    grads = finish([late, late_row, late_core], place, 1, layers)
    early_row = trade(early, 2)
    row = trade(total, 2)
    input_grad = fill_input(full, far_dx0, far_dx1, place, rows, seq_len)
    both = jnp.stack([early, early_row])
    early_core = trade(both, 1)
    (pair,) = hold([jnp.stack([total, row])], place, [input_grad, grads[0]])
    core_part = trade(pair, 1)
    other_rows = (1 - side) * rows * seq_len
    activations = lax.dynamic_update_slice(activations, far_tok, (other_rows, jnp.int32(0)))
    out_grad, inner_grad, outer_grad, qkv_grad, gain_grad = finish(
        [early, early_row, early_core], place, 0, layers, [total, row, core_part], grads
    )
    outer_grad = outer_grad.reshape(outer_weight.shape)
    return (activations, input_grad, qkv_grad, out_grad, inner_grad, outer_grad, gain_grad)


def solution(mesh):
    return jax.shard_map(
        shards,
        mesh=mesh,
        in_specs=(
            P("dp", None),
            P("dp", None),
            P(None, None, None, "head"),
            P(None, "head", None),
            P(None, None, "head"),
            P(None, None, "head"),
            P(),
            P("dp", None),
        ),
        out_specs=(
            P("dp", None),
            P("dp", None),
            P(None, None, None, "head"),
            P(None, "head", None),
            P(None, None, "head"),
            P(None, None, "head"),
            P(),
        ),
        check_vma=False,
    )
```
